32 devices in a mesh: dp: 8 (over z, core), seq: 4 (over y, x).
Axes of the slice: x: 2, y: 2, z: 4, core: 2. Of those that a mesh axis runs over, the one named last changes fastest.
Arguments:
- tokens: bfloat16 [8, 64, 16, 1152], P('dp', None, 'seq'), may hold values from -6 to 6
- slot_owner: int32 [8, 64], P('dp'), may hold values from 0 to 7, as said below
- clip_pieces: int32 [8, 4, 16], P('dp'), may hold values from 0 to 63, as said below
- clip_length: int32 [8, 4], P('dp'), may hold values from 64 to 256, as said below
- modulation: bfloat16 [8, 4, 3, 1152], P('dp'), may hold values from -4 to 4
- qkv_weight: bfloat16 [1152, 3, 1152], P(None, None, 'seq'), may hold values from -0.1875 to 0.1875
- qk_gain: float32 [2, 72], replicated, may hold values from 0.1 to 1.9
- proj_weight: bfloat16 [1152, 1152], P('seq'), may hold values from -0.1875 to 0.1875
Outputs:
- block_output: bfloat16 [8, 64, 16, 1152], P('dp', None, 'seq')
The draws below stay inside these ranges and needn't reach their ends.
Inputs may be any that keep to these rules, and one draw needn't show every extreme that they name: `slot_owner`: each row names every owner exactly 8 times. `clip_pieces`: each owner's table holds every arrival index 0 to 63 exactly once. `clip_length`: every owner has one clip of 256 tokens.
All inputs are finite; a program needn't handle non-finite values.
Results may differ from the reference program's by a relative error of at most 0.0045.
Values may be sent and summed in bfloat16 or wider, within the bound.
No kernel may reach another device: no remote copies, remote signals or barrier semaphores. Data moves between devices by JAX's collectives and lax.ppermute only.
A program may use at most 64 MiB of HBM per device.

```python
import math
import jax
import jax.numpy as jnp
from jax import lax

D = 1152
HEADS = 16
HD = 72
PIECES_DEV = 64
PIECES = 16
PEER_PIECES = 8
CLIPS_OWN = 4
PIECE_TOK = 16
CLIP_TOK = 256
N_DP = 8


def draw_slot_owner(key, part):
    key = jax.random.fold_in(key, 11)
    repeated = jnp.repeat(jnp.arange(N_DP, dtype=jnp.int32), PIECES_DEV // N_DP)
    row_keys = jax.random.split(key, N_DP)
    shuffled = jax.vmap(lambda row_key: jax.random.permutation(row_key, repeated))(row_keys)
    return shuffled.astype(jnp.int32)


def draw_clip_pieces(key, part):
    key = jax.random.fold_in(key, 12)
    numbers = jnp.arange(PIECES_DEV, dtype=jnp.int32)
    row_keys = jax.random.split(key, N_DP)
    shuffled = jax.vmap(lambda row_key: jax.random.permutation(row_key, numbers))(row_keys)
    return shuffled.reshape(N_DP, CLIPS_OWN, PIECES).astype(jnp.int32)


def draw_clip_length(key, part):
    key = jax.random.fold_in(key, 13)
    first_key, second_key = jax.random.split(key)
    drawn = jax.random.randint(first_key, (N_DP, CLIPS_OWN), CLIP_TOK // 4, CLIP_TOK + 1, dtype=jnp.int32)
    longest = jax.random.randint(second_key, (N_DP, 1), 0, CLIPS_OWN, dtype=jnp.int32)
    column = jnp.arange(CLIPS_OWN, dtype=jnp.int32)[None, :]
    return jnp.where(column == longest, CLIP_TOK, drawn).astype(jnp.int32)


def block_levels(own_key, dims, shards, least, high):
    def one(position, shards_of):
        heights = jax.random.uniform(jax.random.fold_in(jax.random.fold_in(own_key, 6), position), (shards_of,), jnp.float32, least / len(shards), high / len(shards))
        return jnp.repeat(jnp.exp(heights), dims[position] // shards_of).reshape((-1,) + (1,) * (len(dims) - position - 1))

    factor_of = one(*shards[0])
    for cut in shards[1:]:
        factor_of = factor_of * one(*cut)
    return factor_of


def noise(stream_key, extent, deviation, limit, cuts=(), held_as=jnp.bfloat16):
    values = jax.random.normal(stream_key, extent, jnp.float32) * deviation
    if len(cuts) > 0:
        values = block_levels(stream_key, extent, cuts, -0.22, 0.18) * values
    return jnp.clip(values, min=-limit, max=limit).astype(held_as)


def setup_inputs(seed: int = 0) -> dict:
    key_of = jax.random.split(jax.random.key(seed), 9)
    return {
        "tokens": noise(key_of[0], (N_DP, PIECES_DEV, PIECE_TOK, D), 1.0, 6.0, ((0, 8), (2, 4))),
        "slot_owner": draw_slot_owner(jax.random.fold_in(key_of[8], 71), 0),
        "clip_pieces": draw_clip_pieces(jax.random.fold_in(key_of[8], 71), 0),
        "clip_length": draw_clip_length(jax.random.fold_in(key_of[8], 71), 0),
        "modulation": noise(key_of[4], (N_DP, CLIPS_OWN, 3, D), 1.0, 4.0, ((0, 8),)),
        "qkv_weight": noise(key_of[5], (D, 3, HEADS * HD), D ** -0.5, 0.1875, ((2, 4),)),
        "qk_gain": jnp.clip(1.0 + 0.18 * jax.random.normal(key_of[6], (2, HD), jnp.float32), 0.1, 1.9),
        "proj_weight": noise(key_of[7], (HEADS * HD, D), (HEADS * HD) ** -0.5, 0.1875, ((0, 4),)),
    }


EPSILON = 1e-06

def scaled_norm(head_block, gain_row):
    mean_square = lax.optimization_barrier(jnp.mean(head_block * head_block, axis=-1, keepdims=True))
    return (head_block * lax.rsqrt(mean_square + EPSILON) * gain_row.astype(jnp.float32)).astype(jnp.bfloat16)

def attend_owner(operands, qkv_weight, qk_gain, proj_weight):
    received, piece_table, lengths, modulation = operands
    clip_rows = received[piece_table.reshape(-1)].reshape(CLIPS_OWN, CLIP_TOK, D)
    clip_float = clip_rows.astype(jnp.float32)
    average = lax.optimization_barrier(jnp.mean(clip_float, axis=-1, keepdims=True))
    centered = clip_float - average
    variance = lax.optimization_barrier(jnp.mean(centered * centered, axis=-1, keepdims=True))
    normed = centered * lax.rsqrt(variance + EPSILON)
    factors = modulation.astype(jnp.float32)
    hidden = (normed * (1.0 + factors[:, 1][:, None, :]) + factors[:, 0][:, None, :]).astype(jnp.bfloat16)
    projected = jnp.dot(hidden.reshape(-1, D), qkv_weight.reshape(D, -1), preferred_element_type=jnp.float32)
    projected = projected.reshape(CLIPS_OWN, CLIP_TOK, 3, HEADS, HD)
    queries = scaled_norm(projected[:, :, 0], qk_gain[0])
    keys_part = scaled_norm(projected[:, :, 1], qk_gain[1])
    values = projected[:, :, 2].astype(jnp.bfloat16)
    scores = jnp.einsum('cqhe,ckhe->chqk', queries.astype(jnp.float32), keys_part.astype(jnp.float32)) * (1.0 / math.sqrt(HD))
    positions = jnp.arange(CLIP_TOK, dtype=jnp.int32)
    in_clip = positions[None, :] < lengths[:, None]
    unscaled = jnp.where(in_clip[:, None, None, :], jnp.exp(scores), 0.0)
    weights = (unscaled / lax.optimization_barrier(jnp.sum(unscaled, axis=-1, keepdims=True))).astype(jnp.bfloat16)
    attended = jnp.einsum('chqk,ckhe->cqhe', weights.astype(jnp.float32), values.astype(jnp.float32)).astype(jnp.bfloat16)
    branch = jnp.dot(attended.reshape(-1, HEADS * HD), proj_weight, preferred_element_type=jnp.float32)
    branch = branch.reshape(CLIPS_OWN, CLIP_TOK, D)
    result = jnp.where(in_clip[:, :, None], clip_float + factors[:, 2][:, None, :] * branch, 0.0).astype(jnp.bfloat16)
    flattened = result.reshape(PIECES_DEV, PIECE_TOK, D)
    inverse = jnp.argsort(piece_table.reshape(-1)).astype(jnp.int32)
    return flattened[inverse]

def reference(tokens, slot_owner, clip_pieces, clip_length, modulation, qkv_weight, qk_gain, proj_weight):
    sorted_slots = jnp.argsort(slot_owner, axis=1, stable=True).astype(jnp.int32)
    sources = jnp.repeat(jnp.arange(N_DP, dtype=jnp.int32), PEER_PIECES)
    arrivals = jnp.tile(jnp.arange(PEER_PIECES, dtype=jnp.int32), N_DP)
    owners = jnp.arange(N_DP, dtype=jnp.int32)
    chosen = sorted_slots[sources[None, :], owners[:, None] * PEER_PIECES + arrivals[None, :]]
    received = tokens[sources[None, :], chosen]
    returned = lax.map(lambda operands: attend_owner(operands, qkv_weight, qk_gain, proj_weight), (received, clip_pieces, clip_length, modulation))
    slot_ranks = jnp.argsort(sorted_slots, axis=1).astype(jnp.int32)
    places = owners[:, None] * PEER_PIECES + slot_ranks - slot_owner * PEER_PIECES
    return returned[slot_owner, places]
```

```python
import functools
import math

import jax
import jax.numpy as jnp
from jax import lax
from jax.experimental import pallas as pl
from jax.experimental.pallas import tpu as pltpu
from jax.sharding import PartitionSpec as P

HEADS = 16
LANES = 128
EPSILON = 1e-06


def partners(array, axis, count):
    found = [array]
    for mask in range(1, count):
        found.append(lax.ppermute(array, axis, [(i, i ^ mask) for i in range(count)]))
    return found


def exchange(arrays, axis, count):
    found = [arrays[0]]
    for mask in range(1, count):
        found.append(lax.ppermute(arrays[mask], axis, [(i, i ^ mask) for i in range(count)]))
    return found


def attention_kernel(seq_count, heads, head_size, per_clip, piece_rows, *refs):
    place_ref, length_ref = refs[:2]
    hidden_refs = refs[2 : 2 + seq_count]
    weight_ref, gain_ref = refs[2 + seq_count : 4 + seq_count]
    out_refs = refs[4 + seq_count : 4 + 2 * seq_count]
    projected_ref = refs[-1]
    clip = pl.program_id(0)
    rows = per_clip * piece_rows
    hidden = jnp.concatenate([ref[0] for ref in hidden_refs], axis=0)
    projected_ref[...] = jnp.dot(hidden, weight_ref[...], preferred_element_type=jnp.float32)
    key = lax.broadcasted_iota(jnp.int32, (1, seq_count * rows), 1)
    inner = lax.rem(key, rows)
    source = jnp.bitwise_xor(lax.div(key, rows), place_ref[0])
    position = (
        lax.div(inner, piece_rows) * (piece_rows * seq_count)
        + source * piece_rows
        + lax.rem(inner, piece_rows)
    )
    in_clip = position < length_ref[clip]
    width = heads * LANES
    outs = []
    for head in range(heads):
        parts = []
        for part in range(3):
            at = part * width + head * LANES
            value = projected_ref[:, at : at + LANES]
            if part < 2:
                square = jnp.sum(value * value, axis=-1, keepdims=True) * (1.0 / head_size)
                value = value * lax.rsqrt(square + EPSILON) * gain_ref[part : part + 1, :]
            parts.append(value.astype(jnp.bfloat16))
        scores = lax.dot_general(
            parts[0], parts[1], (((1,), (1,)), ((), ())), preferred_element_type=jnp.float32
        )
        unscaled = jnp.where(in_clip, jnp.exp(scores * (1.0 / math.sqrt(head_size))), 0.0)
        total = jnp.sum(unscaled, axis=-1, keepdims=True)
        weights = (unscaled * (1.0 / total)).astype(jnp.bfloat16)
        attended = jnp.dot(weights, parts[2], preferred_element_type=jnp.float32)
        outs.append(attended.astype(jnp.bfloat16)[:, :head_size])
    joined = jnp.concatenate(outs, axis=1)
    for index, ref in enumerate(out_refs):
        ref[0] = joined[index * rows : (index + 1) * rows]


def output_kernel(seq_count, clip_rows_here, per_clip, piece_rows, *refs):
    place_ref, length_ref = refs[:2]
    head_refs = refs[2 : 2 + seq_count]
    weight_refs = refs[2 + seq_count : 2 + 2 * seq_count]
    row_ref, gate_ref, out_ref = refs[2 + 2 * seq_count :]
    clip = pl.program_id(0)
    branch = jnp.dot(head_refs[0][0], weight_refs[0][...], preferred_element_type=jnp.float32)
    for head_ref, weight_ref in zip(head_refs[1:], weight_refs[1:]):
        branch += jnp.dot(head_ref[0], weight_ref[...], preferred_element_type=jnp.float32)
    row = lax.broadcasted_iota(jnp.int32, (clip_rows_here, 1), 0)
    position = (
        lax.div(row, piece_rows) * (piece_rows * seq_count)
        + place_ref[0] * piece_rows
        + lax.rem(row, piece_rows)
    )
    result = row_ref[0].astype(jnp.float32) + gate_ref[0].astype(jnp.float32) * branch
    out_ref[0] = jnp.where(position < length_ref[clip], result, 0.0).astype(jnp.bfloat16)


def body(
    tokens, slot_owner, clip_pieces, clip_length, modulation, qkv_weight, qk_gain, proj_weight
):
    dp_count = lax.axis_size("dp")
    seq_count = lax.axis_size("seq")
    pieces_here = tokens.shape[1]
    piece_rows = tokens.shape[2]
    model_width = tokens.shape[3]
    per_peer = pieces_here // dp_count
    head_size = qk_gain.shape[1]
    heads = HEADS // seq_count
    head_width = heads * head_size
    clips_here, per_clip = clip_pieces.shape[1:]
    rows = per_clip * piece_rows
    place = lax.axis_index("seq").astype(jnp.int32).reshape(1)
    lengths = clip_length[0]

    core = lax.rem(lax.axis_index("dp"), 2)
    half = head_width // 2
    half_weight = lax.dynamic_slice_in_dim(proj_weight, core * half, half, axis=0)
    swap = [(i, i ^ 1) for i in range(dp_count)]
    own_halves = lax.all_gather(half_weight, "seq", axis=0, tiled=False)
    other_halves = lax.ppermute(own_halves, "dp", swap)
    proj_all = jnp.where(
        core == 0,
        jnp.concatenate([own_halves, other_halves], axis=1),
        jnp.concatenate([other_halves, own_halves], axis=1),
    )

    by_head = jnp.transpose(qkv_weight, (1, 2, 0)).reshape(3, heads, head_size, model_width)
    by_head = jnp.pad(by_head, ((0, 0), (0, 0), (0, LANES - head_size), (0, 0)))
    weight = jnp.transpose(by_head.reshape(3 * heads * LANES, model_width))
    gains = jnp.pad(qk_gain, ((0, 0), (0, LANES - head_size)))

    owner = slot_owner[0]
    slots = jnp.arange(pieces_here, dtype=jnp.int32)
    earlier = (owner[None, :] == owner[:, None]) & (slots[None, :] < slots[:, None])
    rank = owner * per_peer + jnp.sum(earlier.astype(jnp.int32), axis=1)
    sorted_slots = jnp.sum(
        jnp.where(rank[None, :] == slots[:, None], slots[None, :], 0), axis=1
    )
    outgoing = tokens[0][sorted_slots].reshape(dp_count, per_peer, piece_rows, model_width)
    arrived = lax.all_to_all(outgoing, "dp", split_axis=0, concat_axis=0, tiled=True).reshape(
        pieces_here, piece_rows, model_width
    )
    piece_table = clip_pieces[0].reshape(-1)
    clip_rows = arrived[piece_table].reshape(clips_here, rows, model_width)
    factors = modulation[0].astype(jnp.float32)
    clip_float = clip_rows.astype(jnp.float32)
    average = jnp.mean(clip_float, axis=-1, keepdims=True)
    centered = clip_float - average
    variance = jnp.mean(centered * centered, axis=-1, keepdims=True)
    normed = centered * lax.rsqrt(variance + EPSILON)
    hidden = (normed * (1.0 + factors[:, 1][:, None, :]) + factors[:, 0][:, None, :]).astype(
        jnp.bfloat16
    )
    hiddens = partners(hidden, "seq", seq_count)

    smem = pl.BlockSpec(memory_space=pltpu.SMEM)
    vmem = pl.BlockSpec(memory_space=pltpu.VMEM)
    hidden_spec = pl.BlockSpec((1, rows, model_width), lambda c: (c, 0, 0))
    head_spec = pl.BlockSpec((1, rows, head_width), lambda c: (c, 0, 0))
    attended = pl.pallas_call(
        functools.partial(
            attention_kernel, seq_count, heads, head_size, per_clip, piece_rows
        ),
        grid=(clips_here,),
        in_specs=[smem, smem] + [hidden_spec] * seq_count + [vmem, vmem],
        out_specs=[head_spec] * seq_count,
        out_shape=[
            jax.ShapeDtypeStruct((clips_here, rows, head_width), jnp.bfloat16)
        ] * seq_count,
        scratch_shapes=[
            pltpu.VMEM((seq_count * rows, 3 * heads * LANES), jnp.float32),
        ],
        compiler_params=pltpu.CompilerParams(vmem_limit_bytes=40 * 2**20),
    )(place, lengths, *hiddens, weight, gains)
    returned = exchange(attended, "seq", seq_count)

    ordered = jnp.bitwise_xor(jnp.arange(seq_count, dtype=jnp.int32), place[0])
    proj_list = [
        lax.dynamic_index_in_dim(proj_all, ordered[mask], 0, keepdims=False)
        for mask in range(seq_count)
    ]
    gate = modulation[0][:, 2:3]
    result = pl.pallas_call(
        functools.partial(output_kernel, seq_count, rows, per_clip, piece_rows),
        grid=(clips_here,),
        in_specs=[smem, smem]
        + [head_spec] * seq_count
        + [vmem] * seq_count
        + [hidden_spec, pl.BlockSpec((1, 1, model_width), lambda c: (c, 0, 0))],
        out_specs=hidden_spec,
        out_shape=jax.ShapeDtypeStruct((clips_here, rows, model_width), jnp.bfloat16),
        compiler_params=pltpu.CompilerParams(vmem_limit_bytes=40 * 2**20),
    )(place, lengths, *returned, *proj_list, clip_rows, gate)

    inverse = jnp.sum(
        jnp.where(piece_table[None, :] == slots[:, None], slots[None, :], 0), axis=1
    )
    home_pieces = result.reshape(pieces_here, piece_rows, model_width)[inverse]
    home_pieces = home_pieces.reshape(dp_count, per_peer, piece_rows, model_width)
    came_back = lax.all_to_all(home_pieces, "dp", split_axis=0, concat_axis=0, tiled=True).reshape(
        pieces_here, piece_rows, model_width
    )
    return came_back[rank][None]


def solution(mesh):
    return jax.shard_map(
        body,
        mesh=mesh,
        in_specs=(
            P("dp", None, "seq", None),
            P("dp", None),
            P("dp", None, None),
            P("dp", None),
            P("dp", None, None, None),
            P(None, None, "seq"),
            P(),
            P("seq", None),
        ),
        out_specs=P("dp", None, "seq", None),
        check_vma=False,
    )
```

```python
import functools
import math

import jax
import jax.numpy as jnp
from jax import lax
from jax.experimental import pallas as pl
from jax.experimental.pallas import tpu as pltpu
from jax.sharding import PartitionSpec as P

HEADS = 16
EPSILON = 1e-06


def partners(array, axis, count):
    found = [array]
    for mask in range(1, count):
        found.append(lax.ppermute(array, axis, [(i, i ^ mask) for i in range(count)]))
    return found


def exchange(arrays, axis, count):
    found = [arrays[0]]
    for mask in range(1, count):
        found.append(lax.ppermute(arrays[mask], axis, [(i, i ^ mask) for i in range(count)]))
    return found


def attention_kernel(seq_count, heads, head_size, per_clip, piece_rows, *refs):
    place_ref, length_ref = refs[:2]
    hidden_refs = refs[2 : 2 + seq_count]
    weight_ref, gain_ref = refs[2 + seq_count : 4 + seq_count]
    out_refs = refs[4 + seq_count : 4 + 2 * seq_count]
    projected_ref = refs[-1]
    clip = pl.program_id(0)
    rows = per_clip * piece_rows
    head_width = heads * head_size
    hidden = jnp.concatenate([ref[0] for ref in hidden_refs], axis=0)
    projected_ref[...] = lax.dot_general(
        weight_ref[...], hidden, (((1,), (1,)), ((), ())), preferred_element_type=jnp.float32
    )
    key = lax.broadcasted_iota(jnp.int32, (seq_count * rows, 1), 0)
    inner = lax.rem(key, rows)
    source = jnp.bitwise_xor(lax.div(key, rows), place_ref[0])
    position = (
        lax.div(inner, piece_rows) * (piece_rows * seq_count)
        + source * piece_rows
        + lax.rem(inner, piece_rows)
    )
    in_clip = position < length_ref[clip]
    outs = []
    for head in range(heads):
        parts = []
        for part in range(3):
            at = part * head_width + head * head_size
            value = projected_ref[at : at + head_size, :]
            if part < 2:
                square = jnp.sum(value * value, axis=0, keepdims=True) * (1.0 / head_size)
                value = value * lax.rsqrt(square + EPSILON) * gain_ref[:, part : part + 1]
            parts.append(value)
        queries = parts[0].astype(jnp.bfloat16)
        keys = jnp.transpose(parts[1]).astype(jnp.bfloat16)
        scores = jnp.dot(keys, queries, preferred_element_type=jnp.float32)
        unscaled = jnp.where(in_clip, jnp.exp(scores * (1.0 / math.sqrt(head_size))), 0.0)
        total = jnp.sum(unscaled, axis=0, keepdims=True)
        weights = (unscaled * (1.0 / total)).astype(jnp.bfloat16)
        outs.append(
            jnp.dot(parts[2].astype(jnp.bfloat16), weights, preferred_element_type=jnp.float32)
        )
    joined = jnp.transpose(jnp.concatenate(outs, axis=0)).astype(jnp.bfloat16)
    for index, ref in enumerate(out_refs):
        ref[0] = joined[index * rows : (index + 1) * rows]


def output_kernel(seq_count, clip_rows_here, per_clip, piece_rows, *refs):
    place_ref, length_ref = refs[:2]
    head_refs = refs[2 : 2 + seq_count]
    weight_refs = refs[2 + seq_count : 2 + 2 * seq_count]
    row_ref, gate_ref, out_ref = refs[2 + 2 * seq_count :]
    clip = pl.program_id(0)
    branch = jnp.dot(head_refs[0][0], weight_refs[0][...], preferred_element_type=jnp.float32)
    for head_ref, weight_ref in zip(head_refs[1:], weight_refs[1:]):
        branch += jnp.dot(head_ref[0], weight_ref[...], preferred_element_type=jnp.float32)
    row = lax.broadcasted_iota(jnp.int32, (clip_rows_here, 1), 0)
    position = (
        lax.div(row, piece_rows) * (piece_rows * seq_count)
        + place_ref[0] * piece_rows
        + lax.rem(row, piece_rows)
    )
    result = row_ref[0].astype(jnp.float32) + gate_ref[0].astype(jnp.float32) * branch
    out_ref[0] = jnp.where(position < length_ref[clip], result, 0.0).astype(jnp.bfloat16)


def body(
    tokens, slot_owner, clip_pieces, clip_length, modulation, qkv_weight, qk_gain, proj_weight
):
    dp_count = lax.axis_size("dp")
    seq_count = lax.axis_size("seq")
    pieces_here = tokens.shape[1]
    piece_rows = tokens.shape[2]
    model_width = tokens.shape[3]
    per_peer = pieces_here // dp_count
    head_size = qk_gain.shape[1]
    heads = HEADS // seq_count
    head_width = heads * head_size
    clips_here, per_clip = clip_pieces.shape[1:]
    rows = per_clip * piece_rows
    place = lax.axis_index("seq").astype(jnp.int32).reshape(1)
    lengths = clip_length[0]

    core = lax.rem(lax.axis_index("dp"), 2)
    half = head_width // 2
    half_weight = lax.dynamic_slice_in_dim(proj_weight, core * half, half, axis=0)
    swap = [(i, i ^ 1) for i in range(dp_count)]
    own_halves = jnp.stack(partners(half_weight, "seq", seq_count))
    other_halves = lax.ppermute(own_halves, "dp", swap)
    proj_all = jnp.where(
        core == 0,
        jnp.concatenate([own_halves, other_halves], axis=1),
        jnp.concatenate([other_halves, own_halves], axis=1),
    )

    weight = jnp.transpose(qkv_weight, (1, 2, 0)).reshape(3 * head_width, model_width)
    gains = jnp.transpose(qk_gain)

    owner = slot_owner[0]
    slots = jnp.arange(pieces_here, dtype=jnp.int32)
    earlier = (owner[None, :] == owner[:, None]) & (slots[None, :] < slots[:, None])
    rank = owner * per_peer + jnp.sum(earlier.astype(jnp.int32), axis=1)
    sorted_slots = jnp.sum(
        jnp.where(rank[None, :] == slots[:, None], slots[None, :], 0), axis=1
    )
    outgoing = tokens[0][sorted_slots].reshape(dp_count, per_peer, piece_rows, model_width)
    arrived = lax.all_to_all(outgoing, "dp", split_axis=0, concat_axis=0, tiled=True).reshape(
        pieces_here, piece_rows, model_width
    )
    piece_table = clip_pieces[0].reshape(-1)
    clip_rows = arrived[piece_table].reshape(clips_here, rows, model_width)
    factors = modulation[0].astype(jnp.float32)
    clip_float = clip_rows.astype(jnp.float32)
    average = jnp.mean(clip_float, axis=-1, keepdims=True)
    centered = clip_float - average
    variance = jnp.mean(centered * centered, axis=-1, keepdims=True)
    normed = centered * lax.rsqrt(variance + EPSILON)
    hidden = (normed * (1.0 + factors[:, 1][:, None, :]) + factors[:, 0][:, None, :]).astype(
        jnp.bfloat16
    )
    hiddens = partners(hidden, "seq", seq_count)

    smem = pl.BlockSpec(memory_space=pltpu.SMEM)
    vmem = pl.BlockSpec(memory_space=pltpu.VMEM)
    hidden_spec = pl.BlockSpec((1, rows, model_width), lambda c: (c, 0, 0))
    head_spec = pl.BlockSpec((1, rows, head_width), lambda c: (c, 0, 0))
    attended = pl.pallas_call(
        functools.partial(
            attention_kernel, seq_count, heads, head_size, per_clip, piece_rows
        ),
        grid=(clips_here,),
        in_specs=[smem, smem] + [hidden_spec] * seq_count + [vmem, vmem],
        out_specs=[head_spec] * seq_count,
        out_shape=[
            jax.ShapeDtypeStruct((clips_here, rows, head_width), jnp.bfloat16)
        ] * seq_count,
        scratch_shapes=[
            pltpu.VMEM((3 * head_width, seq_count * rows), jnp.float32),
        ],
        compiler_params=pltpu.CompilerParams(vmem_limit_bytes=40 * 2**20),
    )(place, lengths, *hiddens, weight, gains)
    returned = exchange(attended, "seq", seq_count)

    proj_list = [proj_all[mask] for mask in range(seq_count)]
    gate = modulation[0][:, 2:3]
    result = pl.pallas_call(
        functools.partial(output_kernel, seq_count, rows, per_clip, piece_rows),
        grid=(clips_here,),
        in_specs=[smem, smem]
        + [head_spec] * seq_count
        + [vmem] * seq_count
        + [hidden_spec, pl.BlockSpec((1, 1, model_width), lambda c: (c, 0, 0))],
        out_specs=hidden_spec,
        out_shape=jax.ShapeDtypeStruct((clips_here, rows, model_width), jnp.bfloat16),
        compiler_params=pltpu.CompilerParams(vmem_limit_bytes=40 * 2**20),
    )(place, lengths, *returned, *proj_list, clip_rows, gate)

    inverse = jnp.sum(
        jnp.where(piece_table[None, :] == slots[:, None], slots[None, :], 0), axis=1
    )
    home_pieces = result.reshape(pieces_here, piece_rows, model_width)[inverse]
    home_pieces = home_pieces.reshape(dp_count, per_peer, piece_rows, model_width)
    came_back = lax.all_to_all(home_pieces, "dp", split_axis=0, concat_axis=0, tiled=True).reshape(
        pieces_here, piece_rows, model_width
    )
    return came_back[rank][None]


def solution(mesh):
    return jax.shard_map(
        body,
        mesh=mesh,
        in_specs=(
            P("dp", None, "seq", None),
            P("dp", None),
            P("dp", None, None),
            P("dp", None),
            P("dp", None, None, None),
            P(None, None, "seq"),
            P(),
            P("seq", None),
        ),
        out_specs=P("dp", None, "seq", None),
        check_vma=False,
    )
```

```python
import functools
import math

import jax
import jax.numpy as jnp
from jax import lax
from jax.experimental import pallas as pl
from jax.experimental.pallas import tpu as pltpu
from jax.sharding import PartitionSpec as P

HEADS = 16
EPSILON = 1e-06


def send(array, axis, mask):
    if mask == 0:
        return array
    count = lax.axis_size(axis)
    return lax.ppermute(array, axis, [(i, i ^ mask) for i in range(count)])


def relative(array, place, count):
    bit = 1
    while bit < count:
        split = array.reshape((count // (2 * bit), 2, bit) + array.shape[1:])
        flipped = split[:, ::-1].reshape(array.shape)
        array = jnp.where((place & bit) > 0, flipped, array)
        bit *= 2
    return array


def positions(shape, axis, source, rows, piece_rows, seq_count):
    token = lax.broadcasted_iota(jnp.int32, shape, axis)
    inner = lax.rem(token, rows)
    owner = jnp.bitwise_xor(lax.div(token, rows), source)
    return (
        lax.div(inner, piece_rows) * (piece_rows * seq_count)
        + owner * piece_rows
        + lax.rem(inner, piece_rows)
    )


def attention_kernel(seq_count, groups, head_size, piece_rows, *refs):
    scalar_ref = refs[0]
    hidden_refs = refs[1 : 1 + seq_count]
    weight_refs = refs[1 + seq_count : 1 + seq_count + groups]
    gain_ref = refs[1 + seq_count + groups]
    out_refs = refs[2 + seq_count + groups : 2 + 2 * seq_count + groups]
    projected_ref = refs[-1]
    rows = hidden_refs[0].shape[0]
    group_width = weight_refs[0].shape[1]
    shards, _, shard_width = out_refs[0].shape
    hidden = jnp.concatenate([ref[...] for ref in hidden_refs], axis=0)
    in_clip = (
        positions((seq_count * rows, 1), 0, scalar_ref[0], rows, piece_rows, seq_count)
        < scalar_ref[1]
    )
    outs = []
    for group in range(groups):
        for part in range(3):
            projected_ref[part] = lax.dot_general(
                weight_refs[group][part],
                hidden,
                (((1,), (1,)), ((), ())),
                preferred_element_type=jnp.float32,
            )
        for start in range(0, group_width, head_size):
            parts = []
            for part in range(3):
                value = projected_ref[part, start : start + head_size, :]
                if part < 2:
                    square = jnp.sum(value * value, axis=0, keepdims=True) * (1.0 / head_size)
                    value = value * lax.rsqrt(square + EPSILON) * gain_ref[:, part : part + 1]
                parts.append(value)
            queries = parts[0].astype(jnp.bfloat16)
            keys = jnp.transpose(parts[1]).astype(jnp.bfloat16)
            scores = jnp.dot(keys, queries, preferred_element_type=jnp.float32)
            unscaled = jnp.where(in_clip, jnp.exp(scores * (1.0 / math.sqrt(head_size))), 0.0)
            total = jnp.sum(unscaled, axis=0, keepdims=True)
            weights = (unscaled * (1.0 / total)).astype(jnp.bfloat16)
            outs.append(
                jnp.dot(parts[2].astype(jnp.bfloat16), weights, preferred_element_type=jnp.float32)
            )
    per_shard = shard_width // head_size
    for shard in range(shards):
        joined = jnp.concatenate(outs[shard * per_shard : (shard + 1) * per_shard], axis=0)
        joined = jnp.transpose(joined).astype(jnp.bfloat16)
        for index, ref in enumerate(out_refs):
            ref[shard] = joined[index * rows : (index + 1) * rows]


def output_kernel(seq_count, y_count, x_count, clips_each, halves, piece_rows, *refs):
    place_ref, length_ref = refs[:2]
    refs = refs[2:]
    head_refs, refs = refs[: seq_count * clips_each], refs[seq_count * clips_each :]
    weight_refs, refs = refs[: seq_count * halves], refs[seq_count * halves :]
    row_ref, gate_ref, out_ref = refs
    clips, rows, _ = row_ref.shape
    branch = None
    for mask in range(seq_count):
        y_mask, x_mask = mask // x_count, mask % x_count
        left = jnp.concatenate(
            [
                head_refs[(my * x_count + x_mask) * clips_each + i][y_mask ^ my]
                for my in range(y_count)
                for i in range(clips_each)
            ],
            axis=0,
        )
        right = jnp.concatenate(
            [weight_refs[mask * halves + half][...] for half in range(halves)], axis=0
        )
        term = jnp.dot(left, right, preferred_element_type=jnp.float32)
        branch = term if branch is None else branch + term
    position = positions((rows, 1), 0, place_ref[0], rows, piece_rows, seq_count)
    for clip in range(clips):
        result = row_ref[clip].astype(jnp.float32) + gate_ref[clip : clip + 1].astype(
            jnp.float32
        ) * branch[clip * rows : (clip + 1) * rows]
        out_ref[clip] = jnp.where(position < length_ref[clip], result, 0.0).astype(jnp.bfloat16)


def body(
    tokens, slot_owner, clip_pieces, clip_length, modulation, qkv_weight, qk_gain, proj_weight
):
    dp_count = lax.axis_size("dp")
    seq_count = lax.axis_size("seq")
    x_count = y_count = math.isqrt(seq_count)
    pieces_here = tokens.shape[1]
    piece_rows = tokens.shape[2]
    model_width = tokens.shape[3]
    per_peer = pieces_here // dp_count
    head_size = qk_gain.shape[1]
    heads = HEADS // seq_count
    head_width = heads * head_size
    clips_here, per_clip = clip_pieces.shape[1:]
    clips_each = clips_here // y_count
    rows = per_clip * piece_rows
    place = lax.axis_index("seq").astype(jnp.int32)
    place_y = lax.div(place, x_count)
    core = lax.rem(lax.axis_index("dp"), 2).astype(jnp.int32)
    halves = 2 if heads % 2 == 0 else 1
    half = head_width // halves

    weight = jnp.transpose(qkv_weight, (1, 2, 0))
    qkv_own = weight
    if halves == 2:
        qkv_own = lax.dynamic_slice_in_dim(weight, core * half, half, axis=1)
        qkv_other = lax.dynamic_slice_in_dim(weight, (1 - core) * half, half, axis=1)
    qkv_fetched = [send(qkv_own, "seq", my * x_count) for my in range(y_count)]
    gains = jnp.transpose(qk_gain)

    def order(array):
        split = array.reshape((y_count, clips_each) + array.shape[1:])
        return relative(split, place_y, y_count).reshape(array.shape)

    lengths = order(clip_length[0])
    factors = order(modulation[0])
    piece_table = order(clip_pieces[0]).reshape(-1)

    owner = slot_owner[0]
    slots = jnp.arange(pieces_here, dtype=jnp.int32)
    earlier = (owner[None, :] == owner[:, None]) & (slots[None, :] < slots[:, None])
    rank = owner * per_peer + jnp.sum(earlier.astype(jnp.int32), axis=1)
    sorted_slots = jnp.sum(
        jnp.where(rank[None, :] == slots[:, None], slots[None, :], 0), axis=1
    )
    outgoing = tokens[0][sorted_slots].reshape(dp_count, per_peer, piece_rows, model_width)

    proj_weight, outgoing = lax.optimization_barrier((proj_weight, outgoing))
    proj_own = proj_weight
    if halves == 2:
        proj_own = lax.dynamic_slice_in_dim(proj_weight, core * half, half, axis=0)
        proj_other = lax.dynamic_slice_in_dim(proj_weight, (1 - core) * half, half, axis=0)
    proj_fetched = [send(proj_own, "seq", my * x_count) for my in range(y_count)]
    proj_near = [send(proj_own, "seq", mx) for mx in range(1, x_count)]

    arrived = lax.all_to_all(outgoing, "dp", split_axis=0, concat_axis=0, tiled=True).reshape(
        pieces_here, piece_rows, model_width
    )
    arrived, qkv_fetched, proj_fetched, proj_near = lax.optimization_barrier(
        (arrived, qkv_fetched, proj_fetched, proj_near)
    )
    if halves == 2:
        groups = [qkv_own, qkv_other]
        for fetched in qkv_fetched[1:]:
            groups += [fetched, send(fetched, "dp", 1)]
    else:
        groups = qkv_fetched
    proj_parts = []
    for my in range(y_count):
        for mx in range(x_count):
            fetched = proj_fetched[my]
            if mx > 0:
                fetched = proj_near[mx - 1] if my == 0 else send(fetched, "seq", mx)
            proj_parts.append(fetched)
            if halves == 2:
                proj_parts.append(proj_other if my + mx == 0 else send(fetched, "dp", 1))
    clip_rows = arrived[piece_table].reshape(clips_here, rows, model_width)
    shift, scale = factors[:, 0].astype(jnp.float32), factors[:, 1].astype(jnp.float32)
    clip_float = clip_rows.astype(jnp.float32)
    average = jnp.mean(clip_float, axis=-1, keepdims=True)
    centered = clip_float - average
    variance = jnp.mean(centered * centered, axis=-1, keepdims=True)
    normed = centered * lax.rsqrt(variance + EPSILON)
    hidden = (normed * (1.0 + scale[:, None, :]) + shift[:, None, :]).astype(jnp.bfloat16)

    smem = pl.BlockSpec(memory_space=pltpu.SMEM)
    vmem = pl.BlockSpec(memory_space=pltpu.VMEM)
    returned = [[None] * clips_each for _ in range(seq_count)]
    flops = 2 * seq_count * rows * model_width * 3 * HEADS // x_count * head_size
    for i in range(clips_each):
        arriving = [
            send(hidden[(mask // x_count) * clips_each + i], "seq", mask)
            for mask in range(seq_count)
        ]
        attended = pl.pallas_call(
            functools.partial(attention_kernel, seq_count, len(groups), head_size, piece_rows),
            in_specs=[smem] + [vmem] * (seq_count + len(groups) + 1),
            out_specs=[vmem] * seq_count,
            out_shape=[
                jax.ShapeDtypeStruct((y_count, rows, head_width), jnp.bfloat16)
            ] * seq_count,
            scratch_shapes=[pltpu.VMEM((3, half, seq_count * rows), jnp.float32)],
            compiler_params=pltpu.CompilerParams(vmem_limit_bytes=40 * 2**20),
            cost_estimate=pl.CostEstimate(
                flops=2 * flops, bytes_accessed=6 * 2**20, transcendentals=0
            ),
        )(jnp.stack([place, lengths[i]]), *arriving, *groups, gains)
        for mask in range(seq_count):
            returned[mask][i] = send(attended[mask], "seq", mask)

    result = pl.pallas_call(
        functools.partial(
            output_kernel, seq_count, y_count, x_count, clips_each, halves, piece_rows
        ),
        in_specs=[smem, smem] + [vmem] * (seq_count * (clips_each + halves) + 2),
        out_specs=vmem,
        out_shape=jax.ShapeDtypeStruct((clips_here, rows, model_width), jnp.bfloat16),
        compiler_params=pltpu.CompilerParams(vmem_limit_bytes=40 * 2**20),
    )(
        place.reshape(1),
        lengths,
        *[array for row in returned for array in row],
        *proj_parts,
        clip_rows,
        factors[:, 2],
    )

    inverse = jnp.sum(
        jnp.where(piece_table[None, :] == slots[:, None], slots[None, :], 0), axis=1
    )
    home_pieces = result.reshape(pieces_here, piece_rows, model_width)[inverse]
    home_pieces = home_pieces.reshape(dp_count, per_peer, piece_rows, model_width)
    came_back = lax.all_to_all(home_pieces, "dp", split_axis=0, concat_axis=0, tiled=True).reshape(
        pieces_here, piece_rows, model_width
    )
    return came_back[rank][None]


def solution(mesh):
    return jax.shard_map(
        body,
        mesh=mesh,
        in_specs=(
            P("dp", None, "seq", None),
            P("dp", None),
            P("dp", None, None),
            P("dp", None),
            P("dp", None, None, None),
            P(None, None, "seq"),
            P(),
            P("seq", None),
        ),
        out_specs=P("dp", None, "seq", None),
        check_vma=False,
    )
```

```python
import functools
import math

import jax
import jax.numpy as jnp
from jax import lax
from jax.experimental import pallas as pl
from jax.experimental.pallas import tpu as pltpu
from jax.sharding import PartitionSpec as P

HEADS = 16
EPSILON = 1e-06
BF16 = jnp.bfloat16
F32 = jnp.float32


def send(array, axis, mask):
    if mask == 0:
        return array
    count = lax.axis_size(axis)
    return lax.ppermute(array, axis, [(i, i ^ mask) for i in range(count)])


def route_kernel(per_peer, piece_rows, owner_ref, place_ref, token_ref, *refs):
    slot_ref, block_refs, filled_ref = refs[0], refs[1:-1], refs[-1]
    peers = len(block_refs)
    for peer in range(peers):
        filled_ref[peer] = peer * per_peer

    @pl.loop(0, peers * per_peer, unroll=8)
    def _(slot):
        peer = jnp.bitwise_xor(owner_ref[slot], place_ref[0])
        at = filled_ref[peer]
        filled_ref[peer] = at + 1
        slot_ref[at] = slot

    for peer, ref in enumerate(block_refs):
        for m in range(per_peer):
            ref[m * piece_rows : (m + 1) * piece_rows, :] = token_ref[slot_ref[peer * per_peer + m]]


def place_kernel(per_peer, piece_rows, slot_ref, *refs):
    block_refs, out_ref = refs[:-1], refs[-1]
    for peer, ref in enumerate(block_refs):
        for m in range(per_peer):
            out_ref[slot_ref[peer * per_peer + m]] = ref[m * piece_rows : (m + 1) * piece_rows, :]


def pick(clip, table):
    rows = jnp.broadcast_to(table[0:1], (clip.shape[0], table.shape[1]))
    for index in range(1, table.shape[0]):
        rows = jnp.where(clip == index, table[index : index + 1], rows)
    return rows


def norm_kernel(clip_tokens, code_ref, shift_ref, scale_ref, *refs):
    block_refs, out_ref = refs[:-1], refs[-1]
    clip = lax.div(code_ref[...], clip_tokens)
    rows = jnp.concatenate([ref[...].astype(F32) for ref in block_refs], axis=0)
    average = jnp.mean(rows, axis=-1, keepdims=True)
    centered = rows - average
    variance = jnp.mean(centered * centered, axis=-1, keepdims=True)
    normed = centered * lax.rsqrt(variance + EPSILON)
    scale = pick(clip, scale_ref[...].astype(F32))
    shift = pick(clip, shift_ref[...].astype(F32))
    out_ref[...] = (normed * (1.0 + scale) + shift).astype(BF16)


def project_kernel(head_size, weight_ref, gain_ref, *refs):
    hidden_refs, out_ref = refs[:-1], refs[-1]
    hidden = jnp.concatenate([ref[...] for ref in hidden_refs], axis=0)
    width = weight_ref.shape[1]
    for part in range(3):
        projected = lax.dot_general(
            weight_ref[part], hidden, (((1,), (1,)), ((), ())), preferred_element_type=F32
        )
        if part == 2:
            out_ref[part] = projected.astype(BF16)
            continue
        gain = gain_ref[:, part : part + 1]
        found = []
        for start in range(0, width, head_size):
            value = projected[start : start + head_size]
            square = jnp.sum(value * value, axis=0, keepdims=True) * (1.0 / head_size)
            found.append(value * lax.rsqrt(square + EPSILON) * gain)
        out_ref[part] = jnp.concatenate(found, axis=0).astype(BF16)


def attention_kernel(clips, clip_tokens, head_size, length_ref, code_ref, *refs):
    part_refs, out_refs, all_ref = refs[:2], refs[2:-1], refs[-1]
    stacked = [
        jnp.concatenate([ref[part] for ref in part_refs], axis=1) for part in range(3)
    ]
    width = stacked[0].shape[0]
    code = code_ref[...]
    position = lax.broadcasted_iota(jnp.int32, (clip_tokens, 1), 0)
    for clip in range(clips):
        chosen = jnp.where(code == position + clip * clip_tokens, 1.0, 0.0).astype(BF16)
        queries, keys, values = [
            lax.dot_general(
                array, chosen, (((1,), (1,)), ((), ())), preferred_element_type=F32
            )
            for array in stacked
        ]
        in_clip = position < length_ref[clip]
        outs = []
        for start in range(0, width, head_size):
            at = slice(start, start + head_size)
            scores = jnp.dot(
                jnp.transpose(keys[at]).astype(BF16),
                queries[at].astype(BF16),
                preferred_element_type=F32,
            )
            unscaled = jnp.where(in_clip, jnp.exp(scores * (1.0 / math.sqrt(head_size))), 0.0)
            total = jnp.sum(unscaled, axis=0, keepdims=True)
            weights = (unscaled * (1.0 / total)).astype(BF16)
            outs.append(jnp.dot(values[at].astype(BF16), weights, preferred_element_type=F32))
        attended = jnp.concatenate(outs, axis=0).astype(BF16)
        back = jnp.dot(attended, chosen, preferred_element_type=F32)
        if clip == 0:
            all_ref[...] = back
        else:
            all_ref[...] += back
    joined = jnp.transpose(all_ref[...]).astype(BF16)
    count = joined.shape[0] // 2
    rows = count // len(out_refs)
    for index, ref in enumerate(out_refs):
        for group in range(2):
            start = group * count + index * rows
            ref[group * rows : (group + 1) * rows, :] = joined[start : start + rows]


def output_kernel(
    seq_count, halves, clip_tokens, core_ref, length_ref, code_ref, gate_ref, *refs
):
    head_refs, refs = refs[:seq_count], refs[seq_count:]
    weight_refs, refs = refs[: seq_count * halves], refs[seq_count * halves :]
    block_refs, out_refs = refs[: len(refs) // 2], refs[len(refs) // 2 :]
    branch = None
    for mask in range(seq_count):
        weight = [ref[...] for ref in weight_refs[mask * halves : (mask + 1) * halves]]
        if halves == 2:
            first = core_ref[0] == 0
            weight = [
                jnp.where(first, weight[0], weight[1]),
                jnp.where(first, weight[1], weight[0]),
            ]
        term = jnp.dot(
            head_refs[mask][...], jnp.concatenate(weight, axis=0), preferred_element_type=F32
        )
        branch = term if branch is None else branch + term
    code = code_ref[...]
    clip = lax.div(code, clip_tokens)
    limit = jnp.full(code.shape, length_ref[0], jnp.int32)
    for index in range(1, length_ref.shape[0]):
        limit = jnp.where(clip == index, length_ref[index], limit)
    kept = lax.rem(code, clip_tokens) < limit
    branch = pick(clip, gate_ref[...].astype(F32)) * branch
    rows = block_refs[0].shape[0]
    for index, (block_ref, out_ref) in enumerate(zip(block_refs, out_refs)):
        at = slice(index * rows, (index + 1) * rows)
        result = block_ref[...].astype(F32) + branch[at]
        out_ref[...] = jnp.where(kept[at], result, 0.0).astype(BF16)


def body(
    tokens, slot_owner, clip_pieces, clip_length, modulation, qkv_weight, qk_gain, proj_weight
):
    dp_count = lax.axis_size("dp")
    seq_count = lax.axis_size("seq")
    pieces_here = tokens.shape[1]
    piece_rows = tokens.shape[2]
    model_width = tokens.shape[3]
    per_peer = pieces_here // dp_count
    head_size = qk_gain.shape[1]
    heads = HEADS // seq_count
    head_width = heads * head_size
    clips_here, per_clip = clip_pieces.shape[1:]
    clip_tokens = per_clip * piece_rows * seq_count
    block_rows = per_peer * piece_rows
    rows_here = pieces_here * piece_rows
    group_rows = rows_here // 2
    place = lax.axis_index("seq").astype(jnp.int32)
    owner_place = lax.axis_index("dp").astype(jnp.int32)
    core = lax.rem(owner_place, 2)
    halves = 2 if heads % 2 == 0 else 1
    half = head_width // halves
    lengths = clip_length[0]
    x_count = math.isqrt(seq_count)

    smem = pl.BlockSpec(memory_space=pltpu.SMEM)
    vmem = pl.BlockSpec(memory_space=pltpu.VMEM)

    def call(kernel, inputs, outputs, scratch=(), scalars=0, out_scalars=0, limit=16, flops=0):
        return pl.pallas_call(
            kernel,
            in_specs=[smem] * scalars + [vmem] * (len(inputs) - scalars),
            out_specs=[smem] * out_scalars + [vmem] * (len(outputs) - out_scalars),
            out_shape=[jax.ShapeDtypeStruct(shape, dtype) for shape, dtype in outputs],
            scratch_shapes=list(scratch),
            compiler_params=pltpu.CompilerParams(vmem_limit_bytes=limit * 2**20),
            cost_estimate=pl.CostEstimate(
                flops=flops, bytes_accessed=2**20, transcendentals=0
            ),
        )(*inputs)

    proj_own = proj_weight
    if halves == 2:
        proj_own = lax.dynamic_slice_in_dim(proj_weight, core * half, half, axis=0)
    proj_near = {
        mask: send(proj_own, "seq", mask)
        for mask in range(seq_count)
        if mask % x_count == 0 or mask < x_count
    }

    slots, *blocks = call(
        functools.partial(route_kernel, per_peer, piece_rows),
        [slot_owner[0], owner_place.reshape(1), tokens[0]],
        [((pieces_here,), jnp.int32)] + [((block_rows, model_width), BF16)] * dp_count,
        scratch=[pltpu.SMEM((dp_count,), jnp.int32)],
        scalars=2,
        out_scalars=1,
    )
    arrived = [send(block, "dp", mask) for mask, block in enumerate(blocks)]

    index = jnp.arange(pieces_here, dtype=jnp.int32)
    arrival = jnp.bitwise_xor(index // per_peer, owner_place) * per_peer + index % per_peer
    found = clip_pieces[0].reshape(1, -1) == arrival[:, None]
    in_order = jnp.sum(jnp.where(found, index[None, :], 0), axis=1)
    base = in_order.reshape(2, 1, -1, 1) * (piece_rows * seq_count) + jnp.arange(
        piece_rows, dtype=jnp.int32
    )
    source = jnp.bitwise_xor(jnp.arange(seq_count, dtype=jnp.int32), place) * piece_rows
    code = (base + source[None, :, None, None]).reshape(1, -1)
    code_here = (base + source[0]).reshape(-1, 1)

    gains = jnp.transpose(qk_gain)
    weight = jnp.transpose(qkv_weight, (1, 2, 0))
    shift, scale, gate = [modulation[0][:, part] for part in range(3)]
    half_count = dp_count // 2
    stacked = []
    for group in range(2):
        (hidden,) = call(
            functools.partial(norm_kernel, clip_tokens),
            [code_here[group * group_rows : (group + 1) * group_rows], shift, scale]
            + arrived[group * half_count : (group + 1) * half_count],
            [((group_rows, model_width), BF16)],
        )
        if group == 1:
            proj_near, hidden = lax.optimization_barrier((proj_near, hidden))
        hiddens = [send(hidden, "seq", mask) for mask in range(seq_count)]
        (projected,) = call(
            functools.partial(project_kernel, head_size),
            [weight, gains] + hiddens,
            [((3, head_width, seq_count * group_rows), BF16)],
            flops=2 * 3 * head_width * model_width * seq_count * group_rows,
        )
        stacked.append(projected)

    proj_parts = []
    for mask in range(seq_count):
        if mask in proj_near:
            fetched = proj_near[mask]
        else:
            fetched = send(proj_near[mask - mask % x_count], "seq", mask % x_count)
        proj_parts.append(fetched)
        if halves == 2:
            if mask == 0:
                proj_parts.append(
                    lax.dynamic_slice_in_dim(proj_weight, (1 - core) * half, half, axis=0)
                )
            else:
                proj_parts.append(send(fetched, "dp", 1))

    attended = call(
        functools.partial(attention_kernel, clips_here, clip_tokens, head_size),
        [lengths, code] + stacked,
        [((rows_here, head_width), BF16)] * seq_count,
        scratch=[pltpu.VMEM((head_width, seq_count * rows_here), F32)],
        scalars=1,
        limit=16 if clip_tokens <= 256 else 48,
        flops=2 * 3 * head_width * model_width * seq_count * group_rows,
    )
    returned = [send(array, "seq", mask) for mask, array in enumerate(attended)]

    results = call(
        functools.partial(output_kernel, seq_count, halves, clip_tokens),
        [core.reshape(1), lengths, code_here, gate] + returned + proj_parts + arrived,
        [((block_rows, model_width), BF16)] * dp_count,
        scalars=2,
    )
    came_back = [None] * dp_count
    for mask in list(range(half_count, dp_count)) + list(range(half_count)):
        came_back[mask] = send(results[mask], "dp", mask)
    (out,) = call(
        functools.partial(place_kernel, per_peer, piece_rows),
        [slots] + came_back,
        [((pieces_here, piece_rows, model_width), BF16)],
        scalars=1,
    )
    return out[None]


def solution(mesh):
    return jax.shard_map(
        body,
        mesh=mesh,
        in_specs=(
            P("dp", None, "seq", None),
            P("dp", None),
            P("dp", None, None),
            P("dp", None),
            P("dp", None, None, None),
            P(None, None, "seq"),
            P(),
            P("seq", None),
        ),
        out_specs=P("dp", None, "seq", None),
        check_vma=False,
    )
```

```python
import functools
import math

import jax
import jax.numpy as jnp
from jax import lax
from jax.experimental import pallas as pl
from jax.experimental.pallas import tpu as pltpu
from jax.sharding import PartitionSpec as P

HEADS = 16
EPSILON = 1e-06
BF16 = jnp.bfloat16
F32 = jnp.float32


def send(array, axis, mask):
    if mask == 0:
        return array
    count = lax.axis_size(axis)
    return lax.ppermute(array, axis, [(i, i ^ mask) for i in range(count)])


def route_kernel(per_peer, piece_rows, owner_ref, place_ref, token_ref, *refs):
    slot_ref, own_ref, other_ref, filled_ref = refs
    peers = filled_ref.shape[0]
    for peer in range(peers):
        filled_ref[peer] = peer * per_peer

    @pl.loop(0, peers * per_peer, unroll=8)
    def _(slot):
        peer = jnp.bitwise_xor(owner_ref[0, slot], place_ref[0])
        at = filled_ref[peer]
        filled_ref[peer] = at + 1
        slot_ref[at] = slot

    for peer in range(peers):
        ref = own_ref if peer % 2 == 0 else other_ref
        for m in range(per_peer):
            at = (peer // 2 * per_peer + m) * piece_rows
            ref[at : at + piece_rows, :] = token_ref[0, slot_ref[peer * per_peer + m]]


def merge_kernel(rows, own_ref, other_ref, *refs):
    for index, ref in enumerate(refs):
        ref[:rows] = own_ref[index * rows : (index + 1) * rows]
        ref[rows:] = other_ref[index * rows : (index + 1) * rows]


def half_kernel(core_ref, weight_ref, out_ref):
    rows = out_ref.shape[0]
    out_ref[...] = weight_ref[pl.ds(pl.multiple_of(core_ref[0] * rows, 8), rows), :]


def join_kernel(*refs):
    rows = refs[0].shape[0]
    for index, ref in enumerate(refs[:-1]):
        refs[-1][index * rows : (index + 1) * rows] = ref[...]


def place_kernel(per_peer, piece_rows, order, slot_ref, *refs):
    block_refs, out_ref = refs[:-1], refs[-1]
    for peer, ref in zip(order, block_refs):
        for m in range(per_peer):
            slot = slot_ref[peer * per_peer + m]
            out_ref[0, slot] = ref[m * piece_rows : (m + 1) * piece_rows, :]


def arrival_of(piece, per_peer, owner_place):
    source = jnp.bitwise_xor(lax.div(piece, per_peer), owner_place)
    return source * per_peer + lax.rem(piece, per_peer)


def row_codes(rows, first_piece, per_peer, piece_rows, token_rows, owner_place, place, table):
    row = lax.broadcasted_iota(jnp.int32, (rows, 1), 0)
    arrival = arrival_of(first_piece + lax.div(row, piece_rows), per_peer, owner_place)
    lane = lax.broadcasted_iota(jnp.int32, (1, table.shape[1]), 1)
    found = jnp.zeros((rows, 1), jnp.int32)
    for clip in range(table.shape[0]):
        number = jnp.where(
            arrival == table[clip : clip + 1], lane + clip * table.shape[1], 0
        )
        found += jnp.sum(number, axis=1, keepdims=True)
    return found * token_rows + place * piece_rows + lax.rem(row, piece_rows)


def pick(clip, table):
    rows = jnp.broadcast_to(table[0:1], (clip.shape[0], table.shape[1]))
    for index in range(1, table.shape[0]):
        rows = jnp.where(clip == index, table[index : index + 1], rows)
    return rows


def norm_kernel(
    clip_tokens, codes_of, owner_ref, place_ref, table_ref, modulation_ref, *refs
):
    block_refs, out_ref = refs[:-1], refs[-1]
    code = codes_of(out_ref.shape[0], owner_ref[0], place_ref[0], table_ref[0])
    clip = lax.div(code, clip_tokens)
    rows = jnp.concatenate([ref[...].astype(F32) for ref in block_refs], axis=0)
    average = jnp.mean(rows, axis=-1, keepdims=True)
    centered = rows - average
    variance = jnp.mean(centered * centered, axis=-1, keepdims=True)
    normed = centered * lax.rsqrt(variance + EPSILON)
    shift = pick(clip, modulation_ref[0].astype(F32))
    scale = pick(clip, modulation_ref[1].astype(F32))
    out_ref[...] = (normed * (1.0 + scale) + shift).astype(BF16)


def project_kernel(head_size, weight_ref, gain_ref, *refs):
    hidden_refs, out_ref = refs[:-1], refs[-1]
    hidden = jnp.concatenate([ref[...] for ref in hidden_refs], axis=0)
    width = weight_ref.shape[1]
    shape = (head_size, head_size)
    diagonal = lax.broadcasted_iota(jnp.int32, shape, 0) == lax.broadcasted_iota(
        jnp.int32, shape, 1
    )
    for part in range(3):
        projected = lax.dot_general(
            weight_ref[part], hidden, (((1,), (1,)), ((), ())), preferred_element_type=F32
        )
        if part == 2:
            out_ref[part] = projected.astype(BF16)
            continue
        gain = jnp.sum(
            jnp.where(diagonal, gain_ref[part : part + 1, :], 0.0), axis=1, keepdims=True
        )
        found = []
        for start in range(0, width, head_size):
            value = projected[start : start + head_size]
            square = jnp.sum(value * value, axis=0, keepdims=True) * (1.0 / head_size)
            found.append(value * lax.rsqrt(square + EPSILON) * gain)
        out_ref[part] = jnp.concatenate(found, axis=0).astype(BF16)


def attention_kernel(
    head_size, per_peer, piece_rows, length_ref, owner_ref, place_ref, table_ref, *refs
):
    part_refs, out_refs, all_ref = refs[:2], refs[2:-1], refs[-1]
    stacked = [
        jnp.concatenate([ref[part] for ref in part_refs], axis=1) for part in range(3)
    ]
    width, tokens = stacked[0].shape
    seq_count = len(out_refs)
    clips, per_clip = table_ref.shape[1:]
    clip_tokens = tokens // clips
    group_rows = tokens // 2 // seq_count
    token = lax.broadcasted_iota(jnp.int32, (1, tokens), 1)
    row = lax.rem(token, group_rows)
    block = lax.div(token, group_rows)
    piece = lax.div(block, seq_count) * (group_rows // piece_rows) + lax.div(row, piece_rows)
    arrival = arrival_of(piece, per_peer, owner_ref[0])
    found = jnp.zeros_like(token)
    for clip in range(clips):
        for p in range(per_clip):
            found = jnp.where(arrival == table_ref[0, clip, p], clip * per_clip + p, found)
    source = jnp.bitwise_xor(lax.rem(block, seq_count), place_ref[0])
    code = found * (piece_rows * seq_count) + source * piece_rows + lax.rem(row, piece_rows)
    position = lax.broadcasted_iota(jnp.int32, (clip_tokens, 1), 0)
    for clip in range(clips):
        chosen = jnp.where(code == position + clip * clip_tokens, 1.0, 0.0).astype(BF16)
        queries, keys, values = [
            lax.dot_general(
                array, chosen, (((1,), (1,)), ((), ())), preferred_element_type=F32
            )
            for array in stacked
        ]
        in_clip = position < length_ref[0, clip]
        outs = []
        for start in range(0, width, head_size):
            at = slice(start, start + head_size)
            scores = jnp.dot(
                jnp.transpose(keys[at]).astype(BF16),
                queries[at].astype(BF16),
                preferred_element_type=F32,
            )
            unscaled = jnp.where(in_clip, jnp.exp(scores * (1.0 / math.sqrt(head_size))), 0.0)
            total = jnp.sum(unscaled, axis=0, keepdims=True)
            weights = (unscaled * (1.0 / total)).astype(BF16)
            outs.append(jnp.dot(values[at].astype(BF16), weights, preferred_element_type=F32))
        attended = jnp.concatenate(outs, axis=0).astype(BF16)
        back = jnp.dot(attended, chosen, preferred_element_type=F32)
        if clip == 0:
            all_ref[...] = back
        else:
            all_ref[...] += back
    for index, ref in enumerate(out_refs):
        for group in range(2):
            start = (group * seq_count + index) * group_rows
            ref[:, group * group_rows : (group + 1) * group_rows] = all_ref[
                :, start : start + group_rows
            ].astype(BF16)


def output_kernel(
    seq_count,
    halves,
    clip_tokens,
    codes_of,
    core_ref,
    length_ref,
    owner_ref,
    place_ref,
    table_ref,
    modulation_ref,
    weight_ref,
    *refs,
):
    head_refs, refs = refs[:seq_count], refs[seq_count:]
    fetched = seq_count - 2 + halves
    fetched_refs, refs = refs[:fetched], refs[fetched:]
    count = len(refs) // 3
    block_refs, out_refs = refs[:count], refs[count:]
    rows = out_refs[0].shape[0]
    branch = None
    for mask in range(seq_count):
        if mask == 0:
            weight = weight_ref[...]
        else:
            parts = [fetched_refs[mask - 1][...]]
            if halves == 2:
                half = parts[0].shape[0]
                parts.append(fetched_refs[-1][(mask - 1) * half : mask * half])
                first = core_ref[0] == 0
                parts = [
                    jnp.where(first, parts[0], parts[1]),
                    jnp.where(first, parts[1], parts[0]),
                ]
            weight = jnp.concatenate(parts, axis=0)
        term = lax.dot_general(
            head_refs[mask][...],
            weight,
            (((0,), (0,)), ((), ())),
            preferred_element_type=F32,
        )
        branch = term if branch is None else branch + term
    code = codes_of(branch.shape[0], owner_ref[0], place_ref[0], table_ref[0])
    clip = lax.div(code, clip_tokens)
    limit = jnp.zeros_like(code)
    for index in range(length_ref.shape[1]):
        limit = jnp.where(clip == index, length_ref[0, index], limit)
    kept = lax.rem(code, clip_tokens) < limit
    branch = pick(clip, modulation_ref[2].astype(F32)) * branch
    for index, out_ref in enumerate(out_refs):
        at = slice(index * rows, (index + 1) * rows)
        side = slice(index % 2 * rows, (index % 2 + 1) * rows)
        result = block_refs[index // 2][side].astype(F32) + branch[at]
        out_ref[...] = jnp.where(kept[at], result, 0.0).astype(BF16)


def body(
    tokens, slot_owner, clip_pieces, clip_length, modulation, qkv_weight, qk_gain, proj_weight
):
    dp_count = lax.axis_size("dp")
    seq_count = lax.axis_size("seq")
    pieces_here = tokens.shape[1]
    piece_rows = tokens.shape[2]
    model_width = tokens.shape[3]
    per_peer = pieces_here // dp_count
    head_size = qk_gain.shape[1]
    heads = HEADS // seq_count
    head_width = heads * head_size
    clips_here, per_clip = clip_pieces.shape[1:]
    clip_tokens = per_clip * piece_rows * seq_count
    block_rows = per_peer * piece_rows
    rows_here = pieces_here * piece_rows
    group_rows = rows_here // 2
    chips = dp_count // 2
    owner_place = lax.axis_index("dp").astype(jnp.int32)
    place = lax.axis_index("seq").astype(jnp.int32).reshape(1)
    core = lax.rem(owner_place, 2).reshape(1)
    owner_place = owner_place.reshape(1)
    halves = 2 if heads % 2 == 0 else 1

    smem = pl.BlockSpec(memory_space=pltpu.SMEM)
    vmem = pl.BlockSpec(memory_space=pltpu.VMEM)

    def call(kernel, scalars, inputs, outputs, scratch=(), out_scalars=0, limit=16, flops=10**9):
        return pl.pallas_call(
            kernel,
            in_specs=[smem] * len(scalars) + [vmem] * len(inputs),
            out_specs=[smem] * out_scalars + [vmem] * (len(outputs) - out_scalars),
            out_shape=[jax.ShapeDtypeStruct(shape, dtype) for shape, dtype in outputs],
            scratch_shapes=list(scratch),
            compiler_params=pltpu.CompilerParams(vmem_limit_bytes=limit * 2**20),
            cost_estimate=pl.CostEstimate(
                flops=flops, bytes_accessed=2**20, transcendentals=0
            ),
        )(*scalars, *inputs)

    slots, own, other = call(
        functools.partial(route_kernel, per_peer, piece_rows),
        [slot_owner, owner_place],
        [tokens],
        [((pieces_here,), jnp.int32)] + [((chips * block_rows, model_width), BF16)] * 2,
        scratch=[pltpu.SMEM((dp_count,), jnp.int32)],
        out_scalars=1,
    )
    payloads = call(
        functools.partial(merge_kernel, block_rows),
        [],
        [own, send(other, "dp", 1)],
        [((2 * block_rows, model_width), BF16)] * chips,
    )
    arrived = [send(payload, "dp", 2 * mask) for mask, payload in enumerate(payloads)]

    def codes_of(group):
        return lambda rows, *places: row_codes(
            rows,
            group * (pieces_here // 2),
            per_peer,
            piece_rows,
            piece_rows * seq_count,
            *places,
        )

    weight = jnp.transpose(qkv_weight, (1, 2, 0))
    factors = jnp.transpose(modulation[0], (1, 0, 2))
    stacked, arriving = [], []
    for group in range(2):
        blocks = arrived[group * chips // 2 : (group + 1) * chips // 2]
        (hidden,) = call(
            functools.partial(norm_kernel, clip_tokens, codes_of(group)),
            [owner_place, place],
            [clip_pieces, factors] + blocks,
            [((group_rows, model_width), BF16)],
            flops=(1 + 10 * group) * 10**9,
        )
        if group == 1:
            proj_late, hidden, hiddens = lax.optimization_barrier(
                (proj_weight, hidden, hiddens)
            )
            arriving[0] = hiddens
        hiddens = [send(hidden, "seq", mask) for mask in range(seq_count)]
        arriving.append(hiddens)
    for hiddens in arriving:
        (projected,) = call(
            functools.partial(project_kernel, head_size),
            [],
            [weight, qk_gain] + hiddens,
            [((3, head_width, seq_count * group_rows), BF16)],
            flops=3 * 10**9,
        )
        stacked.append(projected)

    proj_own = proj_late
    if halves == 2:
        (proj_own,) = call(
            half_kernel, [core], [proj_late], [((head_width // 2, model_width), BF16)]
        )
    proj_parts = [send(proj_own, "seq", mask) for mask in range(1, seq_count)]

    attended = call(
        functools.partial(attention_kernel, head_size, per_peer, piece_rows),
        [clip_length, owner_place, place, clip_pieces],
        stacked,
        [((head_width, rows_here), BF16)] * seq_count,
        scratch=[pltpu.VMEM((head_width, seq_count * rows_here), F32)],
        limit=16 if clip_tokens <= 256 else 48,
        flops=8 * 10**9,
    )
    returned = [send(array, "seq", mask) for mask, array in enumerate(attended)]
    _, proj_parts = lax.optimization_barrier((attended[0], proj_parts))
    if halves == 2:
        (joined,) = call(
            join_kernel,
            [],
            proj_parts,
            [(((seq_count - 1) * head_width // 2, model_width), BF16)],
        )
        proj_parts.append(send(joined, "dp", 1))

    results = call(
        functools.partial(output_kernel, seq_count, halves, clip_tokens, codes_of(0)),
        [core, clip_length, owner_place, place],
        [clip_pieces, factors, proj_weight] + returned + proj_parts + arrived,
        [((block_rows, model_width), BF16)] * dp_count,
        flops=3 * 10**9,
    )
    order = list(range(dp_count // 2, dp_count)) + list(range(dp_count // 2))
    came_back = [send(results[mask], "dp", mask) for mask in order]
    (out,) = call(
        functools.partial(place_kernel, per_peer, piece_rows, order),
        [slots],
        came_back,
        [(tokens.shape, BF16)],
    )
    return out


def solution(mesh):
    return jax.shard_map(
        body,
        mesh=mesh,
        in_specs=(
            P("dp", None, "seq", None),
            P("dp", None),
            P("dp", None, None),
            P("dp", None),
            P("dp", None, None, None),
            P(None, None, "seq"),
            P(),
            P("seq", None),
        ),
        out_specs=P("dp", None, "seq", None),
        check_vma=False,
    )
```

```python
import functools
import math

import jax
import jax.numpy as jnp
from jax import lax
from jax.experimental import pallas as pl
from jax.experimental.pallas import tpu as pltpu
from jax.sharding import PartitionSpec as P

HEADS = 16
EPSILON = 1e-06
BF16 = jnp.bfloat16
F32 = jnp.float32


def send(array, axis, mask):
    if mask == 0:
        return array
    count = lax.axis_size(axis)
    return lax.ppermute(array, axis, [(i, i ^ mask) for i in range(count)])


def route_kernel(per_peer, piece_rows, place_ref, owner_hbm, token_hbm, *refs):
    slot_ref, own_ref, other_ref, filled_ref, owner_ref, token_ref, sems = refs
    peers = filled_ref.shape[0]
    owner_copy = pltpu.make_async_copy(owner_hbm, owner_ref, sems.at[0])
    token_copy = pltpu.make_async_copy(token_hbm, token_ref, sems.at[1])
    owner_copy.start()
    token_copy.start()
    for peer in range(peers):
        filled_ref[peer] = peer * per_peer
    owner_copy.wait()

    @pl.loop(0, peers * per_peer, unroll=8)
    def _(slot):
        peer = jnp.bitwise_xor(owner_ref[0, slot], place_ref[0])
        at = filled_ref[peer]
        filled_ref[peer] = at + 1
        slot_ref[at] = slot

    token_copy.wait()
    for peer in range(peers):
        ref = own_ref if peer % 2 == 0 else other_ref
        for m in range(per_peer):
            at = (peer // 2 * per_peer + m) * piece_rows
            ref[at : at + piece_rows, :] = token_ref[0, slot_ref[peer * per_peer + m]]


def merge_kernel(rows, own_ref, other_ref, *refs):
    for index, ref in enumerate(refs):
        ref[:rows] = own_ref[index * rows : (index + 1) * rows]
        ref[rows:] = other_ref[index * rows : (index + 1) * rows]


def half_kernel(core_ref, weight_hbm, out_ref, sem):
    rows = out_ref.shape[0]
    start = pl.multiple_of(core_ref[0] * rows, 16)
    copy = pltpu.make_async_copy(weight_hbm.at[pl.ds(start, rows), :], out_ref, sem)
    copy.start()
    copy.wait()


def join_kernel(*refs):
    rows = refs[0].shape[0]
    for index, ref in enumerate(refs[:-1]):
        refs[-1][index * rows : (index + 1) * rows] = ref[...]


def place_kernel(per_peer, piece_rows, order, slot_ref, *refs):
    block_refs, out_ref = refs[:-1], refs[-1]
    for peer, ref in zip(order, block_refs):
        for m in range(per_peer):
            slot = slot_ref[peer * per_peer + m]
            out_ref[0, slot] = ref[m * piece_rows : (m + 1) * piece_rows, :]


def arrival_of(piece, per_peer, owner_place):
    source = jnp.bitwise_xor(lax.div(piece, per_peer), owner_place)
    return source * per_peer + lax.rem(piece, per_peer)


def row_codes(rows, first_piece, per_peer, piece_rows, token_rows, owner_place, place, table):
    row = lax.broadcasted_iota(jnp.int32, (rows, 1), 0)
    arrival = arrival_of(first_piece + lax.div(row, piece_rows), per_peer, owner_place)
    lane = lax.broadcasted_iota(jnp.int32, (1, table.shape[1]), 1)
    found = jnp.zeros((rows, 1), jnp.int32)
    for clip in range(table.shape[0]):
        number = jnp.where(
            arrival == table[clip : clip + 1], lane + clip * table.shape[1], 0
        )
        found += jnp.sum(number, axis=1, keepdims=True)
    return found * token_rows + place * piece_rows + lax.rem(row, piece_rows)


def pick(clip, table):
    rows = jnp.broadcast_to(table[0:1], (clip.shape[0], table.shape[1]))
    for index in range(1, table.shape[0]):
        rows = jnp.where(clip == index, table[index : index + 1], rows)
    return rows


def norm_kernel(
    clip_tokens, codes_of, owner_ref, place_ref, table_ref, modulation_ref, *refs
):
    block_refs, out_ref = refs[:-1], refs[-1]
    code = codes_of(out_ref.shape[0], owner_ref[0], place_ref[0], table_ref[0])
    clip = lax.div(code, clip_tokens)
    rows = jnp.concatenate([ref[...].astype(F32) for ref in block_refs], axis=0)
    average = jnp.mean(rows, axis=-1, keepdims=True)
    centered = rows - average
    variance = jnp.mean(centered * centered, axis=-1, keepdims=True)
    normed = centered * lax.rsqrt(variance + EPSILON)
    shift = pick(clip, modulation_ref[0].astype(F32))
    scale = pick(clip, modulation_ref[1].astype(F32))
    out_ref[...] = (normed * (1.0 + scale) + shift).astype(BF16)


def project_kernel(head_size, weight_ref, gain_ref, *refs):
    hidden_refs, out_ref = refs[:-1], refs[-1]
    hidden = jnp.concatenate([ref[...] for ref in hidden_refs], axis=0)
    projected = lax.dot_general(
        weight_ref[...], hidden, (((1,), (1,)), ((), ())), preferred_element_type=F32
    )
    width = weight_ref.shape[0] // 3
    shape = (head_size, head_size)
    diagonal = lax.broadcasted_iota(jnp.int32, shape, 0) == lax.broadcasted_iota(
        jnp.int32, shape, 1
    )
    found = []
    for part in range(2):
        gain = jnp.sum(
            jnp.where(diagonal, gain_ref[part : part + 1, :], 0.0), axis=1, keepdims=True
        )
        for start in range(part * width, (part + 1) * width, head_size):
            value = projected[start : start + head_size]
            square = jnp.sum(value * value, axis=0, keepdims=True) * (1.0 / head_size)
            found.append(value * lax.rsqrt(square + EPSILON) * gain)
    found.append(projected[2 * width :])
    out_ref[...] = jnp.concatenate(found, axis=0).astype(BF16)


def attention_kernel(
    head_size, per_peer, piece_rows, length_ref, owner_ref, place_ref, table_ref, *refs
):
    part_refs, out_refs, all_ref = refs[:2], refs[2:-1], refs[-1]
    stacked = jnp.concatenate([ref[...] for ref in part_refs], axis=1)
    width, tokens = stacked.shape[0] // 3, stacked.shape[1]
    seq_count = len(out_refs)
    clips, per_clip = table_ref.shape[1:]
    clip_tokens = tokens // clips
    group_rows = tokens // 2 // seq_count
    token = lax.broadcasted_iota(jnp.int32, (1, tokens), 1)
    row = lax.rem(token, group_rows)
    block = lax.div(token, group_rows)
    piece = lax.div(block, seq_count) * (group_rows // piece_rows) + lax.div(row, piece_rows)
    arrival = arrival_of(piece, per_peer, owner_ref[0])
    found = jnp.zeros_like(token)
    for clip in range(clips):
        for p in range(per_clip):
            found = jnp.where(arrival == table_ref[0, clip, p], clip * per_clip + p, found)
    source = jnp.bitwise_xor(lax.rem(block, seq_count), place_ref[0])
    code = found * (piece_rows * seq_count) + source * piece_rows + lax.rem(row, piece_rows)
    position = lax.broadcasted_iota(jnp.int32, (clip_tokens, 1), 0)
    key = lax.broadcasted_iota(jnp.int32, (8, clip_tokens), 1)
    heads = range(0, width, head_size)
    scale = math.log2(math.e) / math.sqrt(head_size)
    for clip in range(clips):
        chosen = jnp.where(code == position + clip * clip_tokens, 1.0, 0.0).astype(BF16)
        picked = lax.dot_general(
            stacked, chosen, (((1,), (1,)), ((), ())), preferred_element_type=F32
        )
        in_clip = jnp.where(key < length_ref[0, clip], 1.0, 0.0)
        scores = [
            jnp.dot(
                jnp.transpose(picked[width + head : width + head + head_size]).astype(BF16),
                picked[head : head + head_size].astype(BF16),
                preferred_element_type=F32,
            )
            for head in heads
        ]
        unscaled = [jnp.exp2(score * scale).astype(BF16) for score in scores]
        outs = []
        for head, weights in zip(heads, unscaled):
            values = picked[2 * width + head : 2 * width + head + head_size] * in_clip[:1]
            values = jnp.concatenate([values, in_clip], axis=0).astype(BF16)
            summed = jnp.dot(values, weights, preferred_element_type=F32)
            outs.append(summed[:head_size] * (1.0 / summed[head_size : head_size + 1]))
        attended = jnp.concatenate(outs, axis=0).astype(BF16)
        back = jnp.dot(attended, chosen, preferred_element_type=F32)
        if clip == 0:
            all_ref[...] = back
        else:
            all_ref[...] += back
    for index, ref in enumerate(out_refs):
        for group in range(2):
            start = (group * seq_count + index) * group_rows
            ref[:, group * group_rows : (group + 1) * group_rows] = all_ref[
                :, start : start + group_rows
            ].astype(BF16)


def output_kernel(
    seq_count,
    halves,
    clip_tokens,
    codes_of,
    core_ref,
    length_ref,
    owner_ref,
    place_ref,
    table_ref,
    modulation_ref,
    weight_ref,
    *refs,
):
    head_refs, refs = refs[:seq_count], refs[seq_count:]
    fetched = seq_count - 2 + halves
    fetched_refs, refs = refs[:fetched], refs[fetched:]
    count = len(refs) // 3
    block_refs, out_refs = refs[:count], refs[count:]
    rows = out_refs[0].shape[0]
    branch = None
    for mask in range(seq_count):
        if mask == 0:
            weight = weight_ref[...]
        else:
            parts = [fetched_refs[mask - 1][...]]
            if halves == 2:
                half = parts[0].shape[0]
                parts.append(fetched_refs[-1][(mask - 1) * half : mask * half])
                first = core_ref[0] == 0
                parts = [
                    jnp.where(first, parts[0], parts[1]),
                    jnp.where(first, parts[1], parts[0]),
                ]
            weight = jnp.concatenate(parts, axis=0)
        term = lax.dot_general(
            head_refs[mask][...],
            weight,
            (((0,), (0,)), ((), ())),
            preferred_element_type=F32,
        )
        branch = term if branch is None else branch + term
    code = codes_of(branch.shape[0], owner_ref[0], place_ref[0], table_ref[0])
    clip = lax.div(code, clip_tokens)
    limit = jnp.zeros_like(code)
    for index in range(length_ref.shape[1]):
        limit = jnp.where(clip == index, length_ref[0, index], limit)
    kept = lax.rem(code, clip_tokens) < limit
    branch = pick(clip, modulation_ref[2].astype(F32)) * branch
    for index, out_ref in enumerate(out_refs):
        at = slice(index * rows, (index + 1) * rows)
        side = slice(index % 2 * rows, (index % 2 + 1) * rows)
        result = block_refs[index // 2][side].astype(F32) + branch[at]
        out_ref[...] = jnp.where(kept[at], result, 0.0).astype(BF16)


def body(
    tokens, slot_owner, clip_pieces, clip_length, modulation, qkv_weight, qk_gain, proj_weight
):
    dp_count = lax.axis_size("dp")
    seq_count = lax.axis_size("seq")
    pieces_here = tokens.shape[1]
    piece_rows = tokens.shape[2]
    model_width = tokens.shape[3]
    per_peer = pieces_here // dp_count
    head_size = qk_gain.shape[1]
    heads = HEADS // seq_count
    head_width = heads * head_size
    clips_here, per_clip = clip_pieces.shape[1:]
    clip_tokens = per_clip * piece_rows * seq_count
    block_rows = per_peer * piece_rows
    rows_here = pieces_here * piece_rows
    group_rows = rows_here // 2
    chips = dp_count // 2
    owner_place = lax.axis_index("dp").astype(jnp.int32)
    place = lax.axis_index("seq").astype(jnp.int32).reshape(1)
    core = lax.rem(owner_place, 2).reshape(1)
    owner_place = owner_place.reshape(1)
    halves = 2 if heads % 2 == 0 else 1

    smem = pl.BlockSpec(memory_space=pltpu.SMEM)
    vmem = pl.BlockSpec(memory_space=pltpu.VMEM)

    def call(
        kernel, scalars, inputs, outputs, scratch=(), out_scalars=0, limit=16, flops=10**9, where=vmem
    ):
        return pl.pallas_call(
            kernel,
            in_specs=[smem] * len(scalars) + [where] * len(inputs),
            out_specs=[smem] * out_scalars + [vmem] * (len(outputs) - out_scalars),
            out_shape=[jax.ShapeDtypeStruct(shape, dtype) for shape, dtype in outputs],
            scratch_shapes=list(scratch),
            compiler_params=pltpu.CompilerParams(vmem_limit_bytes=limit * 2**20),
            cost_estimate=pl.CostEstimate(
                flops=flops, bytes_accessed=2**20, transcendentals=0
            ),
        )(*scalars, *inputs)

    x_count = math.isqrt(seq_count)
    anywhere = pl.BlockSpec(memory_space=pl.ANY)
    proj_own = proj_weight
    if halves == 2:
        (proj_own,) = call(
            half_kernel,
            [core],
            [proj_weight],
            [((head_width // 2, model_width), BF16)],
            scratch=[pltpu.SemaphoreType.DMA],
            where=anywhere,
        )
    proj_parts = {mask: send(proj_own, "seq", mask) for mask in range(1, x_count)}
    for mask in range(x_count, seq_count, x_count):
        proj_parts[mask] = send(proj_own, "seq", mask)

    slots, own, other = call(
        functools.partial(route_kernel, per_peer, piece_rows),
        [owner_place],
        [slot_owner, tokens],
        [((pieces_here,), jnp.int32)] + [((chips * block_rows, model_width), BF16)] * 2,
        scratch=[
            pltpu.SMEM((dp_count,), jnp.int32),
            pltpu.SMEM(slot_owner.shape, jnp.int32),
            pltpu.VMEM(tokens.shape, BF16),
            pltpu.SemaphoreType.DMA((2,)),
        ],
        out_scalars=1,
        where=anywhere,
    )
    payloads = call(
        functools.partial(merge_kernel, block_rows),
        [],
        [own, send(other, "dp", 1)],
        [((2 * block_rows, model_width), BF16)] * chips,
    )
    arrived = [send(payloads[mask], "dp", 2 * mask) for mask in range(chips // 2)]
    arrived, payloads = lax.optimization_barrier((arrived, payloads))
    arrived += [send(payloads[mask], "dp", 2 * mask) for mask in range(chips // 2, chips)]

    def codes_of(group):
        return lambda rows, *places: row_codes(
            rows,
            group * (pieces_here // 2),
            per_peer,
            piece_rows,
            piece_rows * seq_count,
            *places,
        )

    weight = jnp.transpose(qkv_weight, (1, 2, 0)).reshape(3 * head_width, model_width)
    factors = jnp.transpose(modulation[0], (1, 0, 2))
    stacked, arriving = [], []
    for group in range(2):
        blocks = arrived[group * chips // 2 : (group + 1) * chips // 2]
        (hidden,) = call(
            functools.partial(norm_kernel, clip_tokens, codes_of(group)),
            [owner_place, place],
            [clip_pieces, factors] + blocks,
            [((group_rows, model_width), BF16)],
            flops=(1 + 10 * group) * 10**9,
        )
        if group == 0:
            hidden, proj_parts = lax.optimization_barrier((hidden, proj_parts))
        else:
            hidden, hiddens = lax.optimization_barrier((hidden, hiddens))
            arriving[0] = hiddens
        hiddens = [send(hidden, "seq", mask) for mask in range(seq_count)]
        arriving.append(hiddens)
    for hiddens in arriving:
        (projected,) = call(
            functools.partial(project_kernel, head_size),
            [],
            [weight, qk_gain] + hiddens,
            [((3 * head_width, seq_count * group_rows), BF16)],
            flops=3 * 10**9,
        )
        stacked.append(projected)

    if seq_count > 1:
        hiddens[x_count], proj_parts = lax.optimization_barrier((hiddens[x_count], proj_parts))
    for mask in range(x_count, seq_count):
        if mask % x_count > 0:
            proj_parts[mask] = send(proj_parts[mask - mask % x_count], "seq", mask % x_count)
    proj_parts = [proj_parts[mask] for mask in range(1, seq_count)]

    attended = call(
        functools.partial(attention_kernel, head_size, per_peer, piece_rows),
        [clip_length, owner_place, place, clip_pieces],
        stacked,
        [((head_width, rows_here), BF16)] * seq_count,
        scratch=[pltpu.VMEM((head_width, seq_count * rows_here), F32)],
        limit=16 if clip_tokens <= 256 else 48,
        flops=8 * 10**9,
    )
    returned = [send(array, "seq", mask) for mask, array in enumerate(attended)]
    _, proj_parts = lax.optimization_barrier((attended[0], proj_parts))
    if halves == 2:
        (joined,) = call(
            join_kernel,
            [],
            proj_parts,
            [(((seq_count - 1) * head_width // 2, model_width), BF16)],
        )
        proj_parts.append(send(joined, "dp", 1))

    results = call(
        functools.partial(output_kernel, seq_count, halves, clip_tokens, codes_of(0)),
        [core, clip_length, owner_place, place],
        [clip_pieces, factors, proj_weight] + returned + proj_parts + arrived,
        [((block_rows, model_width), BF16)] * dp_count,
        flops=3 * 10**9,
    )
    order = list(range(dp_count // 2, dp_count)) + list(range(dp_count // 2))
    came_back = [send(results[mask], "dp", mask) for mask in order]
    (out,) = call(
        functools.partial(place_kernel, per_peer, piece_rows, order),
        [slots],
        came_back,
        [(tokens.shape, BF16)],
    )
    return out


def solution(mesh):
    return jax.shard_map(
        body,
        mesh=mesh,
        in_specs=(
            P("dp", None, "seq", None),
            P("dp", None),
            P("dp", None, None),
            P("dp", None),
            P("dp", None, None, None),
            P(None, None, "seq"),
            P(),
            P("seq", None),
        ),
        out_specs=P("dp", None, "seq", None),
        check_vma=False,
    )
```

```python
import functools
import math

import jax
import jax.numpy as jnp
from jax import lax
from jax.experimental import pallas as pl
from jax.experimental.pallas import tpu as pltpu
from jax.sharding import PartitionSpec as P

HEADS = 16
EPSILON = 1e-06
BF16 = jnp.bfloat16
F32 = jnp.float32


def send(array, axis, mask):
    if mask == 0:
        return array
    count = lax.axis_size(axis)
    return lax.ppermute(array, axis, [(i, i ^ mask) for i in range(count)])


def route_kernel(per_peer, piece_rows, place_ref, owner_hbm, token_hbm, *refs):
    slot_ref, own_ref, other_ref, filled_ref, owner_ref, token_ref, sems = refs
    peers = filled_ref.shape[0]
    owner_copy = pltpu.make_async_copy(owner_hbm, owner_ref, sems.at[0])
    token_copy = pltpu.make_async_copy(token_hbm, token_ref, sems.at[1])
    owner_copy.start()
    token_copy.start()
    for peer in range(peers):
        filled_ref[peer] = peer * per_peer
    owner_copy.wait()

    @pl.loop(0, peers * per_peer, unroll=8)
    def _(slot):
        peer = jnp.bitwise_xor(owner_ref[0, slot], place_ref[0])
        at = filled_ref[peer]
        filled_ref[peer] = at + 1
        slot_ref[at] = slot

    token_copy.wait()
    for peer in range(peers):
        ref = own_ref if peer % 2 == 0 else other_ref
        for m in range(per_peer):
            at = (peer // 2 * per_peer + m) * piece_rows
            ref[at : at + piece_rows, :] = token_ref[0, slot_ref[peer * per_peer + m]]


def merge_kernel(rows, own_ref, other_ref, *refs):
    for index, ref in enumerate(refs):
        ref[:rows] = own_ref[index * rows : (index + 1) * rows]
        ref[rows:] = other_ref[index * rows : (index + 1) * rows]


def sides_kernel(*refs):
    count = len(refs) // 2
    for index in range(count):
        rows = refs[count + index].shape[0]
        start = 0 if index < count // 2 else rows
        refs[count + index][...] = refs[index][start : start + rows]


def half_kernel(core_ref, weight_hbm, out_ref, sem):
    rows = out_ref.shape[0]
    start = pl.multiple_of(core_ref[0] * rows, 16)
    copy = pltpu.make_async_copy(weight_hbm.at[pl.ds(start, rows), :], out_ref, sem)
    copy.start()
    copy.wait()


def place_kernel(per_peer, piece_rows, order, slot_ref, *refs):
    block_refs, out_ref = refs[:-1], refs[-1]
    for peer, ref in zip(order, block_refs):
        for m in range(per_peer):
            slot = slot_ref[peer * per_peer + m]
            out_ref[0, slot] = ref[m * piece_rows : (m + 1) * piece_rows, :]


def arrival_of(piece, per_peer, owner_place):
    source = jnp.bitwise_xor(lax.div(piece, per_peer), owner_place)
    return source * per_peer + lax.rem(piece, per_peer)


def row_codes(rows, first_piece, per_peer, piece_rows, token_rows, owner_place, place, table):
    row = lax.broadcasted_iota(jnp.int32, (rows, 1), 0)
    arrival = arrival_of(first_piece + lax.div(row, piece_rows), per_peer, owner_place)
    lane = lax.broadcasted_iota(jnp.int32, (1, table.shape[1]), 1)
    found = jnp.zeros((rows, 1), jnp.int32)
    for clip in range(table.shape[0]):
        number = jnp.where(
            arrival == table[clip : clip + 1], lane + clip * table.shape[1], 0
        )
        found += jnp.sum(number, axis=1, keepdims=True)
    return found * token_rows + place * piece_rows + lax.rem(row, piece_rows)


def pick(clip, table):
    rows = jnp.broadcast_to(table[0:1], (clip.shape[0], table.shape[1]))
    for index in range(1, table.shape[0]):
        rows = jnp.where(clip == index, table[index : index + 1], rows)
    return rows


def norm_kernel(
    clip_tokens, codes_of, owner_ref, place_ref, table_ref, modulation_ref, *refs
):
    block_refs, out_ref = refs[:-1], refs[-1]
    code = codes_of(out_ref.shape[0], owner_ref[0], place_ref[0], table_ref[0])
    clip = lax.div(code, clip_tokens)
    rows = jnp.concatenate([ref[...].astype(F32) for ref in block_refs], axis=0)
    average = jnp.mean(rows, axis=-1, keepdims=True)
    centered = rows - average
    variance = jnp.mean(centered * centered, axis=-1, keepdims=True)
    normed = centered * lax.rsqrt(variance + EPSILON)
    shift = pick(clip, modulation_ref[0].astype(F32))
    scale = pick(clip, modulation_ref[1].astype(F32))
    out_ref[...] = (normed * (1.0 + scale) + shift).astype(BF16)


def project_kernel(head_size, weight_ref, gain_ref, *refs):
    hidden_refs, out_ref = refs[:-1], refs[-1]
    hidden = jnp.concatenate([ref[...] for ref in hidden_refs], axis=0)
    projected = lax.dot_general(
        weight_ref[...], hidden, (((1,), (1,)), ((), ())), preferred_element_type=F32
    )
    width = weight_ref.shape[0] // 3
    shape = (head_size, head_size)
    diagonal = lax.broadcasted_iota(jnp.int32, shape, 0) == lax.broadcasted_iota(
        jnp.int32, shape, 1
    )
    found = []
    for part in range(2):
        gain = jnp.sum(
            jnp.where(diagonal, gain_ref[part : part + 1, :], 0.0), axis=1, keepdims=True
        )
        for start in range(part * width, (part + 1) * width, head_size):
            value = projected[start : start + head_size]
            square = jnp.sum(value * value, axis=0, keepdims=True) * (1.0 / head_size)
            found.append(value * lax.rsqrt(square + EPSILON) * gain)
    found.append(projected[2 * width :])
    out_ref[...] = jnp.concatenate(found, axis=0).astype(BF16)


def attention_kernel(
    head_size, per_peer, piece_rows, length_ref, owner_ref, place_ref, table_ref, *refs
):
    part_refs, out_refs, all_ref = refs[:2], refs[2:-1], refs[-1]
    stacked = jnp.concatenate([ref[...] for ref in part_refs], axis=1)
    width, tokens = stacked.shape[0] // 3, stacked.shape[1]
    seq_count = len(out_refs)
    clips, per_clip = table_ref.shape[1:]
    clip_tokens = tokens // clips
    group_rows = tokens // 2 // seq_count
    token = lax.broadcasted_iota(jnp.int32, (1, tokens), 1)
    row = lax.rem(token, group_rows)
    block = lax.div(token, group_rows)
    piece = lax.div(block, seq_count) * (group_rows // piece_rows) + lax.div(row, piece_rows)
    arrival = arrival_of(piece, per_peer, owner_ref[0])
    found = jnp.zeros_like(token)
    for clip in range(clips):
        for p in range(per_clip):
            found = jnp.where(arrival == table_ref[0, clip, p], clip * per_clip + p, found)
    source = jnp.bitwise_xor(lax.rem(block, seq_count), place_ref[0])
    code = found * (piece_rows * seq_count) + source * piece_rows + lax.rem(row, piece_rows)
    position = lax.broadcasted_iota(jnp.int32, (clip_tokens, 1), 0)
    key = lax.broadcasted_iota(jnp.int32, (8, clip_tokens), 1)
    heads = range(0, width, head_size)
    scale = math.log2(math.e) / math.sqrt(head_size)
    for clip in range(clips):
        chosen = jnp.where(code == position + clip * clip_tokens, 1.0, 0.0).astype(BF16)
        picked = lax.dot_general(
            stacked, chosen, (((1,), (1,)), ((), ())), preferred_element_type=F32
        )
        in_clip = jnp.where(key < length_ref[0, clip], 1.0, 0.0)
        scores = [
            jnp.dot(
                jnp.transpose(picked[width + head : width + head + head_size]).astype(BF16),
                picked[head : head + head_size].astype(BF16),
                preferred_element_type=F32,
            )
            for head in heads
        ]
        unscaled = [jnp.exp2(score * scale).astype(BF16) for score in scores]
        outs = []
        for head, weights in zip(heads, unscaled):
            values = picked[2 * width + head : 2 * width + head + head_size] * in_clip[:1]
            values = jnp.concatenate([values, in_clip], axis=0).astype(BF16)
            summed = jnp.dot(values, weights, preferred_element_type=F32)
            outs.append(summed[:head_size] * (1.0 / summed[head_size : head_size + 1]))
        attended = jnp.concatenate(outs, axis=0).astype(BF16)
        back = jnp.dot(attended, chosen, preferred_element_type=F32)
        if clip == 0:
            all_ref[...] = back
        else:
            all_ref[...] += back
    for index, ref in enumerate(out_refs):
        for group in range(2):
            start = (group * seq_count + index) * group_rows
            ref[:, group * group_rows : (group + 1) * group_rows] = all_ref[
                :, start : start + group_rows
            ].astype(BF16)


def output_kernel(
    seq_count,
    halves,
    clip_tokens,
    codes_of,
    core_ref,
    length_ref,
    owner_ref,
    place_ref,
    table_ref,
    modulation_ref,
    weight_ref,
    *refs,
):
    head_refs, refs = refs[:seq_count], refs[seq_count:]
    fetched = (seq_count - 1) * halves
    fetched_refs, refs = refs[:fetched], refs[fetched:]
    count = len(refs) // 3
    block_refs, out_refs = refs[:count], refs[count:]
    rows = out_refs[0].shape[0]
    branch = None
    for mask in range(seq_count):
        if mask == 0:
            weight = weight_ref[...]
        else:
            parts = [ref[...] for ref in fetched_refs[mask - 1 :: seq_count - 1]]
            if halves == 2:
                first = core_ref[0] == 0
                parts = [
                    jnp.where(first, parts[0], parts[1]),
                    jnp.where(first, parts[1], parts[0]),
                ]
            weight = jnp.concatenate(parts, axis=0)
        term = lax.dot_general(
            head_refs[mask][...],
            weight,
            (((0,), (0,)), ((), ())),
            preferred_element_type=F32,
        )
        branch = term if branch is None else branch + term
    code = codes_of(branch.shape[0], owner_ref[0], place_ref[0], table_ref[0])
    clip = lax.div(code, clip_tokens)
    limit = jnp.zeros_like(code)
    for index in range(length_ref.shape[1]):
        limit = jnp.where(clip == index, length_ref[0, index], limit)
    kept = lax.rem(code, clip_tokens) < limit
    branch = pick(clip, modulation_ref[2].astype(F32)) * branch
    for index, out_ref in enumerate(out_refs):
        at = slice(index * rows, (index + 1) * rows)
        side = slice(index % 2 * rows, (index % 2 + 1) * rows)
        result = block_refs[index // 2][side].astype(F32) + branch[at]
        out_ref[...] = jnp.where(kept[at], result, 0.0).astype(BF16)


def body(
    tokens, slot_owner, clip_pieces, clip_length, modulation, qkv_weight, qk_gain, proj_weight
):
    dp_count = lax.axis_size("dp")
    seq_count = lax.axis_size("seq")
    pieces_here = tokens.shape[1]
    piece_rows = tokens.shape[2]
    model_width = tokens.shape[3]
    per_peer = pieces_here // dp_count
    head_size = qk_gain.shape[1]
    heads = HEADS // seq_count
    head_width = heads * head_size
    clips_here, per_clip = clip_pieces.shape[1:]
    clip_tokens = per_clip * piece_rows * seq_count
    block_rows = per_peer * piece_rows
    rows_here = pieces_here * piece_rows
    group_rows = rows_here // 2
    chips = dp_count // 2
    owner_place = lax.axis_index("dp").astype(jnp.int32)
    place = lax.axis_index("seq").astype(jnp.int32).reshape(1)
    core = lax.rem(owner_place, 2).reshape(1)
    owner_place = owner_place.reshape(1)
    halves = 2 if heads % 2 == 0 else 1

    smem = pl.BlockSpec(memory_space=pltpu.SMEM)
    vmem = pl.BlockSpec(memory_space=pltpu.VMEM)

    def call(
        kernel, scalars, inputs, outputs, scratch=(), out_scalars=0, limit=16, flops=10**9, where=vmem
    ):
        return pl.pallas_call(
            kernel,
            in_specs=[smem] * len(scalars) + [where] * len(inputs),
            out_specs=[smem] * out_scalars + [vmem] * (len(outputs) - out_scalars),
            out_shape=[jax.ShapeDtypeStruct(shape, dtype) for shape, dtype in outputs],
            scratch_shapes=list(scratch),
            compiler_params=pltpu.CompilerParams(vmem_limit_bytes=limit * 2**20),
            cost_estimate=pl.CostEstimate(
                flops=flops, bytes_accessed=2**20, transcendentals=0
            ),
        )(*scalars, *inputs)

    x_count = math.isqrt(seq_count)
    anywhere = pl.BlockSpec(memory_space=pltpu.HBM)
    along_x = list(range(1, x_count))
    along_y = list(range(x_count, seq_count, x_count))

    def proj_half(array, flops):
        if halves == 1:
            return array
        return call(
            half_kernel,
            [core],
            [array],
            [((head_width // 2, model_width), BF16)],
            scratch=[pltpu.SemaphoreType.DMA],
            where=anywhere,
            flops=flops,
        )[0]

    proj_own = proj_half(proj_weight, 10**9)
    proj_parts = {mask: send(proj_own, "seq", mask) for mask in along_y}

    slots, own, other = call(
        functools.partial(route_kernel, per_peer, piece_rows),
        [owner_place],
        [slot_owner, tokens],
        [((pieces_here,), jnp.int32)] + [((chips * block_rows, model_width), BF16)] * 2,
        scratch=[
            pltpu.SMEM((dp_count,), jnp.int32),
            pltpu.SMEM(slot_owner.shape, jnp.int32),
            pltpu.VMEM(tokens.shape, BF16),
            pltpu.SemaphoreType.DMA((2,)),
        ],
        out_scalars=1,
        where=anywhere,
    )
    payloads = call(
        functools.partial(merge_kernel, block_rows),
        [],
        [own, send(other, "dp", 1)],
        [((2 * block_rows, model_width), BF16)] * chips,
    )
    payloads, proj_late = lax.optimization_barrier((payloads, proj_weight))
    arrived = [send(payload, "dp", 2 * mask) for mask, payload in enumerate(payloads)]
    proj_own = proj_half(proj_late, 5 * 10**9)
    proj_side = {mask: send(proj_own, "seq", mask) for mask in along_x}

    def codes_of(group):
        return lambda rows, *places: row_codes(
            rows,
            group * (pieces_here // 2),
            per_peer,
            piece_rows,
            piece_rows * seq_count,
            *places,
        )

    weight = jnp.transpose(qkv_weight, (1, 2, 0)).reshape(3 * head_width, model_width)
    factors = jnp.transpose(modulation[0], (1, 0, 2))
    stacked, arriving = [], []
    for group in range(2):
        (hidden,) = call(
            functools.partial(norm_kernel, clip_tokens, codes_of(group)),
            [owner_place, place],
            [clip_pieces, factors] + arrived[group * chips // 2 : (group + 1) * chips // 2],
            [((group_rows, model_width), BF16)],
            flops=(1 + 10 * group) * 10**9,
        )
        if group == 0:
            hidden, proj_parts = lax.optimization_barrier((hidden, proj_parts))
        else:
            hidden, arriving[0], proj_side = lax.optimization_barrier(
                (hidden, arriving[0], proj_side)
            )
        arriving.append({0: hidden} | {m: send(hidden, "seq", m) for m in along_y + along_x})
    for group in range(2):
        blocks = arriving[group]
        halved = call(
            sides_kernel,
            [],
            [blocks[mask] for mask in along_y + along_x],
            [((group_rows // 2, model_width), BF16)] * (len(along_y) + len(along_x)),
        )
        halved = dict(zip(along_y + along_x, halved))
        diagonal = {}
        for my in along_y:
            for mx in along_x:
                diagonal[my + mx] = [send(halved[my], "seq", mx), send(halved[mx], "seq", my)]
        if group == 0:
            diagonal, arriving[1] = lax.optimization_barrier((diagonal, arriving[1]))
        blocks |= diagonal
        (projected,) = call(
            functools.partial(project_kernel, head_size),
            [],
            [weight, qk_gain]
            + [
                part
                for mask in range(seq_count)
                for part in (blocks[mask] if mask in diagonal else [blocks[mask]])
            ],
            [((3 * head_width, seq_count * group_rows), BF16)],
            flops=3 * 10**9,
        )
        stacked.append(projected)

    proj_parts |= proj_side
    stacked[0], proj_parts = lax.optimization_barrier((stacked[0], proj_parts))
    swapped = {mask: send(proj_parts[mask], "dp", 1) for mask in proj_parts} if halves == 2 else {}
    stacked[1], swapped = lax.optimization_barrier((stacked[1], swapped))
    for my in along_y:
        for mx in along_x:
            proj_parts[my + mx] = send(proj_parts[my], "seq", mx)

    attended = call(
        functools.partial(attention_kernel, head_size, per_peer, piece_rows),
        [clip_length, owner_place, place, clip_pieces],
        stacked,
        [((head_width, rows_here), BF16)] * seq_count,
        scratch=[pltpu.VMEM((head_width, seq_count * rows_here), F32)],
        limit=16 if clip_tokens <= 256 else 48,
        flops=8 * 10**9,
    )
    returned = [send(array, "seq", mask) for mask, array in enumerate(attended)]
    if halves == 2:
        _, late = lax.optimization_barrier((attended[0], proj_parts))
        for mask in range(1, seq_count):
            if mask not in swapped:
                swapped[mask] = send(late[mask], "dp", 1)
        proj_parts = proj_parts | {seq_count + mask: swapped[mask] for mask in swapped}
    proj_parts = [proj_parts[mask] for mask in sorted(proj_parts)]

    results = call(
        functools.partial(output_kernel, seq_count, halves, clip_tokens, codes_of(0)),
        [core, clip_length, owner_place, place],
        [clip_pieces, factors, proj_weight] + returned + proj_parts + arrived,
        [((block_rows, model_width), BF16)] * dp_count,
        flops=3 * 10**9,
    )
    order = list(range(dp_count // 2, dp_count)) + list(range(dp_count // 2))
    came_back = [send(results[mask], "dp", mask) for mask in order]
    (out,) = call(
        functools.partial(place_kernel, per_peer, piece_rows, order),
        [slots],
        came_back,
        [(tokens.shape, BF16)],
    )
    return out


def solution(mesh):
    return jax.shard_map(
        body,
        mesh=mesh,
        in_specs=(
            P("dp", None, "seq", None),
            P("dp", None),
            P("dp", None, None),
            P("dp", None),
            P("dp", None, None, None),
            P(None, None, "seq"),
            P(),
            P("seq", None),
        ),
        out_specs=P("dp", None, "seq", None),
        check_vma=False,
    )
```

```python
import functools
import math

import jax
import jax.numpy as jnp
from jax import lax
from jax.experimental import pallas as pl
from jax.experimental.pallas import tpu as pltpu
from jax.sharding import PartitionSpec as P

HEADS = 16
EPSILON = 1e-06
BF16 = jnp.bfloat16
F32 = jnp.float32


def send(array, axis, mask):
    if mask == 0:
        return array
    count = lax.axis_size(axis)
    return lax.ppermute(array, axis, [(i, i ^ mask) for i in range(count)])


def route_kernel(per_peer, piece_rows, place_ref, owner_hbm, token_hbm, *refs):
    slot_ref, own_ref, other_ref, filled_ref, owner_ref, token_ref, sems = refs
    peers = filled_ref.shape[0]
    owner_copy = pltpu.make_async_copy(owner_hbm, owner_ref, sems.at[0])
    token_copy = pltpu.make_async_copy(token_hbm, token_ref, sems.at[1])
    owner_copy.start()
    token_copy.start()
    for peer in range(peers):
        filled_ref[peer] = peer * per_peer
    owner_copy.wait()

    @pl.loop(0, peers * per_peer, unroll=8)
    def _(slot):
        peer = jnp.bitwise_xor(owner_ref[0, slot], place_ref[0])
        at = filled_ref[peer]
        filled_ref[peer] = at + 1
        slot_ref[at] = slot

    token_copy.wait()
    for peer in range(peers):
        ref = own_ref if peer % 2 == 0 else other_ref
        for m in range(per_peer):
            at = (peer // 2 * per_peer + m) * piece_rows
            ref[at : at + piece_rows, :] = token_ref[0, slot_ref[peer * per_peer + m]]


def merge_kernel(rows, own_ref, other_ref, *refs):
    for index, ref in enumerate(refs):
        ref[:rows] = own_ref[index * rows : (index + 1) * rows]
        ref[rows:] = other_ref[index * rows : (index + 1) * rows]


def cut_kernel(starts, *refs):
    count = len(refs) // 2
    for start, ref, out_ref in zip(starts, refs[:count], refs[count:]):
        out_ref[...] = ref[start : start + out_ref.shape[0]]


def place_kernel(per_peer, piece_rows, order, slot_ref, *refs):
    block_refs, out_ref = refs[:-1], refs[-1]
    for peer, ref in zip(order, block_refs):
        for m in range(per_peer):
            slot = slot_ref[peer * per_peer + m]
            out_ref[0, slot] = ref[m * piece_rows : (m + 1) * piece_rows, :]


def arrival_of(piece, per_peer, owner_place):
    source = jnp.bitwise_xor(lax.div(piece, per_peer), owner_place)
    return source * per_peer + lax.rem(piece, per_peer)


def row_codes(rows, first_piece, per_peer, piece_rows, token_rows, owner_place, place, table):
    row = lax.broadcasted_iota(jnp.int32, (rows, 1), 0)
    arrival = arrival_of(first_piece + lax.div(row, piece_rows), per_peer, owner_place)
    lane = lax.broadcasted_iota(jnp.int32, (1, table.shape[1]), 1)
    found = jnp.zeros((rows, 1), jnp.int32)
    for clip in range(table.shape[0]):
        number = jnp.where(
            arrival == table[clip : clip + 1], lane + clip * table.shape[1], 0
        )
        found += jnp.sum(number, axis=1, keepdims=True)
    return found * token_rows + place * piece_rows + lax.rem(row, piece_rows)


def pick(clip, table):
    rows = jnp.broadcast_to(table[0:1], (clip.shape[0], table.shape[1]))
    for index in range(1, table.shape[0]):
        rows = jnp.where(clip == index, table[index : index + 1], rows)
    return rows


def normed_rows(rows, code, clip_tokens, factors):
    clip = lax.div(code, clip_tokens)
    average = jnp.mean(rows, axis=-1, keepdims=True)
    centered = rows - average
    variance = jnp.mean(centered * centered, axis=-1, keepdims=True)
    normed = centered * lax.rsqrt(variance + EPSILON)
    shift = pick(clip, factors[0].astype(F32))
    scale = pick(clip, factors[1].astype(F32))
    return (normed * (1.0 + scale) + shift).astype(BF16)


def near_kernel(
    clip_tokens, codes_of, core_ref, owner_ref, place_ref, table_ref, factor_ref, weight_ref, *refs
):
    block_ref, out_ref = refs
    rows = block_ref.shape[0]
    sent = out_ref.shape[0] - rows
    code = codes_of(rows, owner_ref[0], place_ref[0], table_ref[0])
    out_ref[:rows] = normed_rows(block_ref[...].astype(F32), code, clip_tokens, factor_ref)
    if sent < weight_ref.shape[0]:
        start = pl.multiple_of(core_ref[0] * sent, 16)
        out_ref[rows:] = weight_ref[pl.ds(start, sent), :]
    else:
        out_ref[rows:] = weight_ref[...]


def far_kernel(clip_tokens, codes_of, owner_ref, place_ref, table_ref, factor_ref, *refs):
    block_refs, out_ref = refs[:-1], refs[-1]
    code = codes_of(out_ref.shape[0], owner_ref[0], place_ref[0], table_ref[0])
    rows = jnp.concatenate([ref[...].astype(F32) for ref in block_refs], axis=0)
    out_ref[...] = normed_rows(rows, code, clip_tokens, factor_ref)


def project_kernel(head_size, rows, weight_ref, gain_ref, *refs):
    hidden_refs, out_ref = refs[:-1], refs[-1]
    hidden = jnp.concatenate([ref[: min(rows, ref.shape[0])] for ref in hidden_refs], axis=0)
    projected = lax.dot_general(
        weight_ref[...], hidden, (((1,), (1,)), ((), ())), preferred_element_type=F32
    )
    width = weight_ref.shape[0] // 3
    shape = (head_size, head_size)
    diagonal = lax.broadcasted_iota(jnp.int32, shape, 0) == lax.broadcasted_iota(
        jnp.int32, shape, 1
    )
    found = []
    for part in range(2):
        gain = jnp.sum(
            jnp.where(diagonal, gain_ref[part : part + 1, :], 0.0), axis=1, keepdims=True
        )
        for start in range(part * width, (part + 1) * width, head_size):
            value = projected[start : start + head_size]
            square = jnp.sum(value * value, axis=0, keepdims=True) * (1.0 / head_size)
            found.append(value * lax.rsqrt(square + EPSILON) * gain)
    found.append(projected[2 * width :])
    out_ref[...] = jnp.concatenate(found, axis=0).astype(BF16)


def token_codes(masks, first_row, rows, per_peer, piece_rows, owner_ref, place_ref, table_ref):
    clips, per_clip = table_ref.shape[1:]
    token = lax.broadcasted_iota(jnp.int32, (1, len(masks) * rows), 1)
    segment = lax.div(token, rows)
    row = first_row + lax.rem(token, rows)
    arrival = arrival_of(lax.div(row, piece_rows), per_peer, owner_ref[0])
    found = jnp.zeros_like(token)
    for clip in range(clips):
        for p in range(per_clip):
            found = jnp.where(arrival == table_ref[0, clip, p], clip * per_clip + p, found)
    mask = jnp.zeros_like(token)
    for index, value in enumerate(masks):
        mask = jnp.where(segment == index, value, mask)
    token_rows = piece_rows * len(masks)
    source = jnp.bitwise_xor(mask, place_ref[0])
    return found * token_rows + source * piece_rows + lax.rem(row, piece_rows)


def attention_kernel(
    head_size,
    per_peer,
    piece_rows,
    masks,
    near_rows,
    length_ref,
    owner_ref,
    place_ref,
    table_ref,
    *refs,
):
    seq_count = len(masks)
    part_refs, out_refs = refs[:3], refs[3 : 3 + seq_count]
    total_refs = refs[3 + seq_count :]
    far_rows = out_refs[0].shape[1] - near_rows
    stacked = [
        part_refs[0][...],
        jnp.concatenate([ref[...] for ref in part_refs[1:]], axis=1),
    ]
    width = stacked[0].shape[0] // 3
    clips = table_ref.shape[1]
    clip_tokens = seq_count * out_refs[0].shape[1] // clips
    codes = [
        token_codes(
            order, first, rows, per_peer, piece_rows, owner_ref, place_ref, table_ref
        )
        for order, first, rows in (
            (list(range(seq_count)), 0, near_rows),
            (masks, near_rows, far_rows),
        )
    ]
    position = lax.broadcasted_iota(jnp.int32, (clip_tokens, 1), 0)
    key = lax.broadcasted_iota(jnp.int32, (8, clip_tokens), 1)
    heads = range(0, width, head_size)
    scale = math.log2(math.e) / math.sqrt(head_size)
    for clip in range(clips):
        chosen = [
            jnp.where(code == position + clip * clip_tokens, 1.0, 0.0).astype(BF16)
            for code in codes
        ]
        picked = None
        for part, one_hot in zip(stacked, chosen):
            term = lax.dot_general(
                part, one_hot, (((1,), (1,)), ((), ())), preferred_element_type=F32
            )
            picked = term if picked is None else picked + term
        in_clip = jnp.where(key < length_ref[0, clip], 1.0, 0.0)
        scores = [
            jnp.dot(
                jnp.transpose(picked[width + head : width + head + head_size]).astype(BF16),
                picked[head : head + head_size].astype(BF16),
                preferred_element_type=F32,
            )
            for head in heads
        ]
        unscaled = [jnp.exp2(score * scale).astype(BF16) for score in scores]
        outs = []
        for head, weights in zip(heads, unscaled):
            values = picked[2 * width + head : 2 * width + head + head_size] * in_clip[:1]
            values = jnp.concatenate([values, in_clip], axis=0).astype(BF16)
            summed = jnp.dot(values, weights, preferred_element_type=F32)
            outs.append(summed[:head_size] * (1.0 / summed[head_size : head_size + 1]))
        attended = jnp.concatenate(outs, axis=0).astype(BF16)
        for total_ref, one_hot in zip(total_refs, chosen):
            back = jnp.dot(attended, one_hot, preferred_element_type=F32)
            if clip == 0:
                total_ref[...] = back
            else:
                total_ref[...] += back
    for mask, ref in enumerate(out_refs):
        start = mask * near_rows
        ref[:, :near_rows] = total_refs[0][:, start : start + near_rows].astype(BF16)
        start = masks.index(mask) * far_rows
        ref[:, near_rows:] = total_refs[1][:, start : start + far_rows].astype(BF16)


def output_kernel(
    seq_count,
    halves,
    clip_tokens,
    codes_of,
    core_ref,
    length_ref,
    owner_ref,
    place_ref,
    table_ref,
    modulation_ref,
    weight_ref,
    *refs,
):
    head_refs, refs = refs[:seq_count], refs[seq_count:]
    fetched = (seq_count - 1) * halves
    fetched_refs, refs = refs[:fetched], refs[fetched:]
    count = len(refs) // 3
    block_refs, out_refs = refs[:count], refs[count:]
    rows = out_refs[0].shape[0]
    branch = None
    for mask in range(seq_count):
        if mask == 0:
            weight = weight_ref[...]
        else:
            parts = [
                ref[ref.shape[0] - weight_ref.shape[0] // halves :]
                for ref in fetched_refs[mask - 1 :: seq_count - 1]
            ]
            if halves == 2:
                first = core_ref[0] == 0
                parts = [
                    jnp.where(first, parts[0], parts[1]),
                    jnp.where(first, parts[1], parts[0]),
                ]
            weight = jnp.concatenate(parts, axis=0)
        term = lax.dot_general(
            head_refs[mask][...],
            weight,
            (((0,), (0,)), ((), ())),
            preferred_element_type=F32,
        )
        branch = term if branch is None else branch + term
    code = codes_of(branch.shape[0], owner_ref[0], place_ref[0], table_ref[0])
    clip = lax.div(code, clip_tokens)
    limit = jnp.zeros_like(code)
    for index in range(length_ref.shape[1]):
        limit = jnp.where(clip == index, length_ref[0, index], limit)
    kept = lax.rem(code, clip_tokens) < limit
    branch = pick(clip, modulation_ref[2].astype(F32)) * branch
    for index, out_ref in enumerate(out_refs):
        at = slice(index * rows, (index + 1) * rows)
        side = slice(index % 2 * rows, (index % 2 + 1) * rows)
        result = block_refs[index // 2][side].astype(F32) + branch[at]
        out_ref[...] = jnp.where(kept[at], result, 0.0).astype(BF16)


def body(
    tokens, slot_owner, clip_pieces, clip_length, modulation, qkv_weight, qk_gain, proj_weight
):
    dp_count = lax.axis_size("dp")
    seq_count = lax.axis_size("seq")
    pieces_here = tokens.shape[1]
    piece_rows = tokens.shape[2]
    model_width = tokens.shape[3]
    per_peer = pieces_here // dp_count
    head_size = qk_gain.shape[1]
    heads = HEADS // seq_count
    head_width = heads * head_size
    clips_here, per_clip = clip_pieces.shape[1:]
    clip_tokens = per_clip * piece_rows * seq_count
    block_rows = per_peer * piece_rows
    rows_here = pieces_here * piece_rows
    group_rows = rows_here // 2
    chips = dp_count // 2
    owner_place = lax.axis_index("dp").astype(jnp.int32)
    place = lax.axis_index("seq").astype(jnp.int32).reshape(1)
    core = lax.rem(owner_place, 2).reshape(1)
    owner_place = owner_place.reshape(1)
    halves = 2 if heads % 2 == 0 else 1

    smem = pl.BlockSpec(memory_space=pltpu.SMEM)
    vmem = pl.BlockSpec(memory_space=pltpu.VMEM)

    def call(
        kernel, scalars, inputs, outputs, scratch=(), out_scalars=0, limit=16, flops=10**9, where=vmem
    ):
        return pl.pallas_call(
            kernel,
            in_specs=[smem] * len(scalars) + [where] * len(inputs),
            out_specs=[smem] * out_scalars + [vmem] * (len(outputs) - out_scalars),
            out_shape=[jax.ShapeDtypeStruct(shape, dtype) for shape, dtype in outputs],
            scratch_shapes=list(scratch),
            compiler_params=pltpu.CompilerParams(vmem_limit_bytes=limit * 2**20),
            cost_estimate=pl.CostEstimate(
                flops=flops, bytes_accessed=2**20, transcendentals=0
            ),
        )(*scalars, *inputs)

    x_count = math.isqrt(seq_count)
    anywhere = pl.BlockSpec(memory_space=pltpu.HBM)
    along_x = list(range(1, x_count))
    along_y = list(range(x_count, seq_count, x_count))
    across = [(my, mx) for my in along_y for mx in along_x]

    slots, own, other = call(
        functools.partial(route_kernel, per_peer, piece_rows),
        [owner_place],
        [slot_owner, tokens],
        [((pieces_here,), jnp.int32)] + [((chips * block_rows, model_width), BF16)] * 2,
        scratch=[
            pltpu.SMEM((dp_count,), jnp.int32),
            pltpu.SMEM(slot_owner.shape, jnp.int32),
            pltpu.VMEM(tokens.shape, BF16),
            pltpu.SemaphoreType.DMA((2,)),
        ],
        out_scalars=1,
        limit=63,
        where=anywhere,
    )
    payloads = call(
        functools.partial(merge_kernel, block_rows),
        [],
        [own, send(other, "dp", 1)],
        [((2 * block_rows, model_width), BF16)] * chips,
    )
    arrived = [send(payload, "dp", 2 * mask) for mask, payload in enumerate(payloads)]

    def codes_of(first_piece):
        return lambda rows, *places: row_codes(
            rows, first_piece, per_peer, piece_rows, piece_rows * seq_count, *places
        )

    def cut(blocks, starts, rows):
        outputs = [((count, model_width), BF16) for count in rows]
        return call(functools.partial(cut_kernel, starts), [], blocks, outputs)

    weight = jnp.transpose(qkv_weight, (1, 2, 0)).reshape(3 * head_width, model_width)
    factors = jnp.transpose(modulation[0], (1, 0, 2))

    def project(blocks, rows):
        (projected,) = call(
            functools.partial(project_kernel, head_size, rows),
            [],
            [weight, qk_gain] + blocks,
            [((3 * head_width, rows * len(blocks)), BF16)],
            flops=3 * 10**9,
        )
        return projected

    near_rows = 2 * block_rows
    far_rows = rows_here - near_rows
    sent_rows = head_width // halves
    (near,) = call(
        functools.partial(near_kernel, clip_tokens, codes_of(0)),
        [core, owner_place, place],
        [clip_pieces, factors, proj_weight, arrived[0]],
        [((near_rows + sent_rows, model_width), BF16)],
    )
    near_sides = {mask: send(near, "seq", mask) for mask in along_y + along_x}
    (far,) = call(
        functools.partial(far_kernel, clip_tokens, codes_of(2 * per_peer)),
        [owner_place, place],
        [clip_pieces, factors] + arrived[1:],
        [((far_rows, model_width), BF16)],
        flops=11 * 10**9,
    )
    far, near_sides = lax.optimization_barrier((far, near_sides))
    far_sides = {mask: send(far, "seq", mask) for mask in along_y + along_x}

    pieces = cut(
        [near_sides[mx] for mx in along_x] + [near_sides[my] for my in along_y],
        [0] * len(along_x) + [near_rows] * len(along_y),
        [near_rows] * len(along_x) + [sent_rows] * len(along_y),
    )
    near_parts = dict(zip(along_x, pieces))
    proj_parts = dict(zip(along_y, pieces[len(along_x) :]))
    near_across = {my + mx: send(near_parts[mx], "seq", my) for my, mx in across}
    near_across, far_sides = lax.optimization_barrier((near_across, far_sides))
    first_half = -(-far_rows // 32) * 16
    pieces = cut(
        [far_sides[my] for my in along_y] + [far_sides[mx] for mx in along_x],
        [0] * len(along_y) + [first_half] * len(along_x),
        [first_half] * len(along_y) + [far_rows - first_half] * len(along_x),
    )
    halved = dict(zip(along_y + along_x, pieces))
    far_across = {
        my + mx: [send(halved[my], "seq", mx), send(halved[mx], "seq", my)] for my, mx in across
    }
    near_blocks = {0: near} | near_sides | near_across
    stacked_near = project([near_blocks[mask] for mask in range(seq_count)], near_rows)
    sides = [0] + along_x + along_y
    diagonals = [my + mx for my, mx in across]
    stacked_sides = project([({0: far} | far_sides)[mask] for mask in sides], far_rows)

    _, late = lax.optimization_barrier((pieces, (near_sides, proj_parts)))
    near_sides, proj_parts = late
    proj_across = {my + mx: send(proj_parts[my], "seq", mx) for my, mx in across}
    swapped = {}
    if halves == 2:
        swapped = {mask: send(near_sides[mask], "dp", 1) for mask in near_sides}
    (stacked_across,) = call(
        functools.partial(project_kernel, head_size, far_rows),
        [],
        [weight, qk_gain] + [part for mask in diagonals for part in far_across[mask]],
        [((3 * head_width, far_rows * len(diagonals)), BF16)],
        flops=3 * 10**9,
    )
    stacked_across, swapped = lax.optimization_barrier((stacked_across, swapped))
    stacked = [stacked_near, stacked_sides, stacked_across]

    attended = call(
        functools.partial(
            attention_kernel, head_size, per_peer, piece_rows, sides + diagonals, near_rows
        ),
        [clip_length, owner_place, place, clip_pieces],
        stacked,
        [((head_width, rows_here), BF16)] * seq_count,
        scratch=[
            pltpu.VMEM((head_width, seq_count * rows), F32) for rows in (near_rows, far_rows)
        ],
        limit=16 if clip_tokens <= 256 else 56,
        flops=8 * 10**9,
    )
    returned = [send(array, "seq", mask) for mask, array in enumerate(attended)]
    fetched = [(near_sides | proj_across)[mask] for mask in range(1, seq_count)]
    if halves == 2:
        _, proj_late = lax.optimization_barrier((attended[0], proj_across))
        swapped = swapped | {mask: send(proj_late[mask], "dp", 1) for mask in proj_late}
        fetched += [swapped[mask] for mask in range(1, seq_count)]

    results = call(
        functools.partial(output_kernel, seq_count, halves, clip_tokens, codes_of(0)),
        [core, clip_length, owner_place, place],
        [clip_pieces, factors, proj_weight] + returned + fetched + arrived,
        [((block_rows, model_width), BF16)] * dp_count,
        flops=3 * 10**9,
    )
    order = list(range(dp_count // 2, dp_count)) + list(range(dp_count // 2))
    came_back = [send(results[mask], "dp", mask) for mask in order]
    (out,) = call(
        functools.partial(place_kernel, per_peer, piece_rows, order),
        [slots],
        came_back,
        [(tokens.shape, BF16)],
    )
    return out


def solution(mesh):
    return jax.shard_map(
        body,
        mesh=mesh,
        in_specs=(
            P("dp", None, "seq", None),
            P("dp", None),
            P("dp", None, None),
            P("dp", None),
            P("dp", None, None, None),
            P(None, None, "seq"),
            P(),
            P("seq", None),
        ),
        out_specs=P("dp", None, "seq", None),
        check_vma=False,
    )
```

```python
import functools
import math

import jax
import jax.numpy as jnp
from jax import lax
from jax.experimental import pallas as pl
from jax.experimental.pallas import tpu as pltpu
from jax.sharding import PartitionSpec as P

HEADS = 16
EPSILON = 1e-06
BF16 = jnp.bfloat16
F32 = jnp.float32


def send(array, axis, mask):
    if mask == 0:
        return array
    count = lax.axis_size(axis)
    return lax.ppermute(array, axis, [(i, i ^ mask) for i in range(count)])


def route_kernel(per_peer, piece_rows, place_ref, owner_hbm, token_hbm, *refs):
    slot_ref, own_ref, other_ref, filled_ref, owner_ref, token_ref, sems = refs
    peers = filled_ref.shape[0]
    owner_copy = pltpu.make_async_copy(owner_hbm, owner_ref, sems.at[0])
    token_copy = pltpu.make_async_copy(token_hbm, token_ref, sems.at[1])
    owner_copy.start()
    token_copy.start()
    for peer in range(peers):
        filled_ref[peer] = peer * per_peer
    owner_copy.wait()

    @pl.loop(0, peers * per_peer, unroll=8)
    def _(slot):
        peer = jnp.bitwise_xor(owner_ref[0, slot], place_ref[0])
        at = filled_ref[peer]
        filled_ref[peer] = at + 1
        slot_ref[at] = slot

    token_copy.wait()
    for peer in range(peers):
        ref = own_ref if peer % 2 == 0 else other_ref
        for m in range(per_peer):
            at = (peer // 2 * per_peer + m) * piece_rows
            ref[at : at + piece_rows, :] = token_ref[0, slot_ref[peer * per_peer + m]]


def merge_kernel(rows, own_hbm, other_ref, *refs):
    refs, own_ref, sem = refs[:-2], refs[-2], refs[-1]
    copy = pltpu.make_async_copy(own_hbm, own_ref, sem)
    copy.start()
    for index, ref in enumerate(refs):
        ref[rows:] = other_ref[index * rows : (index + 1) * rows]
    copy.wait()
    for index, ref in enumerate(refs):
        ref[:rows] = own_ref[index * rows : (index + 1) * rows]


def sides_kernel(*refs):
    count = len(refs) // 2
    for index in range(count):
        rows = refs[count + index].shape[0]
        start = 0 if index < count // 2 else rows
        refs[count + index][...] = refs[index][start : start + rows]


def half_kernel(core_ref, weight_hbm, out_ref, sem):
    rows = out_ref.shape[0]
    start = pl.multiple_of(core_ref[0] * rows, 16)
    copy = pltpu.make_async_copy(weight_hbm.at[pl.ds(start, rows), :], out_ref, sem)
    copy.start()
    copy.wait()


def place_kernel(per_peer, piece_rows, order, slot_ref, *refs):
    block_refs, out_ref = refs[:-1], refs[-1]
    for peer, ref in zip(order, block_refs):
        for m in range(per_peer):
            slot = slot_ref[peer * per_peer + m]
            out_ref[0, slot] = ref[m * piece_rows : (m + 1) * piece_rows, :]


def arrival_of(piece, per_peer, owner_place):
    source = jnp.bitwise_xor(lax.div(piece, per_peer), owner_place)
    return source * per_peer + lax.rem(piece, per_peer)


def row_codes(rows, first_piece, per_peer, piece_rows, token_rows, owner_place, place, table):
    row = lax.broadcasted_iota(jnp.int32, (rows, 1), 0)
    arrival = arrival_of(first_piece + lax.div(row, piece_rows), per_peer, owner_place)
    lane = lax.broadcasted_iota(jnp.int32, (1, table.shape[1]), 1)
    found = jnp.zeros((rows, 1), jnp.int32)
    for clip in range(table.shape[0]):
        number = jnp.where(
            arrival == table[clip : clip + 1], lane + clip * table.shape[1], 0
        )
        found += jnp.sum(number, axis=1, keepdims=True)
    return found * token_rows + place * piece_rows + lax.rem(row, piece_rows)


def pick(clip, table):
    rows = jnp.broadcast_to(table[0:1], (clip.shape[0], table.shape[1]))
    for index in range(1, table.shape[0]):
        rows = jnp.where(clip == index, table[index : index + 1], rows)
    return rows


def norm_kernel(
    clip_tokens, codes_of, owner_ref, place_ref, table_ref, modulation_ref, *refs
):
    block_refs, out_ref = refs[:-1], refs[-1]
    code = codes_of(out_ref.shape[0], owner_ref[0], place_ref[0], table_ref[0])
    clip = lax.div(code, clip_tokens)
    rows = jnp.concatenate([ref[...].astype(F32) for ref in block_refs], axis=0)
    average = jnp.mean(rows, axis=-1, keepdims=True)
    centered = rows - average
    variance = jnp.mean(centered * centered, axis=-1, keepdims=True)
    normed = centered * lax.rsqrt(variance + EPSILON)
    shift = pick(clip, modulation_ref[0].astype(F32))
    scale = pick(clip, modulation_ref[1].astype(F32))
    out_ref[...] = (normed * (1.0 + scale) + shift).astype(BF16)


def project_kernel(head_size, weight_ref, gain_ref, *refs):
    hidden_refs, out_ref = refs[:-1], refs[-1]
    hidden = jnp.concatenate([ref[...] for ref in hidden_refs], axis=0)
    projected = lax.dot_general(
        weight_ref[...], hidden, (((1,), (1,)), ((), ())), preferred_element_type=F32
    )
    width = weight_ref.shape[0] // 3
    shape = (head_size, head_size)
    diagonal = lax.broadcasted_iota(jnp.int32, shape, 0) == lax.broadcasted_iota(
        jnp.int32, shape, 1
    )
    found = []
    for part in range(2):
        gain = jnp.sum(
            jnp.where(diagonal, gain_ref[part : part + 1, :], 0.0), axis=1, keepdims=True
        )
        for start in range(part * width, (part + 1) * width, head_size):
            value = projected[start : start + head_size]
            square = jnp.sum(value * value, axis=0, keepdims=True) * (1.0 / head_size)
            found.append(value * lax.rsqrt(square + EPSILON) * gain)
    found.append(projected[2 * width :])
    out_ref[...] = jnp.concatenate(found, axis=0).astype(BF16)


def attention_kernel(
    head_size, per_peer, piece_rows, length_ref, owner_ref, place_ref, table_ref, *refs
):
    part_refs, out_refs, all_ref = refs[:2], refs[2:-1], refs[-1]
    stacked = jnp.concatenate([ref[...] for ref in part_refs], axis=1)
    width, tokens = stacked.shape[0] // 3, stacked.shape[1]
    seq_count = len(out_refs)
    clips, per_clip = table_ref.shape[1:]
    clip_tokens = tokens // clips
    group_rows = tokens // 2 // seq_count
    token = lax.broadcasted_iota(jnp.int32, (1, tokens), 1)
    row = lax.rem(token, group_rows)
    block = lax.div(token, group_rows)
    piece = lax.div(block, seq_count) * (group_rows // piece_rows) + lax.div(row, piece_rows)
    arrival = arrival_of(piece, per_peer, owner_ref[0])
    found = jnp.zeros_like(token)
    for clip in range(clips):
        for p in range(per_clip):
            found = jnp.where(arrival == table_ref[0, clip, p], clip * per_clip + p, found)
    source = jnp.bitwise_xor(lax.rem(block, seq_count), place_ref[0])
    code = found * (piece_rows * seq_count) + source * piece_rows + lax.rem(row, piece_rows)
    position = lax.broadcasted_iota(jnp.int32, (clip_tokens, 1), 0)
    key = lax.broadcasted_iota(jnp.int32, (8, clip_tokens), 1)
    heads = range(0, width, head_size)
    scale = math.log2(math.e) / math.sqrt(head_size)
    for clip in range(clips):
        chosen = jnp.where(code == position + clip * clip_tokens, 1.0, 0.0).astype(BF16)
        picked = lax.dot_general(
            stacked, chosen, (((1,), (1,)), ((), ())), preferred_element_type=F32
        )
        in_clip = jnp.where(key < length_ref[0, clip], 1.0, 0.0)
        scores = [
            jnp.dot(
                jnp.transpose(picked[width + head : width + head + head_size]).astype(BF16),
                picked[head : head + head_size].astype(BF16),
                preferred_element_type=F32,
            )
            for head in heads
        ]
        unscaled = [jnp.exp2(score * scale).astype(BF16) for score in scores]
        outs = []
        for head, weights in zip(heads, unscaled):
            values = picked[2 * width + head : 2 * width + head + head_size] * in_clip[:1]
            values = jnp.concatenate([values, in_clip], axis=0).astype(BF16)
            summed = jnp.dot(values, weights, preferred_element_type=F32)
            outs.append(summed[:head_size] * (1.0 / summed[head_size : head_size + 1]))
        attended = jnp.concatenate(outs, axis=0).astype(BF16)
        back = jnp.dot(attended, chosen, preferred_element_type=F32)
        if clip == 0:
            all_ref[...] = back
        else:
            all_ref[...] += back
    for index, ref in enumerate(out_refs):
        for group in range(2):
            start = (group * seq_count + index) * group_rows
            ref[:, group * group_rows : (group + 1) * group_rows] = all_ref[
                :, start : start + group_rows
            ].astype(BF16)


def output_kernel(
    seq_count,
    halves,
    clip_tokens,
    codes_of,
    core_ref,
    length_ref,
    owner_ref,
    place_ref,
    table_ref,
    modulation_ref,
    weight_ref,
    *refs,
):
    head_refs, refs = refs[:seq_count], refs[seq_count:]
    fetched = (seq_count - 1) * halves
    fetched_refs, refs = refs[:fetched], refs[fetched:]
    count = len(refs) // 3
    block_refs, out_refs = refs[:count], refs[count:]
    rows = out_refs[0].shape[0]
    branch = None
    for mask in range(seq_count):
        if mask == 0:
            weight = weight_ref[...]
        else:
            parts = [ref[...] for ref in fetched_refs[mask - 1 :: seq_count - 1]]
            if halves == 2:
                first = core_ref[0] == 0
                parts = [
                    jnp.where(first, parts[0], parts[1]),
                    jnp.where(first, parts[1], parts[0]),
                ]
            weight = jnp.concatenate(parts, axis=0)
        term = lax.dot_general(
            head_refs[mask][...],
            weight,
            (((0,), (0,)), ((), ())),
            preferred_element_type=F32,
        )
        branch = term if branch is None else branch + term
    code = codes_of(branch.shape[0], owner_ref[0], place_ref[0], table_ref[0])
    clip = lax.div(code, clip_tokens)
    limit = jnp.zeros_like(code)
    for index in range(length_ref.shape[1]):
        limit = jnp.where(clip == index, length_ref[0, index], limit)
    kept = lax.rem(code, clip_tokens) < limit
    branch = pick(clip, modulation_ref[2].astype(F32)) * branch
    for index, out_ref in enumerate(out_refs):
        at = slice(index * rows, (index + 1) * rows)
        side = slice(index % 2 * rows, (index % 2 + 1) * rows)
        result = block_refs[index // 2][side].astype(F32) + branch[at]
        out_ref[...] = jnp.where(kept[at], result, 0.0).astype(BF16)


def body(
    tokens, slot_owner, clip_pieces, clip_length, modulation, qkv_weight, qk_gain, proj_weight
):
    dp_count = lax.axis_size("dp")
    seq_count = lax.axis_size("seq")
    pieces_here = tokens.shape[1]
    piece_rows = tokens.shape[2]
    model_width = tokens.shape[3]
    per_peer = pieces_here // dp_count
    head_size = qk_gain.shape[1]
    heads = HEADS // seq_count
    head_width = heads * head_size
    clips_here, per_clip = clip_pieces.shape[1:]
    clip_tokens = per_clip * piece_rows * seq_count
    block_rows = per_peer * piece_rows
    rows_here = pieces_here * piece_rows
    group_rows = rows_here // 2
    chips = dp_count // 2
    owner_place = lax.axis_index("dp").astype(jnp.int32)
    place = lax.axis_index("seq").astype(jnp.int32).reshape(1)
    core = lax.rem(owner_place, 2).reshape(1)
    owner_place = owner_place.reshape(1)
    halves = 2 if heads % 2 == 0 else 1

    smem = pl.BlockSpec(memory_space=pltpu.SMEM)
    vmem = pl.BlockSpec(memory_space=pltpu.VMEM)

    def call(
        kernel, scalars, inputs, outputs, scratch=(), out_scalars=0, limit=16, flops=10**9, where=vmem
    ):
        return pl.pallas_call(
            kernel,
            in_specs=[smem] * len(scalars)
            + (where if isinstance(where, list) else [where] * len(inputs)),
            out_specs=[smem] * out_scalars + [vmem] * (len(outputs) - out_scalars),
            out_shape=[jax.ShapeDtypeStruct(shape, dtype) for shape, dtype in outputs],
            scratch_shapes=list(scratch),
            compiler_params=pltpu.CompilerParams(vmem_limit_bytes=int(limit * 2**20)),
            cost_estimate=pl.CostEstimate(
                flops=flops, bytes_accessed=2**20, transcendentals=0
            ),
        )(*scalars, *inputs)

    x_count = math.isqrt(seq_count)
    anywhere = pl.BlockSpec(memory_space=pltpu.HBM)
    along_x = list(range(1, x_count))
    along_y = list(range(x_count, seq_count, x_count))

    slots, own, other = call(
        functools.partial(route_kernel, per_peer, piece_rows),
        [owner_place],
        [slot_owner, tokens],
        [((pieces_here,), jnp.int32)] + [((chips * block_rows, model_width), BF16)] * 2,
        scratch=[
            pltpu.SMEM((dp_count,), jnp.int32),
            pltpu.SMEM(slot_owner.shape, jnp.int32),
            pltpu.VMEM(tokens.shape, BF16),
            pltpu.SemaphoreType.DMA((2,)),
        ],
        out_scalars=1,
        limit=59,
        where=anywhere,
    )
    payloads = call(
        functools.partial(merge_kernel, block_rows),
        [],
        [own, send(other, "dp", 1)],
        [((2 * block_rows, model_width), BF16)] * chips,
        scratch=[pltpu.VMEM(own.shape, BF16), pltpu.SemaphoreType.DMA],
        where=[anywhere, vmem],
    )
    arrived = [send(payload, "dp", 2 * mask) for mask, payload in enumerate(payloads)]

    _, proj_own = lax.optimization_barrier((payloads, proj_weight))
    if halves == 2:
        (proj_own,) = call(
            half_kernel,
            [core],
            [proj_own],
            [((head_width // 2, model_width), BF16)],
            scratch=[pltpu.SemaphoreType.DMA],
            where=anywhere,
        )
    proj_parts = {mask: send(proj_own, "seq", mask) for mask in along_y + along_x}

    def codes_of(group):
        return lambda rows, *places: row_codes(
            rows,
            group * (pieces_here // 2),
            per_peer,
            piece_rows,
            piece_rows * seq_count,
            *places,
        )

    weight = jnp.transpose(qkv_weight, (1, 2, 0)).reshape(3 * head_width, model_width)
    factors = jnp.transpose(modulation[0], (1, 0, 2))
    def project(blocks):
        (projected,) = call(
            functools.partial(project_kernel, head_size),
            [],
            [weight, qk_gain] + blocks,
            [((3 * head_width, seq_count * group_rows), BF16)],
            flops=3 * 10**9,
        )
        return projected

    near, far = [
        call(
            functools.partial(norm_kernel, clip_tokens, codes_of(group)),
            [owner_place, place],
            [clip_pieces, factors] + arrived[group * chips // 2 : (group + 1) * chips // 2],
            [((group_rows, model_width), BF16)],
            flops=10**10,
        )[0]
        for group in range(2)
    ]
    near, proj_parts = lax.optimization_barrier((near, proj_parts))
    sides = {mask: send(near, "seq", mask) for mask in along_y + along_x}
    far, sides = lax.optimization_barrier((far, sides))
    far_blocks = [send(far, "seq", mask) for mask in range(seq_count)]
    halved = call(
        sides_kernel,
        [],
        [sides[mask] for mask in along_y + along_x],
        [((group_rows // 2, model_width), BF16)] * len(sides),
    )
    halved = dict(zip(along_y + along_x, halved))
    near_blocks = []
    for mask in range(seq_count):
        mx = mask % x_count
        my = mask - mx
        if mx > 0 and my > 0:
            near_blocks += [send(halved[my], "seq", mx), send(halved[mx], "seq", my)]
        else:
            near_blocks.append(sides[mask] if mask > 0 else near)
    stacked_near = project(near_blocks)
    far_blocks, stacked_near = lax.optimization_barrier((far_blocks, stacked_near))
    stacked_far = project(far_blocks)
    swapped = {mask: send(proj_parts[mask], "dp", 1) for mask in proj_parts} if halves == 2 else {}
    stacked_far, proj_parts, swapped = lax.optimization_barrier(
        (stacked_far, proj_parts, swapped)
    )
    for my in along_y:
        for mx in along_x:
            proj_parts[my + mx] = send(proj_parts[my], "seq", mx)
    stacked = [stacked_near, stacked_far]

    attended = call(
        functools.partial(attention_kernel, head_size, per_peer, piece_rows),
        [clip_length, owner_place, place, clip_pieces],
        stacked,
        [((head_width, rows_here), BF16)] * seq_count,
        scratch=[pltpu.VMEM((head_width, seq_count * rows_here), F32)],
        limit=16 if clip_tokens <= 256 else 48,
        flops=8 * 10**9,
    )
    returned = [send(array, "seq", mask) for mask, array in enumerate(attended)]
    if halves == 2:
        _, late = lax.optimization_barrier((attended[0], proj_parts))
        swapped |= {mask: send(late[mask], "dp", 1) for mask in late if mask not in swapped}
        proj_parts = proj_parts | {seq_count + mask: swapped[mask] for mask in swapped}
    proj_parts = [proj_parts[mask] for mask in sorted(proj_parts)]

    results = call(
        functools.partial(output_kernel, seq_count, halves, clip_tokens, codes_of(0)),
        [core, clip_length, owner_place, place],
        [clip_pieces, factors, proj_weight] + returned + proj_parts + arrived,
        [((block_rows, model_width), BF16)] * dp_count,
        flops=3 * 10**9,
    )
    order = list(range(dp_count // 2, dp_count)) + list(range(dp_count // 2))
    came_back = [send(results[mask], "dp", mask) for mask in order]
    (out,) = call(
        functools.partial(place_kernel, per_peer, piece_rows, order),
        [slots],
        came_back,
        [(tokens.shape, BF16)],
    )
    return out


def solution(mesh):
    return jax.shard_map(
        body,
        mesh=mesh,
        in_specs=(
            P("dp", None, "seq", None),
            P("dp", None),
            P("dp", None, None),
            P("dp", None),
            P("dp", None, None, None),
            P(None, None, "seq"),
            P(),
            P("seq", None),
        ),
        out_specs=P("dp", None, "seq", None),
        check_vma=False,
    )
```

```python
import functools
import math

import jax
import jax.numpy as jnp
from jax import lax
from jax.experimental import pallas as pl
from jax.experimental.pallas import tpu as pltpu
from jax.sharding import PartitionSpec as P

HEADS = 16
EPSILON = 1e-06
BF16 = jnp.bfloat16
F32 = jnp.float32


def send(array, axis, mask):
    if mask == 0:
        return array
    count = lax.axis_size(axis)
    return lax.ppermute(array, axis, [(i, i ^ mask) for i in range(count)])


def route_kernel(per_peer, piece_rows, place_ref, owner_hbm, token_hbm, *refs):
    slot_ref, own_ref, other_ref, filled_ref, owner_ref, token_ref, sems = refs
    peers = filled_ref.shape[0]
    owner_copy = pltpu.make_async_copy(owner_hbm, owner_ref, sems.at[0])
    token_copy = pltpu.make_async_copy(token_hbm, token_ref, sems.at[1])
    owner_copy.start()
    token_copy.start()
    for peer in range(peers):
        filled_ref[peer] = peer * per_peer
    owner_copy.wait()

    @pl.loop(0, peers * per_peer, unroll=8)
    def _(slot):
        peer = jnp.bitwise_xor(owner_ref[0, slot], place_ref[0])
        at = filled_ref[peer]
        filled_ref[peer] = at + 1
        slot_ref[at] = slot

    token_copy.wait()
    for peer in range(peers):
        ref = own_ref if peer % 2 == 0 else other_ref
        for m in range(per_peer):
            at = (peer // 2 * per_peer + m) * piece_rows
            ref[at : at + piece_rows, :] = token_ref[0, slot_ref[peer * per_peer + m]]


def merge_kernel(rows, own_hbm, other_ref, *refs):
    refs, own_ref, sem = refs[:-2], refs[-2], refs[-1]
    copy = pltpu.make_async_copy(own_hbm, own_ref, sem)
    copy.start()
    for index, ref in enumerate(refs):
        ref[rows:] = other_ref[index * rows : (index + 1) * rows]
    copy.wait()
    for index, ref in enumerate(refs):
        ref[:rows] = own_ref[index * rows : (index + 1) * rows]


def sides_kernel(*refs):
    count = len(refs) // 2
    for index in range(count):
        rows = refs[count + index].shape[0]
        start = 0 if index < count // 2 else rows
        refs[count + index][...] = refs[index][start : start + rows]


def half_kernel(core_ref, weight_hbm, out_ref, sem):
    rows = out_ref.shape[0]
    start = pl.multiple_of(core_ref[0] * rows, 16)
    copy = pltpu.make_async_copy(weight_hbm.at[pl.ds(start, rows), :], out_ref, sem)
    copy.start()
    copy.wait()


def place_kernel(per_peer, piece_rows, places, slot_ref, *refs):
    block_refs, out_ref = refs[:-1], refs[-1]
    for peer, (block, first) in enumerate(places):
        for m in range(per_peer):
            slot = slot_ref[peer * per_peer + m]
            start = first + m * piece_rows
            out_ref[0, slot] = block_refs[block][start : start + piece_rows, :]


def stack_kernel(*refs):
    rows = refs[0].shape[0]
    for index, ref in enumerate(refs[:-1]):
        refs[-1][index * rows : (index + 1) * rows] = ref[...]


def join_kernel(rows, *refs):
    own_refs, other_ref, refs = refs[: len(refs) // 2], refs[len(refs) // 2], refs[len(refs) // 2 + 1 :]
    for index, ref in enumerate(refs):
        ref[:rows] = own_refs[index][...]
        ref[rows:] = other_ref[(index + 1) * rows : (index + 2) * rows]


def arrival_of(piece, per_peer, owner_place):
    source = jnp.bitwise_xor(lax.div(piece, per_peer), owner_place)
    return source * per_peer + lax.rem(piece, per_peer)


def row_codes(rows, first_piece, per_peer, piece_rows, token_rows, owner_place, place, table):
    row = lax.broadcasted_iota(jnp.int32, (rows, 1), 0)
    arrival = arrival_of(first_piece + lax.div(row, piece_rows), per_peer, owner_place)
    lane = lax.broadcasted_iota(jnp.int32, (1, table.shape[1]), 1)
    found = jnp.zeros((rows, 1), jnp.int32)
    for clip in range(table.shape[0]):
        number = jnp.where(
            arrival == table[clip : clip + 1], lane + clip * table.shape[1], 0
        )
        found += jnp.sum(number, axis=1, keepdims=True)
    return found * token_rows + place * piece_rows + lax.rem(row, piece_rows)


def pick(clip, table):
    rows = jnp.broadcast_to(table[0:1], (clip.shape[0], table.shape[1]))
    for index in range(1, table.shape[0]):
        rows = jnp.where(clip == index, table[index : index + 1], rows)
    return rows


def norm_kernel(
    clip_tokens, codes_of, owner_ref, place_ref, table_ref, modulation_ref, *refs
):
    block_refs, out_ref = refs[:-1], refs[-1]
    code = codes_of(out_ref.shape[0], owner_ref[0], place_ref[0], table_ref[0])
    clip = lax.div(code, clip_tokens)
    rows = jnp.concatenate([ref[...].astype(F32) for ref in block_refs], axis=0)
    average = jnp.mean(rows, axis=-1, keepdims=True)
    centered = rows - average
    variance = jnp.mean(centered * centered, axis=-1, keepdims=True)
    normed = centered * lax.rsqrt(variance + EPSILON)
    shift = pick(clip, modulation_ref[0].astype(F32))
    scale = pick(clip, modulation_ref[1].astype(F32))
    out_ref[...] = (normed * (1.0 + scale) + shift).astype(BF16)


def project_kernel(head_size, weight_ref, gain_ref, *refs):
    hidden_refs, out_ref = refs[:-1], refs[-1]
    hidden = jnp.concatenate([ref[...] for ref in hidden_refs], axis=0)
    projected = lax.dot_general(
        weight_ref[...], hidden, (((1,), (1,)), ((), ())), preferred_element_type=F32
    )
    width = weight_ref.shape[0] // 3
    shape = (head_size, head_size)
    diagonal = lax.broadcasted_iota(jnp.int32, shape, 0) == lax.broadcasted_iota(
        jnp.int32, shape, 1
    )
    found = []
    for part in range(2):
        gain = jnp.sum(
            jnp.where(diagonal, gain_ref[part : part + 1, :], 0.0), axis=1, keepdims=True
        )
        for start in range(part * width, (part + 1) * width, head_size):
            value = projected[start : start + head_size]
            square = jnp.sum(value * value, axis=0, keepdims=True) * (1.0 / head_size)
            found.append(value * lax.rsqrt(square + EPSILON) * gain)
    found.append(projected[2 * width :])
    out_ref[...] = jnp.concatenate(found, axis=0).astype(BF16)


def token_codes(tokens, group_rows, per_peer, piece_rows, owner_ref, place_ref, table_ref):
    clips, per_clip = table_ref.shape[1:]
    seq_count = tokens // 2 // group_rows
    token = lax.broadcasted_iota(jnp.int32, (1, tokens), 1)
    row = lax.rem(token, group_rows)
    block = lax.div(token, group_rows)
    piece = lax.div(block, seq_count) * (group_rows // piece_rows) + lax.div(row, piece_rows)
    arrival = arrival_of(piece, per_peer, owner_ref[0])
    found = jnp.zeros_like(token)
    for clip in range(clips):
        for p in range(per_clip):
            found = jnp.where(arrival == table_ref[0, clip, p], clip * per_clip + p, found)
    source = jnp.bitwise_xor(lax.rem(block, seq_count), place_ref[0])
    return found * (piece_rows * seq_count) + source * piece_rows + lax.rem(row, piece_rows)


def gather_kernel(
    group_rows, per_peer, piece_rows, owner_ref, place_ref, table_ref, stacked_ref, out_ref
):
    count = stacked_ref.shape[1]
    code = token_codes(
        2 * count, group_rows, per_peer, piece_rows, owner_ref, place_ref, table_ref
    )[:, :count]
    clip_tokens = out_ref.shape[2]
    position = lax.broadcasted_iota(jnp.int32, (clip_tokens, 1), 0)
    for clip in range(out_ref.shape[0]):
        chosen = jnp.where(code == position + clip * clip_tokens, 1.0, 0.0).astype(BF16)
        out_ref[clip] = lax.dot_general(
            stacked_ref[...], chosen, (((1,), (1,)), ((), ())), preferred_element_type=F32
        ).astype(BF16)


def attention_kernel(
    head_size, per_peer, piece_rows, length_ref, owner_ref, place_ref, table_ref, *refs
):
    near_ref, far_ref, out_refs, all_ref = refs[0], refs[1], refs[2:-1], refs[-1]
    clips, features, clip_tokens = near_ref.shape
    width, tokens = features // 3, clips * clip_tokens
    seq_count = len(out_refs)
    group_rows = tokens // 2 // seq_count
    code = token_codes(
        tokens, group_rows, per_peer, piece_rows, owner_ref, place_ref, table_ref
    )
    position = lax.broadcasted_iota(jnp.int32, (clip_tokens, 1), 0)
    key = lax.broadcasted_iota(jnp.int32, (8, clip_tokens), 1)
    heads = range(0, width, head_size)
    scale = math.log2(math.e) / math.sqrt(head_size)
    for clip in range(clips):
        chosen = jnp.where(code == position + clip * clip_tokens, 1.0, 0.0).astype(BF16)
        picked = near_ref[clip].astype(F32) + lax.dot_general(
            far_ref[...],
            chosen[:, tokens // 2 :],
            (((1,), (1,)), ((), ())),
            preferred_element_type=F32,
        )
        in_clip = jnp.where(key < length_ref[0, clip], 1.0, 0.0)
        scores = [
            jnp.dot(
                jnp.transpose(picked[width + head : width + head + head_size]).astype(BF16),
                picked[head : head + head_size].astype(BF16),
                preferred_element_type=F32,
            )
            for head in heads
        ]
        unscaled = [jnp.exp2(score * scale).astype(BF16) for score in scores]
        outs = []
        for head, weights in zip(heads, unscaled):
            values = picked[2 * width + head : 2 * width + head + head_size] * in_clip[:1]
            values = jnp.concatenate([values, in_clip], axis=0).astype(BF16)
            summed = jnp.dot(values, weights, preferred_element_type=F32)
            outs.append(summed[:head_size] * (1.0 / summed[head_size : head_size + 1]))
        attended = jnp.concatenate(outs, axis=0).astype(BF16)
        back = jnp.dot(attended, chosen, preferred_element_type=F32)
        if clip == 0:
            all_ref[...] = back
        else:
            all_ref[...] += back
    for index, ref in enumerate(out_refs):
        for group in range(2):
            start = (group * seq_count + index) * group_rows
            ref[:, group * group_rows : (group + 1) * group_rows] = all_ref[
                :, start : start + group_rows
            ].astype(BF16)


def output_kernel(
    seq_count,
    halves,
    clip_tokens,
    codes_of,
    owner_masks,
    core_ref,
    length_ref,
    owner_ref,
    place_ref,
    table_ref,
    modulation_ref,
    weight_ref,
    *refs,
):
    head_refs, refs = refs[:seq_count], refs[seq_count:]
    fetched = (seq_count - 1) * halves
    fetched_refs, refs = refs[:fetched], refs[fetched:]
    count = len(owner_masks) // 2
    block_refs, out_refs = refs[:count], refs[count:]
    rows = block_refs[0].shape[0] // 2
    branch = None
    for mask in range(seq_count):
        if mask == 0:
            weight = weight_ref[...]
        else:
            parts = [ref[...] for ref in fetched_refs[mask - 1 :: seq_count - 1]]
            if halves == 2:
                first = core_ref[0] == 0
                parts = [
                    jnp.where(first, parts[0], parts[1]),
                    jnp.where(first, parts[1], parts[0]),
                ]
            weight = jnp.concatenate(parts, axis=0)
        term = lax.dot_general(
            head_refs[mask][...],
            weight,
            (((0,), (0,)), ((), ())),
            preferred_element_type=F32,
        )
        branch = term if branch is None else branch + term
    code = codes_of(branch.shape[0], owner_ref[0], place_ref[0], table_ref[0])
    clip = lax.div(code, clip_tokens)
    limit = jnp.zeros_like(code)
    for index in range(length_ref.shape[1]):
        limit = jnp.where(clip == index, length_ref[0, index], limit)
    kept = lax.rem(code, clip_tokens) < limit
    branch = pick(clip, modulation_ref[2].astype(F32)) * branch
    for index, (out, first) in enumerate(owner_masks):
        at = slice(index * rows, (index + 1) * rows)
        side = slice(index % 2 * rows, (index % 2 + 1) * rows)
        result = block_refs[index // 2][side].astype(F32) + branch[at]
        out_refs[out][first : first + rows] = jnp.where(kept[at], result, 0.0).astype(BF16)


def body(
    tokens, slot_owner, clip_pieces, clip_length, modulation, qkv_weight, qk_gain, proj_weight
):
    dp_count = lax.axis_size("dp")
    seq_count = lax.axis_size("seq")
    pieces_here = tokens.shape[1]
    piece_rows = tokens.shape[2]
    model_width = tokens.shape[3]
    per_peer = pieces_here // dp_count
    head_size = qk_gain.shape[1]
    heads = HEADS // seq_count
    head_width = heads * head_size
    clips_here, per_clip = clip_pieces.shape[1:]
    clip_tokens = per_clip * piece_rows * seq_count
    block_rows = per_peer * piece_rows
    rows_here = pieces_here * piece_rows
    group_rows = rows_here // 2
    chips = dp_count // 2
    owner_place = lax.axis_index("dp").astype(jnp.int32)
    place = lax.axis_index("seq").astype(jnp.int32).reshape(1)
    core = lax.rem(owner_place, 2).reshape(1)
    owner_place = owner_place.reshape(1)
    halves = 2 if heads % 2 == 0 else 1

    smem = pl.BlockSpec(memory_space=pltpu.SMEM)
    vmem = pl.BlockSpec(memory_space=pltpu.VMEM)

    def call(
        kernel, scalars, inputs, outputs, scratch=(), out_scalars=0, limit=16, flops=10**9, where=vmem
    ):
        return pl.pallas_call(
            kernel,
            in_specs=[smem] * len(scalars)
            + (where if isinstance(where, list) else [where] * len(inputs)),
            out_specs=[smem] * out_scalars + [vmem] * (len(outputs) - out_scalars),
            out_shape=[jax.ShapeDtypeStruct(shape, dtype) for shape, dtype in outputs],
            scratch_shapes=list(scratch),
            compiler_params=pltpu.CompilerParams(vmem_limit_bytes=int(limit * 2**20)),
            cost_estimate=pl.CostEstimate(
                flops=flops, bytes_accessed=2**20, transcendentals=0
            ),
        )(*scalars, *inputs)

    x_count = math.isqrt(seq_count)
    anywhere = pl.BlockSpec(memory_space=pltpu.HBM)
    along_x = list(range(1, x_count))
    along_y = list(range(x_count, seq_count, x_count))

    proj_own = proj_weight
    if halves == 2:
        (proj_own,) = call(
            half_kernel,
            [core],
            [proj_weight],
            [((head_width // 2, model_width), BF16)],
            scratch=[pltpu.SemaphoreType.DMA],
            where=anywhere,
        )
    proj_parts = {mask: send(proj_own, "seq", mask) for mask in along_y + along_x}

    slots, own, other = call(
        functools.partial(route_kernel, per_peer, piece_rows),
        [owner_place],
        [slot_owner, tokens],
        [((pieces_here,), jnp.int32)] + [((chips * block_rows, model_width), BF16)] * 2,
        scratch=[
            pltpu.SMEM((dp_count,), jnp.int32),
            pltpu.SMEM(slot_owner.shape, jnp.int32),
            pltpu.VMEM(tokens.shape, BF16),
            pltpu.SemaphoreType.DMA((2,)),
        ],
        out_scalars=1,
        limit=59,
        flops=3 * 10**10,
        where=anywhere,
    )
    payloads = call(
        functools.partial(merge_kernel, block_rows),
        [],
        [own, send(other, "dp", 1)],
        [((2 * block_rows, model_width), BF16)] * chips,
        scratch=[pltpu.VMEM(own.shape, BF16), pltpu.SemaphoreType.DMA],
        where=[anywhere, vmem],
    )
    arrived = [send(payload, "dp", 2 * mask) for mask, payload in enumerate(payloads)]

    def codes_of(group):
        return lambda rows, *places: row_codes(
            rows,
            group * (pieces_here // 2),
            per_peer,
            piece_rows,
            piece_rows * seq_count,
            *places,
        )

    weight = jnp.transpose(qkv_weight, (1, 2, 0)).reshape(3 * head_width, model_width)
    factors = jnp.transpose(modulation[0], (1, 0, 2))
    def project(blocks):
        (projected,) = call(
            functools.partial(project_kernel, head_size),
            [],
            [weight, qk_gain] + blocks,
            [((3 * head_width, seq_count * group_rows), BF16)],
            flops=3 * 10**9,
        )
        return projected

    near, far = [
        call(
            functools.partial(norm_kernel, clip_tokens, codes_of(group)),
            [owner_place, place],
            [clip_pieces, factors] + arrived[group * chips // 2 : (group + 1) * chips // 2],
            [((group_rows, model_width), BF16)],
            flops=(1 + 9 * group) * 10**9,
        )[0]
        for group in range(2)
    ]
    near, proj_parts = lax.optimization_barrier((near, proj_parts))
    near, proj_parts = lax.optimization_barrier((near, proj_parts))
    sides = {mask: send(near, "seq", mask) for mask in along_y + along_x}
    far, sides = lax.optimization_barrier((far, sides))
    far_blocks = [send(far, "seq", mask) for mask in range(seq_count)]
    halved = call(
        sides_kernel,
        [],
        [sides[mask] for mask in along_y + along_x],
        [((group_rows // 2, model_width), BF16)] * len(sides),
    )
    halved = dict(zip(along_y + along_x, halved))
    near_blocks = []
    for mask in range(seq_count):
        mx = mask % x_count
        my = mask - mx
        if mx > 0 and my > 0:
            near_blocks += [send(halved[my], "seq", mx), send(halved[mx], "seq", my)]
        else:
            near_blocks.append(sides[mask] if mask > 0 else near)
    stacked_near = project(near_blocks)
    (gathered,) = call(
        functools.partial(gather_kernel, group_rows, per_peer, piece_rows),
        [owner_place, place, clip_pieces],
        [stacked_near],
        [((clips_here, 3 * head_width, clip_tokens), BF16)],
        limit=16 if clip_tokens <= 256 else 48,
        flops=3 * 10**9,
    )
    gathered, proj_parts = lax.optimization_barrier((gathered, proj_parts))
    far_blocks, gathered = lax.optimization_barrier((far_blocks, gathered))
    stacked_far = project(far_blocks)
    swapped = {mask: send(proj_parts[mask], "dp", 1) for mask in proj_parts} if halves == 2 else {}
    stacked_far, proj_parts, swapped = lax.optimization_barrier(
        (stacked_far, proj_parts, swapped)
    )
    for my in along_y:
        for mx in along_x:
            proj_parts[my + mx] = send(proj_parts[my], "seq", mx)

    attended = call(
        functools.partial(attention_kernel, head_size, per_peer, piece_rows),
        [clip_length, owner_place, place, clip_pieces],
        [gathered, stacked_far],
        [((head_width, rows_here), BF16)] * seq_count,
        scratch=[pltpu.VMEM((head_width, seq_count * rows_here), F32)],
        limit=16 if clip_tokens <= 256 else 48,
        flops=8 * 10**9,
    )
    returned = [send(array, "seq", mask) for mask, array in enumerate(attended)]
    if halves == 2:
        _, late = lax.optimization_barrier((attended[0], proj_parts))
        swapped |= {mask: send(late[mask], "dp", 1) for mask in late if mask not in swapped}
        proj_parts = proj_parts | {seq_count + mask: swapped[mask] for mask in swapped}
    proj_parts = [proj_parts[mask] for mask in sorted(proj_parts)]

    half_count = dp_count // 2
    far_masks = list(range(half_count, dp_count))
    outs = {mask: (index, 0) for index, mask in enumerate(far_masks)}
    for index in range(half_count // 2):
        outs[2 * index] = (half_count + index, 0)
        outs[2 * index + 1] = (half_count + half_count // 2, index * block_rows)
    results = call(
        functools.partial(
            output_kernel,
            seq_count,
            halves,
            clip_tokens,
            codes_of(0),
            [outs[mask] for mask in range(dp_count)],
        ),
        [core, clip_length, owner_place, place],
        [clip_pieces, factors, proj_weight] + returned + proj_parts + arrived,
        [((block_rows, model_width), BF16)] * (half_count + half_count // 2)
        + [((half_count // 2 * block_rows, model_width), BF16)],
        flops=3 * 10**9,
    )
    (far_back,) = call(
        stack_kernel,
        [],
        [send(results[index], "dp", mask) for index, mask in enumerate(far_masks)],
        [((half_count * block_rows, model_width), BF16)],
        flops=12 * 10**9,
    )
    swapped_back = send(results[-1], "dp", 1)
    near_own = list(results[half_count:-1])
    places = {mask: (0, index * block_rows) for index, mask in enumerate(far_masks)}
    places[0], places[1] = (1, 0), (2, 0)
    came_back = [far_back, near_own[0], swapped_back]
    joined = call(
        functools.partial(join_kernel, block_rows),
        [],
        near_own[1:] + [swapped_back],
        [((2 * block_rows, model_width), BF16)] * (half_count // 2 - 1),
    )
    for index, block in enumerate(joined):
        mask = 2 * (index + 1)
        places[mask], places[mask + 1] = (len(came_back), 0), (len(came_back), block_rows)
        came_back.append(send(block, "dp", mask))
    (out,) = call(
        functools.partial(
            place_kernel, per_peer, piece_rows, [places[mask] for mask in range(dp_count)]
        ),
        [slots],
        came_back,
        [(tokens.shape, BF16)],
    )
    return out


def solution(mesh):
    return jax.shard_map(
        body,
        mesh=mesh,
        in_specs=(
            P("dp", None, "seq", None),
            P("dp", None),
            P("dp", None, None),
            P("dp", None),
            P("dp", None, None, None),
            P(None, None, "seq"),
            P(),
            P("seq", None),
        ),
        out_specs=P("dp", None, "seq", None),
        check_vma=False,
    )
```

```python
import functools
import math

import jax
import jax.numpy as jnp
from jax import lax
from jax.experimental import pallas as pl
from jax.experimental.pallas import tpu as pltpu
from jax.sharding import PartitionSpec as P

HEADS = 16
EPSILON = 1e-06
BF16 = jnp.bfloat16
F32 = jnp.float32


def send(array, axis, mask):
    if mask == 0:
        return array
    count = lax.axis_size(axis)
    return lax.ppermute(array, axis, [(i, i ^ mask) for i in range(count)])


def route_kernel(per_peer, piece_rows, place_ref, owner_hbm, token_hbm, *refs):
    slot_ref, own_ref, other_ref, filled_ref, owner_ref, token_ref, sems = refs
    peers = filled_ref.shape[0]
    owner_copy = pltpu.make_async_copy(owner_hbm, owner_ref, sems.at[0])
    token_copy = pltpu.make_async_copy(token_hbm, token_ref, sems.at[1])
    owner_copy.start()
    token_copy.start()
    for peer in range(peers):
        filled_ref[peer] = peer * per_peer
    owner_copy.wait()

    @pl.loop(0, peers * per_peer, unroll=8)
    def _(slot):
        peer = jnp.bitwise_xor(owner_ref[0, slot], place_ref[0])
        at = filled_ref[peer]
        filled_ref[peer] = at + 1
        slot_ref[at] = slot

    token_copy.wait()
    for peer in range(peers):
        ref = own_ref if peer % 2 == 0 else other_ref
        for m in range(per_peer):
            at = (peer // 2 * per_peer + m) * piece_rows
            ref[at : at + piece_rows, :] = token_ref[0, slot_ref[peer * per_peer + m]]


def merge_kernel(rows, own_hbm, other_ref, *refs):
    refs, own_ref, sem = refs[:-2], refs[-2], refs[-1]
    copy = pltpu.make_async_copy(own_hbm, own_ref, sem)
    copy.start()
    for index, ref in enumerate(refs):
        ref[rows:] = other_ref[index * rows : (index + 1) * rows]
    copy.wait()
    for index, ref in enumerate(refs):
        ref[:rows] = own_ref[index * rows : (index + 1) * rows]


def sides_kernel(*refs):
    count = len(refs) // 2
    for index in range(count):
        rows = refs[count + index].shape[0]
        start = 0 if index < count // 2 else rows
        refs[count + index][...] = refs[index][start : start + rows]


def half_kernel(core_ref, weight_hbm, out_ref, sem):
    rows = out_ref.shape[0]
    start = pl.multiple_of(core_ref[0] * rows, 16)
    copy = pltpu.make_async_copy(weight_hbm.at[pl.ds(start, rows), :], out_ref, sem)
    copy.start()
    copy.wait()


def place_kernel(per_peer, piece_rows, places, slot_ref, *refs):
    block_refs, out_ref = refs[:-1], refs[-1]
    for peer, (block, first) in enumerate(places):
        for m in range(per_peer):
            slot = slot_ref[peer * per_peer + m]
            start = first + m * piece_rows
            out_ref[0, slot] = block_refs[block][start : start + piece_rows, :]


def stack_kernel(*refs):
    start = 0
    for ref in refs[:-1]:
        refs[-1][start : start + ref.shape[0]] = ref[...]
        start += ref.shape[0]


def join_kernel(rows, *refs):
    own_refs, other_ref, refs = refs[: len(refs) // 2], refs[len(refs) // 2], refs[len(refs) // 2 + 1 :]
    for index, ref in enumerate(refs):
        ref[:rows] = own_refs[index][...]
        ref[rows:] = other_ref[(index + 1) * rows : (index + 2) * rows]


def arrival_of(piece, per_peer, owner_place):
    source = jnp.bitwise_xor(lax.div(piece, per_peer), owner_place)
    return source * per_peer + lax.rem(piece, per_peer)


def row_codes(rows, first_piece, per_peer, piece_rows, token_rows, owner_place, place, table):
    row = lax.broadcasted_iota(jnp.int32, (rows, 1), 0)
    arrival = arrival_of(first_piece + lax.div(row, piece_rows), per_peer, owner_place)
    lane = lax.broadcasted_iota(jnp.int32, (1, table.shape[1]), 1)
    found = jnp.zeros((rows, 1), jnp.int32)
    for clip in range(table.shape[0]):
        number = jnp.where(
            arrival == table[clip : clip + 1], lane + clip * table.shape[1], 0
        )
        found += jnp.sum(number, axis=1, keepdims=True)
    return found * token_rows + place * piece_rows + lax.rem(row, piece_rows)


def pick(clip, table):
    rows = jnp.broadcast_to(table[0:1], (clip.shape[0], table.shape[1]))
    for index in range(1, table.shape[0]):
        rows = jnp.where(clip == index, table[index : index + 1], rows)
    return rows


def norm_kernel(
    clip_tokens, codes_of, owner_ref, place_ref, table_ref, modulation_ref, *refs
):
    block_refs, out_ref = refs[:-1], refs[-1]
    code = codes_of(out_ref.shape[0], owner_ref[0], place_ref[0], table_ref[0])
    clip = lax.div(code, clip_tokens)
    rows = jnp.concatenate([ref[...].astype(F32) for ref in block_refs], axis=0)
    average = jnp.mean(rows, axis=-1, keepdims=True)
    centered = rows - average
    variance = jnp.mean(centered * centered, axis=-1, keepdims=True)
    normed = centered * lax.rsqrt(variance + EPSILON)
    shift = pick(clip, modulation_ref[0].astype(F32))
    scale = pick(clip, modulation_ref[1].astype(F32))
    out_ref[...] = (normed * (1.0 + scale) + shift).astype(BF16)


def project_kernel(head_size, weight_ref, gain_ref, *refs):
    hidden_refs, out_ref = refs[:-1], refs[-1]
    hidden = jnp.concatenate([ref[...] for ref in hidden_refs], axis=0)
    projected = lax.dot_general(
        weight_ref[...], hidden, (((1,), (1,)), ((), ())), preferred_element_type=F32
    )
    width = weight_ref.shape[0] // 3
    shape = (head_size, head_size)
    diagonal = lax.broadcasted_iota(jnp.int32, shape, 0) == lax.broadcasted_iota(
        jnp.int32, shape, 1
    )
    found = []
    for part in range(2):
        gain = jnp.sum(
            jnp.where(diagonal, gain_ref[part : part + 1, :], 0.0), axis=1, keepdims=True
        )
        for start in range(part * width, (part + 1) * width, head_size):
            value = projected[start : start + head_size]
            square = jnp.sum(value * value, axis=0, keepdims=True) * (1.0 / head_size)
            found.append(value * lax.rsqrt(square + EPSILON) * gain)
    found.append(projected[2 * width :])
    out_ref[...] = jnp.concatenate(found, axis=0).astype(BF16)


def token_codes(tokens, group_rows, per_peer, piece_rows, owner_ref, place_ref, table_ref):
    clips, per_clip = table_ref.shape[1:]
    seq_count = tokens // 2 // group_rows
    token = lax.broadcasted_iota(jnp.int32, (1, tokens), 1)
    row = lax.rem(token, group_rows)
    block = lax.div(token, group_rows)
    piece = lax.div(block, seq_count) * (group_rows // piece_rows) + lax.div(row, piece_rows)
    arrival = arrival_of(piece, per_peer, owner_ref[0])
    found = jnp.zeros_like(token)
    for clip in range(clips):
        for p in range(per_clip):
            found = jnp.where(arrival == table_ref[0, clip, p], clip * per_clip + p, found)
    source = jnp.bitwise_xor(lax.rem(block, seq_count), place_ref[0])
    return found * (piece_rows * seq_count) + source * piece_rows + lax.rem(row, piece_rows)


def gather_kernel(
    group_rows, per_peer, piece_rows, owner_ref, place_ref, table_ref, stacked_ref, out_ref
):
    count = stacked_ref.shape[1]
    code = token_codes(
        2 * count, group_rows, per_peer, piece_rows, owner_ref, place_ref, table_ref
    )[:, :count]
    clip_tokens = out_ref.shape[2]
    position = lax.broadcasted_iota(jnp.int32, (clip_tokens, 1), 0)
    for clip in range(out_ref.shape[0]):
        chosen = jnp.where(code == position + clip * clip_tokens, 1.0, 0.0).astype(BF16)
        out_ref[clip] = lax.dot_general(
            stacked_ref[...], chosen, (((1,), (1,)), ((), ())), preferred_element_type=F32
        ).astype(BF16)


def attention_kernel(
    head_size, per_peer, piece_rows, length_ref, owner_ref, place_ref, table_ref, *refs
):
    near_ref, far_ref, out_refs, all_ref = refs[0], refs[1], refs[2:-1], refs[-1]
    clips, features, clip_tokens = near_ref.shape
    width, tokens = features // 3, clips * clip_tokens
    seq_count = len(out_refs)
    group_rows = tokens // 2 // seq_count
    code = token_codes(
        tokens, group_rows, per_peer, piece_rows, owner_ref, place_ref, table_ref
    )
    position = lax.broadcasted_iota(jnp.int32, (clip_tokens, 1), 0)
    key = lax.broadcasted_iota(jnp.int32, (8, clip_tokens), 1)
    heads = range(0, width, head_size)
    scale = math.log2(math.e) / math.sqrt(head_size)
    for clip in range(clips):
        chosen = jnp.where(code == position + clip * clip_tokens, 1.0, 0.0).astype(BF16)
        picked = near_ref[clip].astype(F32) + lax.dot_general(
            far_ref[...],
            chosen[:, tokens // 2 :],
            (((1,), (1,)), ((), ())),
            preferred_element_type=F32,
        )
        in_clip = jnp.where(key < length_ref[0, clip], 1.0, 0.0)
        scores = [
            jnp.dot(
                jnp.transpose(picked[width + head : width + head + head_size]).astype(BF16),
                picked[head : head + head_size].astype(BF16),
                preferred_element_type=F32,
            )
            for head in heads
        ]
        unscaled = [jnp.exp2(score * scale).astype(BF16) for score in scores]
        outs = []
        for head, weights in zip(heads, unscaled):
            values = picked[2 * width + head : 2 * width + head + head_size] * in_clip[:1]
            values = jnp.concatenate([values, in_clip], axis=0).astype(BF16)
            summed = jnp.dot(values, weights, preferred_element_type=F32)
            outs.append(summed[:head_size] * (1.0 / summed[head_size : head_size + 1]))
        attended = jnp.concatenate(outs, axis=0).astype(BF16)
        back = jnp.dot(attended, chosen, preferred_element_type=F32)
        if clip == 0:
            all_ref[...] = back
        else:
            all_ref[...] += back
    for index, ref in enumerate(out_refs):
        for group in range(2):
            start = (group * seq_count + index) * group_rows
            ref[:, group * group_rows : (group + 1) * group_rows] = all_ref[
                :, start : start + group_rows
            ].astype(BF16)


def projected_rows(masks, halves, core_ref, head_refs, weight_refs):
    branch = None
    for mask, head_ref in zip(masks, head_refs):
        parts = [weight_refs[0][...]]
        if mask > 0:
            parts = [ref[...] for ref in weight_refs[:halves]]
            weight_refs = weight_refs[halves:]
            if halves == 2:
                first = core_ref[0] == 0
                parts = [
                    jnp.where(first, parts[0], parts[1]),
                    jnp.where(first, parts[1], parts[0]),
                ]
        else:
            weight_refs = weight_refs[1:]
        term = lax.dot_general(
            head_ref[...],
            jnp.concatenate(parts, axis=0),
            (((0,), (0,)), ((), ())),
            preferred_element_type=F32,
        )
        branch = term if branch is None else branch + term
    return branch


def sides_output_kernel(masks, halves, core_ref, *refs):
    refs[-1][...] = projected_rows(
        masks, halves, core_ref, refs[: len(masks)], refs[len(masks) : -1]
    )


def output_kernel(
    masks,
    halves,
    clip_tokens,
    codes_of,
    owner_masks,
    core_ref,
    length_ref,
    owner_ref,
    place_ref,
    table_ref,
    modulation_ref,
    partial_ref,
    *refs,
):
    head_refs, refs = refs[: len(masks)], refs[len(masks) :]
    weight_refs, refs = refs[: len(masks) * halves], refs[len(masks) * halves :]
    count = len(owner_masks) // 2
    block_refs, out_refs = refs[:count], refs[count:]
    rows = block_refs[0].shape[0] // 2
    branch = partial_ref[...] + projected_rows(masks, halves, core_ref, head_refs, weight_refs)
    code = codes_of(branch.shape[0], owner_ref[0], place_ref[0], table_ref[0])
    clip = lax.div(code, clip_tokens)
    limit = jnp.zeros_like(code)
    for index in range(length_ref.shape[1]):
        limit = jnp.where(clip == index, length_ref[0, index], limit)
    kept = lax.rem(code, clip_tokens) < limit
    branch = pick(clip, modulation_ref[2].astype(F32)) * branch
    for index, (out, first) in enumerate(owner_masks):
        at = slice(index * rows, (index + 1) * rows)
        side = slice(index % 2 * rows, (index % 2 + 1) * rows)
        result = block_refs[index // 2][side].astype(F32) + branch[at]
        out_refs[out][first : first + rows] = jnp.where(kept[at], result, 0.0).astype(BF16)


def body(
    tokens, slot_owner, clip_pieces, clip_length, modulation, qkv_weight, qk_gain, proj_weight
):
    dp_count = lax.axis_size("dp")
    seq_count = lax.axis_size("seq")
    pieces_here = tokens.shape[1]
    piece_rows = tokens.shape[2]
    model_width = tokens.shape[3]
    per_peer = pieces_here // dp_count
    head_size = qk_gain.shape[1]
    heads = HEADS // seq_count
    head_width = heads * head_size
    clips_here, per_clip = clip_pieces.shape[1:]
    clip_tokens = per_clip * piece_rows * seq_count
    block_rows = per_peer * piece_rows
    rows_here = pieces_here * piece_rows
    group_rows = rows_here // 2
    chips = dp_count // 2
    owner_place = lax.axis_index("dp").astype(jnp.int32)
    place = lax.axis_index("seq").astype(jnp.int32).reshape(1)
    core = lax.rem(owner_place, 2).reshape(1)
    owner_place = owner_place.reshape(1)
    halves = 2 if heads % 2 == 0 else 1

    smem = pl.BlockSpec(memory_space=pltpu.SMEM)
    vmem = pl.BlockSpec(memory_space=pltpu.VMEM)

    def call(
        kernel, scalars, inputs, outputs, scratch=(), out_scalars=0, limit=16, flops=10**9, where=vmem
    ):
        return pl.pallas_call(
            kernel,
            in_specs=[smem] * len(scalars)
            + (where if isinstance(where, list) else [where] * len(inputs)),
            out_specs=[smem] * out_scalars + [vmem] * (len(outputs) - out_scalars),
            out_shape=[jax.ShapeDtypeStruct(shape, dtype) for shape, dtype in outputs],
            scratch_shapes=list(scratch),
            compiler_params=pltpu.CompilerParams(vmem_limit_bytes=int(limit * 2**20)),
            cost_estimate=pl.CostEstimate(
                flops=flops, bytes_accessed=2**20, transcendentals=0
            ),
        )(*scalars, *inputs)

    x_count = math.isqrt(seq_count)
    anywhere = pl.BlockSpec(memory_space=pltpu.HBM)
    along_x = list(range(1, x_count))
    along_y = list(range(x_count, seq_count, x_count))

    proj_own = proj_weight
    if halves == 2:
        (proj_own,) = call(
            half_kernel,
            [core],
            [proj_weight],
            [((head_width // 2, model_width), BF16)],
            scratch=[pltpu.SemaphoreType.DMA],
            where=anywhere,
        )
    proj_parts = {mask: send(proj_own, "seq", mask) for mask in along_y + along_x}

    slots, own, other = call(
        functools.partial(route_kernel, per_peer, piece_rows),
        [owner_place],
        [slot_owner, tokens],
        [((pieces_here,), jnp.int32)] + [((chips * block_rows, model_width), BF16)] * 2,
        scratch=[
            pltpu.SMEM((dp_count,), jnp.int32),
            pltpu.SMEM(slot_owner.shape, jnp.int32),
            pltpu.VMEM(tokens.shape, BF16),
            pltpu.SemaphoreType.DMA((2,)),
        ],
        out_scalars=1,
        limit=59,
        flops=3 * 10**10,
        where=anywhere,
    )
    payloads = call(
        functools.partial(merge_kernel, block_rows),
        [],
        [own, send(other, "dp", 1)],
        [((2 * block_rows, model_width), BF16)] * chips,
        scratch=[pltpu.VMEM(own.shape, BF16), pltpu.SemaphoreType.DMA],
        where=[anywhere, vmem],
    )
    arrived = [send(payload, "dp", 2 * mask) for mask, payload in enumerate(payloads)]

    def codes_of(group):
        return lambda rows, *places: row_codes(
            rows,
            group * (pieces_here // 2),
            per_peer,
            piece_rows,
            piece_rows * seq_count,
            *places,
        )

    weight = jnp.transpose(qkv_weight, (1, 2, 0)).reshape(3 * head_width, model_width)
    factors = jnp.transpose(modulation[0], (1, 0, 2))
    def project(blocks):
        (projected,) = call(
            functools.partial(project_kernel, head_size),
            [],
            [weight, qk_gain] + blocks,
            [((3 * head_width, seq_count * group_rows), BF16)],
            flops=3 * 10**9,
        )
        return projected

    near, far = [
        call(
            functools.partial(norm_kernel, clip_tokens, codes_of(group)),
            [owner_place, place],
            [clip_pieces, factors] + arrived[group * chips // 2 : (group + 1) * chips // 2],
            [((group_rows, model_width), BF16)],
            flops=(1 + 9 * group) * 10**9,
        )[0]
        for group in range(2)
    ]
    near, proj_parts = lax.optimization_barrier((near, proj_parts))
    near, proj_parts = lax.optimization_barrier((near, proj_parts))
    sides = {mask: send(near, "seq", mask) for mask in along_y + along_x}
    far, sides = lax.optimization_barrier((far, sides))
    far_blocks = [send(far, "seq", mask) for mask in range(seq_count)]
    halved = call(
        sides_kernel,
        [],
        [sides[mask] for mask in along_y + along_x],
        [((group_rows // 2, model_width), BF16)] * len(sides),
    )
    halved = dict(zip(along_y + along_x, halved))
    near_blocks = []
    for mask in range(seq_count):
        mx = mask % x_count
        my = mask - mx
        if mx > 0 and my > 0:
            near_blocks += [send(halved[my], "seq", mx), send(halved[mx], "seq", my)]
        else:
            near_blocks.append(sides[mask] if mask > 0 else near)
    stacked_near = project(near_blocks)
    (gathered,) = call(
        functools.partial(gather_kernel, group_rows, per_peer, piece_rows),
        [owner_place, place, clip_pieces],
        [stacked_near],
        [((clips_here, 3 * head_width, clip_tokens), BF16)],
        limit=16 if clip_tokens <= 256 else 48,
        flops=3 * 10**9,
    )
    gathered, proj_parts = lax.optimization_barrier((gathered, proj_parts))
    far_blocks, gathered = lax.optimization_barrier((far_blocks, gathered))
    stacked_far = project(far_blocks)
    swapped = {mask: send(proj_parts[mask], "dp", 1) for mask in proj_parts} if halves == 2 else {}
    stacked_far, proj_parts, swapped = lax.optimization_barrier(
        (stacked_far, proj_parts, swapped)
    )
    for my in along_y:
        for mx in along_x:
            proj_parts[my + mx] = send(proj_parts[my], "seq", mx)

    attended = call(
        functools.partial(attention_kernel, head_size, per_peer, piece_rows),
        [clip_length, owner_place, place, clip_pieces],
        [gathered, stacked_far],
        [((head_width, rows_here), BF16)] * seq_count,
        scratch=[pltpu.VMEM((head_width, seq_count * rows_here), F32)],
        limit=16 if clip_tokens <= 256 else 48,
        flops=8 * 10**9,
    )
    returned = [send(array, "seq", mask) for mask, array in enumerate(attended)]
    if halves == 2:
        _, late = lax.optimization_barrier((attended[0], proj_parts))
        swapped |= {mask: send(late[mask], "dp", 1) for mask in late if mask not in swapped}
    proj_parts = proj_parts | {seq_count + mask: swapped[mask] for mask in swapped}

    half_count = dp_count // 2
    far_masks = list(range(half_count, dp_count))
    outs = {mask: (index, 0) for index, mask in enumerate(far_masks)}
    for index in range(half_count // 2):
        outs[2 * index] = (half_count + index, 0)
        outs[2 * index + 1] = (half_count + half_count // 2, index * block_rows)
    def weights_of(masks):
        return [
            part
            for mask in masks
            for part in (
                [proj_weight]
                if mask == 0
                else [proj_parts[mask + half * seq_count] for half in range(halves)]
            )
        ]

    beside = [0] + along_x + along_y
    across = [mask for mask in range(seq_count) if mask not in beside]
    (partial,) = call(
        functools.partial(sides_output_kernel, beside, halves),
        [core],
        [returned[mask] for mask in beside] + weights_of(beside),
        [((rows_here, model_width), F32)],
        flops=10**10,
    )
    results = call(
        functools.partial(
            output_kernel,
            across,
            halves,
            clip_tokens,
            codes_of(0),
            [outs[mask] for mask in range(dp_count)],
        ),
        [core, clip_length, owner_place, place],
        [clip_pieces, factors, partial]
        + [returned[mask] for mask in across]
        + weights_of(across)
        + arrived,
        [((block_rows, model_width), BF16)] * (half_count + half_count // 2)
        + [((half_count // 2 * block_rows, model_width), BF16)],
        flops=3 * 10**9,
    )
    cut = half_count // 2
    swapped_back = send(results[-1], "dp", 1)
    near_own = list(results[half_count:-1])
    joined = call(
        functools.partial(join_kernel, block_rows),
        [],
        near_own[1:] + [swapped_back],
        [((2 * block_rows, model_width), BF16)] * (cut - 1),
    )
    later, joined = lax.optimization_barrier((list(results[cut:half_count]), list(joined)))
    first = [send(results[index], "dp", far_masks[index]) for index in range(cut)]
    first += [send(block, "dp", 2 * (index + 1)) for index, block in enumerate(joined)]
    last = [send(block, "dp", mask) for block, mask in zip(later, far_masks[cut:])]
    came_back = [near_own[0], swapped_back]
    for blocks, flops in ((first, 10**10), (last, 10**8)):
        rows = sum(block.shape[0] for block in blocks)
        came_back += call(
            stack_kernel, [], blocks, [((rows, model_width), BF16)], flops=flops
        )
    places = {0: (0, 0), 1: (1, 0)}
    for index in range(cut):
        places[far_masks[index]] = (2, index * block_rows)
        places[far_masks[cut + index]] = (3, index * block_rows)
    for mask in range(2, half_count):
        places[mask] = (2, (cut + mask - 2) * block_rows)
    (out,) = call(
        functools.partial(
            place_kernel, per_peer, piece_rows, [places[mask] for mask in range(dp_count)]
        ),
        [slots],
        came_back,
        [(tokens.shape, BF16)],
    )
    return out


def solution(mesh):
    return jax.shard_map(
        body,
        mesh=mesh,
        in_specs=(
            P("dp", None, "seq", None),
            P("dp", None),
            P("dp", None, None),
            P("dp", None),
            P("dp", None, None, None),
            P(None, None, "seq"),
            P(),
            P("seq", None),
        ),
        out_specs=P("dp", None, "seq", None),
        check_vma=False,
    )
```

```python
import functools
import math

import jax
import jax.numpy as jnp
from jax import lax
from jax.experimental import pallas as pl
from jax.experimental.pallas import tpu as pltpu
from jax.sharding import PartitionSpec as P

HEADS = 16
EPSILON = 1e-06
BF16 = jnp.bfloat16
F32 = jnp.float32


def send(array, axis, mask):
    if mask == 0:
        return array
    count = lax.axis_size(axis)
    return lax.ppermute(array, axis, [(i, i ^ mask) for i in range(count)])


def route_kernel(per_peer, piece_rows, place_ref, owner_hbm, token_hbm, *refs):
    slot_ref, own_ref, other_ref, filled_ref, owner_ref, token_ref, sems = refs
    peers = filled_ref.shape[0]
    owner_copy = pltpu.make_async_copy(owner_hbm, owner_ref, sems.at[0])
    token_copy = pltpu.make_async_copy(token_hbm, token_ref, sems.at[1])
    owner_copy.start()
    token_copy.start()
    for peer in range(peers):
        filled_ref[peer] = peer * per_peer
    owner_copy.wait()

    @pl.loop(0, peers * per_peer, unroll=8)
    def _(slot):
        peer = jnp.bitwise_xor(owner_ref[0, slot], place_ref[0])
        at = filled_ref[peer]
        filled_ref[peer] = at + 1
        slot_ref[at] = slot

    token_copy.wait()
    for peer in range(peers):
        ref = own_ref if peer % 2 == 0 else other_ref
        for m in range(per_peer):
            at = (peer // 2 * per_peer + m) * piece_rows
            ref[at : at + piece_rows, :] = token_ref[0, slot_ref[peer * per_peer + m]]


def merge_kernel(rows, own_hbm, other_ref, *refs):
    refs, own_ref, sem = refs[:-2], refs[-2], refs[-1]
    copy = pltpu.make_async_copy(own_hbm, own_ref, sem)
    copy.start()
    for index, ref in enumerate(refs):
        ref[rows:] = other_ref[index * rows : (index + 1) * rows]
    copy.wait()
    for index, ref in enumerate(refs):
        ref[:rows] = own_ref[index * rows : (index + 1) * rows]


def sides_kernel(*refs):
    count = len(refs) // 2
    for index in range(count):
        rows = refs[count + index].shape[0]
        start = 0 if index < count // 2 else rows
        refs[count + index][...] = refs[index][start : start + rows]


def half_kernel(core_ref, weight_hbm, out_ref, sem):
    rows = out_ref.shape[0]
    start = pl.multiple_of(core_ref[0] * rows, 16)
    copy = pltpu.make_async_copy(weight_hbm.at[pl.ds(start, rows), :], out_ref, sem)
    copy.start()
    copy.wait()


def place_kernel(per_peer, piece_rows, places, slot_ref, *refs):
    block_refs, out_ref = refs[:-1], refs[-1]
    for peer, (block, first) in enumerate(places):
        for m in range(per_peer):
            slot = slot_ref[peer * per_peer + m]
            start = first + m * piece_rows
            out_ref[0, slot] = block_refs[block][start : start + piece_rows, :]


def stack_kernel(*refs):
    start = 0
    for ref in refs[:-1]:
        refs[-1][start : start + ref.shape[0]] = ref[...]
        start += ref.shape[0]


def crossing_kernel(rows, own_ref, *refs):
    refs[-1][:rows] = own_ref[...]
    for index, ref in enumerate(refs[:-1]):
        refs[-1][(index + 1) * rows : (index + 2) * rows] = ref[rows:]


def arrival_of(piece, per_peer, owner_place):
    source = jnp.bitwise_xor(lax.div(piece, per_peer), owner_place)
    return source * per_peer + lax.rem(piece, per_peer)


def row_codes(rows, first_piece, per_peer, piece_rows, token_rows, owner_place, place, table):
    row = lax.broadcasted_iota(jnp.int32, (rows, 1), 0)
    arrival = arrival_of(first_piece + lax.div(row, piece_rows), per_peer, owner_place)
    lane = lax.broadcasted_iota(jnp.int32, (1, table.shape[1]), 1)
    found = jnp.zeros((rows, 1), jnp.int32)
    for clip in range(table.shape[0]):
        number = jnp.where(
            arrival == table[clip : clip + 1], lane + clip * table.shape[1], 0
        )
        found += jnp.sum(number, axis=1, keepdims=True)
    return found * token_rows + place * piece_rows + lax.rem(row, piece_rows)


def pick(clip, table):
    rows = jnp.broadcast_to(table[0:1], (clip.shape[0], table.shape[1]))
    for index in range(1, table.shape[0]):
        rows = jnp.where(clip == index, table[index : index + 1], rows)
    return rows


def norm_kernel(
    clip_tokens, codes_of, owner_ref, place_ref, table_ref, modulation_ref, *refs
):
    block_refs, out_ref = refs[:-1], refs[-1]
    code = codes_of(out_ref.shape[0], owner_ref[0], place_ref[0], table_ref[0])
    clip = lax.div(code, clip_tokens)
    rows = jnp.concatenate([ref[...].astype(F32) for ref in block_refs], axis=0)
    average = jnp.mean(rows, axis=-1, keepdims=True)
    centered = rows - average
    variance = jnp.mean(centered * centered, axis=-1, keepdims=True)
    normed = centered * lax.rsqrt(variance + EPSILON)
    shift = pick(clip, modulation_ref[0].astype(F32))
    scale = pick(clip, modulation_ref[1].astype(F32))
    out_ref[...] = (normed * (1.0 + scale) + shift).astype(BF16)


def project_kernel(head_size, weight_ref, gain_ref, *refs):
    hidden_refs, out_ref = refs[:-1], refs[-1]
    hidden = jnp.concatenate([ref[...] for ref in hidden_refs], axis=0)
    projected = lax.dot_general(
        weight_ref[...], hidden, (((1,), (1,)), ((), ())), preferred_element_type=F32
    )
    width = weight_ref.shape[0] // 3
    shape = (head_size, head_size)
    diagonal = lax.broadcasted_iota(jnp.int32, shape, 0) == lax.broadcasted_iota(
        jnp.int32, shape, 1
    )
    found = []
    for part in range(2):
        gain = jnp.sum(
            jnp.where(diagonal, gain_ref[part : part + 1, :], 0.0), axis=1, keepdims=True
        )
        for start in range(part * width, (part + 1) * width, head_size):
            value = projected[start : start + head_size]
            square = jnp.sum(value * value, axis=0, keepdims=True) * (1.0 / head_size)
            found.append(value * lax.rsqrt(square + EPSILON) * gain)
    found.append(projected[2 * width :])
    out_ref[...] = jnp.concatenate(found, axis=0).astype(BF16)


def token_codes(tokens, group_rows, per_peer, piece_rows, owner_ref, place_ref, table_ref):
    clips, per_clip = table_ref.shape[1:]
    seq_count = tokens // 2 // group_rows
    token = lax.broadcasted_iota(jnp.int32, (1, tokens), 1)
    row = lax.rem(token, group_rows)
    block = lax.div(token, group_rows)
    piece = lax.div(block, seq_count) * (group_rows // piece_rows) + lax.div(row, piece_rows)
    arrival = arrival_of(piece, per_peer, owner_ref[0])
    found = jnp.zeros_like(token)
    for clip in range(clips):
        for p in range(per_clip):
            found = jnp.where(arrival == table_ref[0, clip, p], clip * per_clip + p, found)
    source = jnp.bitwise_xor(lax.rem(block, seq_count), place_ref[0])
    return found * (piece_rows * seq_count) + source * piece_rows + lax.rem(row, piece_rows)


def gather_kernel(
    group_rows, per_peer, piece_rows, owner_ref, place_ref, table_ref, stacked_ref, out_ref
):
    count = stacked_ref.shape[1]
    code = token_codes(
        2 * count, group_rows, per_peer, piece_rows, owner_ref, place_ref, table_ref
    )[:, :count]
    clip_tokens = out_ref.shape[2]
    position = lax.broadcasted_iota(jnp.int32, (clip_tokens, 1), 0)
    for clip in range(out_ref.shape[0]):
        chosen = jnp.where(code == position + clip * clip_tokens, 1.0, 0.0).astype(BF16)
        out_ref[clip] = lax.dot_general(
            stacked_ref[...], chosen, (((1,), (1,)), ((), ())), preferred_element_type=F32
        ).astype(BF16)


def attention_kernel(
    head_size, per_peer, piece_rows, length_ref, owner_ref, place_ref, table_ref, *refs
):
    near_ref, far_ref, out_refs, all_ref = refs[0], refs[1], refs[2:-1], refs[-1]
    clips, features, clip_tokens = near_ref.shape
    width, tokens = features // 3, clips * clip_tokens
    seq_count = len(out_refs)
    group_rows = tokens // 2 // seq_count
    code = token_codes(
        tokens, group_rows, per_peer, piece_rows, owner_ref, place_ref, table_ref
    )
    position = lax.broadcasted_iota(jnp.int32, (clip_tokens, 1), 0)
    key = lax.broadcasted_iota(jnp.int32, (8, clip_tokens), 1)
    heads = range(0, width, head_size)
    scale = math.log2(math.e) / math.sqrt(head_size)
    for clip in range(clips):
        chosen = jnp.where(code == position + clip * clip_tokens, 1.0, 0.0).astype(BF16)
        picked = near_ref[clip].astype(F32) + lax.dot_general(
            far_ref[...],
            chosen[:, tokens // 2 :],
            (((1,), (1,)), ((), ())),
            preferred_element_type=F32,
        )
        in_clip = jnp.where(key < length_ref[0, clip], 1.0, 0.0)
        scores = [
            jnp.dot(
                jnp.transpose(picked[width + head : width + head + head_size]).astype(BF16),
                picked[head : head + head_size].astype(BF16),
                preferred_element_type=F32,
            )
            for head in heads
        ]
        unscaled = [jnp.exp2(score * scale).astype(BF16) for score in scores]
        outs = []
        for head, weights in zip(heads, unscaled):
            values = picked[2 * width + head : 2 * width + head + head_size] * in_clip[:1]
            values = jnp.concatenate([values, in_clip], axis=0).astype(BF16)
            summed = jnp.dot(values, weights, preferred_element_type=F32)
            outs.append(summed[:head_size] * (1.0 / summed[head_size : head_size + 1]))
        attended = jnp.concatenate(outs, axis=0).astype(BF16)
        back = jnp.dot(attended, chosen, preferred_element_type=F32)
        if clip == 0:
            all_ref[...] = back
        else:
            all_ref[...] += back
    for index, ref in enumerate(out_refs):
        for group in range(2):
            start = (group * seq_count + index) * group_rows
            ref[:, group * group_rows : (group + 1) * group_rows] = all_ref[
                :, start : start + group_rows
            ].astype(BF16)


def projected_rows(masks, halves, core_ref, head_refs, weight_refs):
    branch = None
    for mask, head_ref in zip(masks, head_refs):
        parts = [weight_refs[0][...]]
        if mask > 0:
            parts = [ref[...] for ref in weight_refs[:halves]]
            weight_refs = weight_refs[halves:]
            if halves == 2:
                first = core_ref[0] == 0
                parts = [
                    jnp.where(first, parts[0], parts[1]),
                    jnp.where(first, parts[1], parts[0]),
                ]
        else:
            weight_refs = weight_refs[1:]
        term = lax.dot_general(
            head_ref[...],
            jnp.concatenate(parts, axis=0),
            (((0,), (0,)), ((), ())),
            preferred_element_type=F32,
        )
        branch = term if branch is None else branch + term
    return branch


def sides_output_kernel(masks, halves, core_ref, *refs):
    refs[-1][...] = projected_rows(
        masks, halves, core_ref, refs[: len(masks)], refs[len(masks) : -1]
    )


def output_kernel(
    masks,
    halves,
    clip_tokens,
    codes_of,
    owner_masks,
    core_ref,
    length_ref,
    owner_ref,
    place_ref,
    table_ref,
    modulation_ref,
    partial_ref,
    *refs,
):
    head_refs, refs = refs[: len(masks)], refs[len(masks) :]
    weight_refs, refs = refs[: len(masks) * halves], refs[len(masks) * halves :]
    count = len(owner_masks) // 2
    block_refs, out_refs = refs[:count], refs[count:]
    rows = block_refs[0].shape[0] // 2
    branch = partial_ref[...] + projected_rows(masks, halves, core_ref, head_refs, weight_refs)
    code = codes_of(branch.shape[0], owner_ref[0], place_ref[0], table_ref[0])
    clip = lax.div(code, clip_tokens)
    limit = jnp.zeros_like(code)
    for index in range(length_ref.shape[1]):
        limit = jnp.where(clip == index, length_ref[0, index], limit)
    kept = lax.rem(code, clip_tokens) < limit
    branch = pick(clip, modulation_ref[2].astype(F32)) * branch
    for index, (out, first) in enumerate(owner_masks):
        at = slice(index * rows, (index + 1) * rows)
        side = slice(index % 2 * rows, (index % 2 + 1) * rows)
        result = block_refs[index // 2][side].astype(F32) + branch[at]
        out_refs[out][first : first + rows] = jnp.where(kept[at], result, 0.0).astype(BF16)


def body(
    tokens, slot_owner, clip_pieces, clip_length, modulation, qkv_weight, qk_gain, proj_weight
):
    dp_count = lax.axis_size("dp")
    seq_count = lax.axis_size("seq")
    pieces_here = tokens.shape[1]
    piece_rows = tokens.shape[2]
    model_width = tokens.shape[3]
    per_peer = pieces_here // dp_count
    head_size = qk_gain.shape[1]
    heads = HEADS // seq_count
    head_width = heads * head_size
    clips_here, per_clip = clip_pieces.shape[1:]
    clip_tokens = per_clip * piece_rows * seq_count
    block_rows = per_peer * piece_rows
    rows_here = pieces_here * piece_rows
    group_rows = rows_here // 2
    chips = dp_count // 2
    owner_place = lax.axis_index("dp").astype(jnp.int32)
    place = lax.axis_index("seq").astype(jnp.int32).reshape(1)
    core = lax.rem(owner_place, 2).reshape(1)
    owner_place = owner_place.reshape(1)
    halves = 2 if heads % 2 == 0 else 1

    smem = pl.BlockSpec(memory_space=pltpu.SMEM)
    vmem = pl.BlockSpec(memory_space=pltpu.VMEM)

    def call(
        kernel, scalars, inputs, outputs, scratch=(), out_scalars=0, limit=16, flops=10**9, where=vmem
    ):
        return pl.pallas_call(
            kernel,
            in_specs=[smem] * len(scalars)
            + (where if isinstance(where, list) else [where] * len(inputs)),
            out_specs=[smem] * out_scalars + [vmem] * (len(outputs) - out_scalars),
            out_shape=[jax.ShapeDtypeStruct(shape, dtype) for shape, dtype in outputs],
            scratch_shapes=list(scratch),
            compiler_params=pltpu.CompilerParams(vmem_limit_bytes=int(limit * 2**20)),
            cost_estimate=pl.CostEstimate(
                flops=flops, bytes_accessed=2**20, transcendentals=0
            ),
        )(*scalars, *inputs)

    x_count = math.isqrt(seq_count)
    anywhere = pl.BlockSpec(memory_space=pltpu.HBM)
    along_x = list(range(1, x_count))
    along_y = list(range(x_count, seq_count, x_count))

    proj_own = proj_weight
    if halves == 2:
        (proj_own,) = call(
            half_kernel,
            [core],
            [proj_weight],
            [((head_width // 2, model_width), BF16)],
            scratch=[pltpu.SemaphoreType.DMA],
            where=anywhere,
        )
    proj_parts = {mask: send(proj_own, "seq", mask) for mask in along_y + along_x}

    slots, own, other = call(
        functools.partial(route_kernel, per_peer, piece_rows),
        [owner_place],
        [slot_owner, tokens],
        [((pieces_here,), jnp.int32)] + [((chips * block_rows, model_width), BF16)] * 2,
        scratch=[
            pltpu.SMEM((dp_count,), jnp.int32),
            pltpu.SMEM(slot_owner.shape, jnp.int32),
            pltpu.VMEM(tokens.shape, BF16),
            pltpu.SemaphoreType.DMA((2,)),
        ],
        out_scalars=1,
        limit=59,
        flops=3 * 10**10,
        where=anywhere,
    )
    payloads = call(
        functools.partial(merge_kernel, block_rows),
        [],
        [own, send(other, "dp", 1)],
        [((2 * block_rows, model_width), BF16)] * chips,
        scratch=[pltpu.VMEM(own.shape, BF16), pltpu.SemaphoreType.DMA],
        where=[anywhere, vmem],
    )
    arrived = [send(payload, "dp", 2 * mask) for mask, payload in enumerate(payloads)]

    def codes_of(group):
        return lambda rows, *places: row_codes(
            rows,
            group * (pieces_here // 2),
            per_peer,
            piece_rows,
            piece_rows * seq_count,
            *places,
        )

    weight = jnp.transpose(qkv_weight, (1, 2, 0)).reshape(3 * head_width, model_width)
    factors = jnp.transpose(modulation[0], (1, 0, 2))
    def project(blocks):
        (projected,) = call(
            functools.partial(project_kernel, head_size),
            [],
            [weight, qk_gain] + blocks,
            [((3 * head_width, seq_count * group_rows), BF16)],
            flops=3 * 10**9,
        )
        return projected

    near, far = [
        call(
            functools.partial(norm_kernel, clip_tokens, codes_of(group)),
            [owner_place, place],
            [clip_pieces, factors] + arrived[group * chips // 2 : (group + 1) * chips // 2],
            [((group_rows, model_width), BF16)],
            flops=(1 + 9 * group) * 10**9,
        )[0]
        for group in range(2)
    ]
    near, proj_parts = lax.optimization_barrier((near, proj_parts))
    near, proj_parts = lax.optimization_barrier((near, proj_parts))
    sides = {mask: send(near, "seq", mask) for mask in along_y + along_x}
    far, sides = lax.optimization_barrier((far, sides))
    far_blocks = [send(far, "seq", mask) for mask in range(seq_count)]
    halved = call(
        sides_kernel,
        [],
        [sides[mask] for mask in along_y + along_x],
        [((group_rows // 2, model_width), BF16)] * len(sides),
    )
    halved = dict(zip(along_y + along_x, halved))
    near_blocks = []
    for mask in range(seq_count):
        mx = mask % x_count
        my = mask - mx
        if mx > 0 and my > 0:
            near_blocks += [send(halved[my], "seq", mx), send(halved[mx], "seq", my)]
        else:
            near_blocks.append(sides[mask] if mask > 0 else near)
    stacked_near = project(near_blocks)
    (gathered,) = call(
        functools.partial(gather_kernel, group_rows, per_peer, piece_rows),
        [owner_place, place, clip_pieces],
        [stacked_near],
        [((clips_here, 3 * head_width, clip_tokens), BF16)],
        limit=16 if clip_tokens <= 256 else 48,
        flops=3 * 10**9,
    )
    gathered, proj_parts = lax.optimization_barrier((gathered, proj_parts))
    far_blocks, gathered = lax.optimization_barrier((far_blocks, gathered))
    stacked_far = project(far_blocks)
    swapped = {mask: send(proj_parts[mask], "dp", 1) for mask in proj_parts} if halves == 2 else {}
    stacked_far, proj_parts, swapped = lax.optimization_barrier(
        (stacked_far, proj_parts, swapped)
    )
    for my in along_y:
        for mx in along_x:
            proj_parts[my + mx] = send(proj_parts[my], "seq", mx)

    attended = call(
        functools.partial(attention_kernel, head_size, per_peer, piece_rows),
        [clip_length, owner_place, place, clip_pieces],
        [gathered, stacked_far],
        [((head_width, rows_here), BF16)] * seq_count,
        scratch=[pltpu.VMEM((head_width, seq_count * rows_here), F32)],
        limit=16 if clip_tokens <= 256 else 48,
        flops=8 * 10**9,
    )
    returned = [send(array, "seq", mask) for mask, array in enumerate(attended)]
    if halves == 2:
        _, late = lax.optimization_barrier((attended[0], proj_parts))
        swapped |= {mask: send(late[mask], "dp", 1) for mask in late if mask not in swapped}
    proj_parts = proj_parts | {seq_count + mask: swapped[mask] for mask in swapped}

    half_count = dp_count // 2
    far_masks = list(range(half_count, dp_count))
    outs = {mask: (index, 0) for index, mask in enumerate(far_masks)}
    for mask in range(2, half_count):
        outs[mask] = (half_count + mask // 2 - 1, mask % 2 * block_rows)
    outs[0], outs[1] = [(half_count + half_count // 2 - 1 + core_of, 0) for core_of in range(2)]

    def weights_of(masks):
        return [
            part
            for mask in masks
            for part in (
                [proj_weight]
                if mask == 0
                else [proj_parts[mask + half * seq_count] for half in range(halves)]
            )
        ]

    beside = [0] + along_x + along_y
    across = [mask for mask in range(seq_count) if mask not in beside]
    (partial,) = call(
        functools.partial(sides_output_kernel, beside, halves),
        [core],
        [returned[mask] for mask in beside] + weights_of(beside),
        [((rows_here, model_width), F32)],
        flops=10**10,
    )
    results = call(
        functools.partial(
            output_kernel,
            across,
            halves,
            clip_tokens,
            codes_of(0),
            [outs[mask] for mask in range(dp_count)],
        ),
        [core, clip_length, owner_place, place],
        [clip_pieces, factors, partial]
        + [returned[mask] for mask in across]
        + weights_of(across)
        + arrived,
        [((block_rows, model_width), BF16)] * half_count
        + [((2 * block_rows, model_width), BF16)] * (half_count // 2 - 1)
        + [((block_rows, model_width), BF16)] * 2,
        flops=3 * 10**9,
    )
    near_back = [
        send(block, "dp", 2 * (index + 1)) for index, block in enumerate(results[half_count:-2])
    ]
    far_back = [send(block, "dp", mask) for block, mask in zip(results, far_masks)]
    (crossing,) = call(
        functools.partial(crossing_kernel, block_rows),
        [],
        [results[-1]] + near_back,
        [((half_count // 2 * block_rows, model_width), BF16)],
    )
    crossed = send(crossing, "dp", 1)
    (far_back,) = call(
        stack_kernel,
        [],
        far_back,
        [((half_count * block_rows, model_width), BF16)],
        flops=10**10,
    )
    came_back = [far_back, crossed, results[-2]] + near_back
    places = {mask: (0, index * block_rows) for index, mask in enumerate(far_masks)}
    places[0] = (2, 0)
    for index in range(half_count // 2):
        places[2 * index + 1] = (1, index * block_rows)
        if index > 0:
            places[2 * index] = (2 + index, 0)
    (out,) = call(
        functools.partial(
            place_kernel, per_peer, piece_rows, [places[mask] for mask in range(dp_count)]
        ),
        [slots],
        came_back,
        [(tokens.shape, BF16)],
    )
    return out


def solution(mesh):
    return jax.shard_map(
        body,
        mesh=mesh,
        in_specs=(
            P("dp", None, "seq", None),
            P("dp", None),
            P("dp", None, None),
            P("dp", None),
            P("dp", None, None, None),
            P(None, None, "seq"),
            P(),
            P("seq", None),
        ),
        out_specs=P("dp", None, "seq", None),
        check_vma=False,
    )
```

```python
import functools
import math

import jax
import jax.numpy as jnp
from jax import lax
from jax.experimental import pallas as pl
from jax.experimental.pallas import tpu as pltpu
from jax.sharding import PartitionSpec as P

HEADS = 16
EPSILON = 1e-06
BF16 = jnp.bfloat16
F32 = jnp.float32


def send(array, axis, mask):
    if mask == 0:
        return array
    count = lax.axis_size(axis)
    return lax.ppermute(array, axis, [(i, i ^ mask) for i in range(count)])


def route_kernel(per_peer, piece_rows, place_ref, owner_hbm, token_hbm, *refs):
    slot_ref, own_ref, other_ref, filled_ref, owner_ref, token_ref, sems = refs
    peers = filled_ref.shape[0]
    owner_copy = pltpu.make_async_copy(owner_hbm, owner_ref, sems.at[0])
    token_copy = pltpu.make_async_copy(token_hbm, token_ref, sems.at[1])
    owner_copy.start()
    token_copy.start()
    for peer in range(peers):
        filled_ref[peer] = peer * per_peer
    owner_copy.wait()

    @pl.loop(0, peers * per_peer, unroll=8)
    def _(slot):
        peer = jnp.bitwise_xor(owner_ref[0, slot], place_ref[0])
        at = filled_ref[peer]
        filled_ref[peer] = at + 1
        slot_ref[at] = slot

    token_copy.wait()
    for peer in range(peers):
        ref = own_ref if peer % 2 == 0 else other_ref
        for m in range(per_peer):
            at = (peer // 2 * per_peer + m) * piece_rows
            ref[at : at + piece_rows, :] = token_ref[0, slot_ref[peer * per_peer + m]]


def merge_kernel(rows, own_hbm, other_ref, *refs):
    refs, own_ref, sem = refs[:-2], refs[-2], refs[-1]
    copy = pltpu.make_async_copy(own_hbm, own_ref, sem)
    copy.start()
    for index, ref in enumerate(refs):
        ref[rows:] = other_ref[index * rows : (index + 1) * rows]
    copy.wait()
    for index, ref in enumerate(refs):
        ref[:rows] = own_ref[index * rows : (index + 1) * rows]


def sides_kernel(*refs):
    count = len(refs) // 2
    for index in range(count):
        rows = refs[count + index].shape[0]
        start = 0 if index < count // 2 else rows
        refs[count + index][...] = refs[index][start : start + rows]


def half_kernel(core_ref, weight_hbm, out_ref, sem):
    rows = out_ref.shape[0]
    start = pl.multiple_of(core_ref[0] * rows, 16)
    copy = pltpu.make_async_copy(weight_hbm.at[pl.ds(start, rows), :], out_ref, sem)
    copy.start()
    copy.wait()


def place_kernel(per_peer, piece_rows, places, slot_ref, *refs):
    block_refs, out_ref = refs[:-1], refs[-1]
    for peer, (block, first) in enumerate(places):
        for m in range(per_peer):
            slot = slot_ref[peer * per_peer + m]
            start = first + m * piece_rows
            out_ref[0, slot] = block_refs[block][start : start + piece_rows, :]


def stack_kernel(*refs):
    start = 0
    for ref in refs[:-1]:
        refs[-1][start : start + ref.shape[0]] = ref[...]
        start += ref.shape[0]


def crossing_kernel(rows, own_ref, *refs):
    refs[-1][:rows] = own_ref[...]
    for index, ref in enumerate(refs[:-1]):
        refs[-1][(index + 1) * rows : (index + 2) * rows] = ref[rows:]


def arrival_of(piece, per_peer, owner_place):
    source = jnp.bitwise_xor(lax.div(piece, per_peer), owner_place)
    return source * per_peer + lax.rem(piece, per_peer)


def row_codes(rows, first_piece, per_peer, piece_rows, token_rows, owner_place, place, table):
    row = lax.broadcasted_iota(jnp.int32, (rows, 1), 0)
    arrival = arrival_of(first_piece + lax.div(row, piece_rows), per_peer, owner_place)
    lane = lax.broadcasted_iota(jnp.int32, (1, table.shape[1]), 1)
    found = jnp.zeros((rows, 1), jnp.int32)
    for clip in range(table.shape[0]):
        number = jnp.where(
            arrival == table[clip : clip + 1], lane + clip * table.shape[1], 0
        )
        found += jnp.sum(number, axis=1, keepdims=True)
    return found * token_rows + place * piece_rows + lax.rem(row, piece_rows)


def pick(clip, table):
    rows = jnp.broadcast_to(table[0:1], (clip.shape[0], table.shape[1]))
    for index in range(1, table.shape[0]):
        rows = jnp.where(clip == index, table[index : index + 1], rows)
    return rows


def norm_kernel(
    clip_tokens, codes_of, owner_ref, place_ref, table_ref, modulation_ref, *refs
):
    block_refs, out_ref = refs[:-1], refs[-1]
    code = codes_of(out_ref.shape[0], owner_ref[0], place_ref[0], table_ref[0])
    clip = lax.div(code, clip_tokens)
    rows = jnp.concatenate([ref[...].astype(F32) for ref in block_refs], axis=0)
    average = jnp.mean(rows, axis=-1, keepdims=True)
    centered = rows - average
    variance = jnp.mean(centered * centered, axis=-1, keepdims=True)
    normed = centered * lax.rsqrt(variance + EPSILON)
    shift = pick(clip, modulation_ref[0].astype(F32))
    scale = pick(clip, modulation_ref[1].astype(F32))
    out_ref[...] = (normed * (1.0 + scale) + shift).astype(BF16)


def project_kernel(head_size, weight_ref, gain_ref, *refs):
    hidden_refs, out_ref = refs[:-1], refs[-1]
    hidden = jnp.concatenate([ref[...] for ref in hidden_refs], axis=0)
    projected = lax.dot_general(
        weight_ref[...], hidden, (((1,), (1,)), ((), ())), preferred_element_type=F32
    )
    width = weight_ref.shape[0] // 3
    shape = (head_size, head_size)
    diagonal = lax.broadcasted_iota(jnp.int32, shape, 0) == lax.broadcasted_iota(
        jnp.int32, shape, 1
    )
    found = []
    for part in range(2):
        gain = jnp.sum(
            jnp.where(diagonal, gain_ref[part : part + 1, :], 0.0), axis=1, keepdims=True
        )
        for start in range(part * width, (part + 1) * width, head_size):
            value = projected[start : start + head_size]
            square = jnp.sum(value * value, axis=0, keepdims=True) * (1.0 / head_size)
            found.append(value * lax.rsqrt(square + EPSILON) * gain)
    found.append(projected[2 * width :])
    out_ref[...] = jnp.concatenate(found, axis=0).astype(BF16)


def token_codes(tokens, group_rows, per_peer, piece_rows, owner_ref, place_ref, table_ref):
    clips, per_clip = table_ref.shape[1:]
    seq_count = tokens // 2 // group_rows
    token = lax.broadcasted_iota(jnp.int32, (1, tokens), 1)
    row = lax.rem(token, group_rows)
    block = lax.div(token, group_rows)
    piece = lax.div(block, seq_count) * (group_rows // piece_rows) + lax.div(row, piece_rows)
    arrival = arrival_of(piece, per_peer, owner_ref[0])
    found = jnp.zeros_like(token)
    for clip in range(clips):
        for p in range(per_clip):
            found = jnp.where(arrival == table_ref[0, clip, p], clip * per_clip + p, found)
    source = jnp.bitwise_xor(lax.rem(block, seq_count), place_ref[0])
    return found * (piece_rows * seq_count) + source * piece_rows + lax.rem(row, piece_rows)


def gather_kernel(
    first, group_rows, per_peer, piece_rows, owner_ref, place_ref, table_ref, stacked_ref, *refs
):
    out_ref = refs[-1]
    clips, _, clip_tokens = out_ref.shape
    code = token_codes(
        clips * clip_tokens, group_rows, per_peer, piece_rows, owner_ref, place_ref, table_ref
    )[:, first : first + stacked_ref.shape[1]]
    position = lax.broadcasted_iota(jnp.int32, (clip_tokens, 1), 0)
    for clip in range(clips):
        chosen = jnp.where(code == position + clip * clip_tokens, 1.0, 0.0).astype(BF16)
        picked = lax.dot_general(
            stacked_ref[...], chosen, (((1,), (1,)), ((), ())), preferred_element_type=F32
        )
        if len(refs) > 1:
            picked += refs[0][clip].astype(F32)
        out_ref[clip] = picked.astype(BF16)


def attention_kernel(
    head_size, per_peer, piece_rows, length_ref, owner_ref, place_ref, table_ref, *refs
):
    early_ref, late_ref, out_refs, all_ref = refs[0], refs[1], refs[2:-1], refs[-1]
    clips, features, clip_tokens = early_ref.shape
    width, tokens = features // 3, clips * clip_tokens
    seq_count = len(out_refs)
    group_rows = tokens // 2 // seq_count
    code = token_codes(
        tokens, group_rows, per_peer, piece_rows, owner_ref, place_ref, table_ref
    )
    position = lax.broadcasted_iota(jnp.int32, (clip_tokens, 1), 0)
    key = lax.broadcasted_iota(jnp.int32, (8, clip_tokens), 1)
    heads = range(0, width, head_size)
    scale = math.log2(math.e) / math.sqrt(head_size)
    for clip in range(clips):
        chosen = jnp.where(code == position + clip * clip_tokens, 1.0, 0.0).astype(BF16)
        picked = early_ref[clip].astype(F32) + lax.dot_general(
            late_ref[...],
            chosen[:, tokens - late_ref.shape[1] :],
            (((1,), (1,)), ((), ())),
            preferred_element_type=F32,
        )
        in_clip = jnp.where(key < length_ref[0, clip], 1.0, 0.0)
        scores = [
            jnp.dot(
                jnp.transpose(picked[width + head : width + head + head_size]).astype(BF16),
                picked[head : head + head_size].astype(BF16),
                preferred_element_type=F32,
            )
            for head in heads
        ]
        unscaled = [jnp.exp2(score * scale).astype(BF16) for score in scores]
        outs = []
        for head, weights in zip(heads, unscaled):
            values = picked[2 * width + head : 2 * width + head + head_size] * in_clip[:1]
            values = jnp.concatenate([values, in_clip], axis=0).astype(BF16)
            summed = jnp.dot(values, weights, preferred_element_type=F32)
            outs.append(summed[:head_size] * (1.0 / summed[head_size : head_size + 1]))
        attended = jnp.concatenate(outs, axis=0).astype(BF16)
        back = jnp.dot(attended, chosen, preferred_element_type=F32)
        if clip == 0:
            all_ref[...] = back
        else:
            all_ref[...] += back
    for index, ref in enumerate(out_refs):
        for group in range(2):
            start = (group * seq_count + index) * group_rows
            ref[:, group * group_rows : (group + 1) * group_rows] = all_ref[
                :, start : start + group_rows
            ].astype(BF16)


def projected_rows(masks, halves, core_ref, head_refs, weight_refs):
    branch = None
    for mask, head_ref in zip(masks, head_refs):
        parts = [weight_refs[0][...]]
        if mask > 0:
            parts = [ref[...] for ref in weight_refs[:halves]]
            weight_refs = weight_refs[halves:]
            if halves == 2:
                first = core_ref[0] == 0
                parts = [
                    jnp.where(first, parts[0], parts[1]),
                    jnp.where(first, parts[1], parts[0]),
                ]
        else:
            weight_refs = weight_refs[1:]
        term = lax.dot_general(
            head_ref[...],
            jnp.concatenate(parts, axis=0),
            (((0,), (0,)), ((), ())),
            preferred_element_type=F32,
        )
        branch = term if branch is None else branch + term
    return branch


def sides_output_kernel(masks, halves, core_ref, *refs):
    refs[-1][...] = projected_rows(
        masks, halves, core_ref, refs[: len(masks)], refs[len(masks) : -1]
    )


def output_kernel(
    masks,
    halves,
    clip_tokens,
    codes_of,
    owner_masks,
    core_ref,
    length_ref,
    owner_ref,
    place_ref,
    table_ref,
    modulation_ref,
    partial_ref,
    *refs,
):
    head_refs, refs = refs[: len(masks)], refs[len(masks) :]
    weight_refs, refs = refs[: len(masks) * halves], refs[len(masks) * halves :]
    count = len(owner_masks) // 2
    block_refs, out_refs = refs[:count], refs[count:]
    rows = block_refs[0].shape[0] // 2
    branch = partial_ref[...] + projected_rows(masks, halves, core_ref, head_refs, weight_refs)
    code = codes_of(branch.shape[0], owner_ref[0], place_ref[0], table_ref[0])
    clip = lax.div(code, clip_tokens)
    limit = jnp.zeros_like(code)
    for index in range(length_ref.shape[1]):
        limit = jnp.where(clip == index, length_ref[0, index], limit)
    kept = lax.rem(code, clip_tokens) < limit
    branch = pick(clip, modulation_ref[2].astype(F32)) * branch
    for index, (out, first) in enumerate(owner_masks):
        at = slice(index * rows, (index + 1) * rows)
        side = slice(index % 2 * rows, (index % 2 + 1) * rows)
        result = block_refs[index // 2][side].astype(F32) + branch[at]
        out_refs[out][first : first + rows] = jnp.where(kept[at], result, 0.0).astype(BF16)


def body(
    tokens, slot_owner, clip_pieces, clip_length, modulation, qkv_weight, qk_gain, proj_weight
):
    dp_count = lax.axis_size("dp")
    seq_count = lax.axis_size("seq")
    pieces_here = tokens.shape[1]
    piece_rows = tokens.shape[2]
    model_width = tokens.shape[3]
    per_peer = pieces_here // dp_count
    head_size = qk_gain.shape[1]
    heads = HEADS // seq_count
    head_width = heads * head_size
    clips_here, per_clip = clip_pieces.shape[1:]
    clip_tokens = per_clip * piece_rows * seq_count
    block_rows = per_peer * piece_rows
    rows_here = pieces_here * piece_rows
    group_rows = rows_here // 2
    chips = dp_count // 2
    owner_place = lax.axis_index("dp").astype(jnp.int32)
    place = lax.axis_index("seq").astype(jnp.int32).reshape(1)
    core = lax.rem(owner_place, 2).reshape(1)
    owner_place = owner_place.reshape(1)
    halves = 2 if heads % 2 == 0 else 1

    smem = pl.BlockSpec(memory_space=pltpu.SMEM)
    vmem = pl.BlockSpec(memory_space=pltpu.VMEM)

    def call(
        kernel, scalars, inputs, outputs, scratch=(), out_scalars=0, limit=16, flops=10**9, where=vmem
    ):
        return pl.pallas_call(
            kernel,
            in_specs=[smem] * len(scalars)
            + (where if isinstance(where, list) else [where] * len(inputs)),
            out_specs=[smem] * out_scalars + [vmem] * (len(outputs) - out_scalars),
            out_shape=[jax.ShapeDtypeStruct(shape, dtype) for shape, dtype in outputs],
            scratch_shapes=list(scratch),
            compiler_params=pltpu.CompilerParams(vmem_limit_bytes=int(limit * 2**20)),
            cost_estimate=pl.CostEstimate(
                flops=flops, bytes_accessed=2**20, transcendentals=0
            ),
        )(*scalars, *inputs)

    x_count = math.isqrt(seq_count)
    anywhere = pl.BlockSpec(memory_space=pltpu.HBM)
    along_x = list(range(1, x_count))
    along_y = list(range(x_count, seq_count, x_count))

    proj_own = proj_weight
    if halves == 2:
        (proj_own,) = call(
            half_kernel,
            [core],
            [proj_weight],
            [((head_width // 2, model_width), BF16)],
            scratch=[pltpu.SemaphoreType.DMA],
            where=anywhere,
        )
    proj_parts = {mask: send(proj_own, "seq", mask) for mask in along_y + along_x}

    slots, own, other = call(
        functools.partial(route_kernel, per_peer, piece_rows),
        [owner_place],
        [slot_owner, tokens],
        [((pieces_here,), jnp.int32)] + [((chips * block_rows, model_width), BF16)] * 2,
        scratch=[
            pltpu.SMEM((dp_count,), jnp.int32),
            pltpu.SMEM(slot_owner.shape, jnp.int32),
            pltpu.VMEM(tokens.shape, BF16),
            pltpu.SemaphoreType.DMA((2,)),
        ],
        out_scalars=1,
        limit=59,
        flops=3 * 10**10,
        where=anywhere,
    )
    payloads = call(
        functools.partial(merge_kernel, block_rows),
        [],
        [own, send(other, "dp", 1)],
        [((2 * block_rows, model_width), BF16)] * chips,
        scratch=[pltpu.VMEM(own.shape, BF16), pltpu.SemaphoreType.DMA],
        where=[anywhere, vmem],
    )
    arrived = [send(payload, "dp", 2 * mask) for mask, payload in enumerate(payloads)]

    def codes_of(group):
        return lambda rows, *places: row_codes(
            rows,
            group * (pieces_here // 2),
            per_peer,
            piece_rows,
            piece_rows * seq_count,
            *places,
        )

    weight = jnp.transpose(qkv_weight, (1, 2, 0)).reshape(3 * head_width, model_width)
    factors = jnp.transpose(modulation[0], (1, 0, 2))
    def project(blocks, flops=3 * 10**9):
        (projected,) = call(
            functools.partial(project_kernel, head_size),
            [],
            [weight, qk_gain] + blocks,
            [((3 * head_width, sum(block.shape[0] for block in blocks)), BF16)],
            flops=flops,
        )
        return projected

    near, far = [
        call(
            functools.partial(norm_kernel, clip_tokens, codes_of(group)),
            [owner_place, place],
            [clip_pieces, factors] + arrived[group * chips // 2 : (group + 1) * chips // 2],
            [((group_rows, model_width), BF16)],
            flops=(1 + 9 * group) * 10**9,
        )[0]
        for group in range(2)
    ]
    near, proj_parts = lax.optimization_barrier((near, proj_parts))
    near, proj_parts = lax.optimization_barrier((near, proj_parts))
    sides = {mask: send(near, "seq", mask) for mask in along_y + along_x}
    far, sides = lax.optimization_barrier((far, sides))
    far_blocks = [send(far, "seq", mask) for mask in range(seq_count)]
    halved = call(
        sides_kernel,
        [],
        [sides[mask] for mask in along_y + along_x],
        [((group_rows // 2, model_width), BF16)] * len(sides),
    )
    halved = dict(zip(along_y + along_x, halved))
    near_blocks = []
    for mask in range(seq_count):
        mx = mask % x_count
        my = mask - mx
        if mx > 0 and my > 0:
            near_blocks += [send(halved[my], "seq", mx), send(halved[mx], "seq", my)]
        else:
            near_blocks.append(sides[mask] if mask > 0 else near)
    stacked_near = project(near_blocks)
    def gather(first, *arrays):
        (gathered,) = call(
            functools.partial(gather_kernel, first, group_rows, per_peer, piece_rows),
            [owner_place, place, clip_pieces],
            list(arrays),
            [((clips_here, 3 * head_width, clip_tokens), BF16)],
            limit=16 if clip_tokens <= 256 else 48,
            flops=3 * 10**9,
        )
        return gathered

    gathered = gather(0, stacked_near)
    gathered, proj_parts = lax.optimization_barrier((gathered, proj_parts))
    early_blocks, late_blocks = far_blocks[: seq_count // 2], far_blocks[seq_count // 2 :]
    early_blocks, gathered = lax.optimization_barrier((early_blocks, gathered))
    gathered = gather(seq_count * group_rows, project(early_blocks), gathered)
    swapped = {mask: send(proj_parts[mask], "dp", 1) for mask in proj_parts} if halves == 2 else {}
    gathered, proj_parts = lax.optimization_barrier((gathered, proj_parts))
    for my in along_y:
        for mx in along_x:
            proj_parts[my + mx] = send(proj_parts[my], "seq", mx)
    late_blocks, gathered = lax.optimization_barrier((late_blocks, gathered))
    stacked_late, swapped = lax.optimization_barrier((project(late_blocks, 10**8), swapped))

    attended = call(
        functools.partial(attention_kernel, head_size, per_peer, piece_rows),
        [clip_length, owner_place, place, clip_pieces],
        [gathered, stacked_late],
        [((head_width, rows_here), BF16)] * seq_count,
        scratch=[pltpu.VMEM((head_width, seq_count * rows_here), F32)],
        limit=16 if clip_tokens <= 256 else 48,
        flops=10**8,
    )
    returned = [send(array, "seq", mask) for mask, array in enumerate(attended)]
    if halves == 2:
        _, late = lax.optimization_barrier((attended[0], proj_parts))
        swapped |= {mask: send(late[mask], "dp", 1) for mask in late if mask not in swapped}
    proj_parts = proj_parts | {seq_count + mask: swapped[mask] for mask in swapped}

    half_count = dp_count // 2
    far_masks = list(range(half_count, dp_count))
    outs = {mask: (index, 0) for index, mask in enumerate(far_masks)}
    for mask in range(2, half_count):
        outs[mask] = (half_count + mask // 2 - 1, mask % 2 * block_rows)
    outs[0], outs[1] = [(half_count + half_count // 2 - 1 + core_of, 0) for core_of in range(2)]

    def weights_of(masks):
        return [
            part
            for mask in masks
            for part in (
                [proj_weight]
                if mask == 0
                else [proj_parts[mask + half * seq_count] for half in range(halves)]
            )
        ]

    beside = [0] + along_x + along_y
    across = [mask for mask in range(seq_count) if mask not in beside]
    (partial,) = call(
        functools.partial(sides_output_kernel, beside, halves),
        [core],
        [returned[mask] for mask in beside] + weights_of(beside),
        [((rows_here, model_width), F32)],
        flops=10**10,
    )
    results = call(
        functools.partial(
            output_kernel,
            across,
            halves,
            clip_tokens,
            codes_of(0),
            [outs[mask] for mask in range(dp_count)],
        ),
        [core, clip_length, owner_place, place],
        [clip_pieces, factors, partial]
        + [returned[mask] for mask in across]
        + weights_of(across)
        + arrived,
        [((block_rows, model_width), BF16)] * half_count
        + [((2 * block_rows, model_width), BF16)] * (half_count // 2 - 1)
        + [((block_rows, model_width), BF16)] * 2,
        flops=3 * 10**9,
    )
    near_back = [
        send(block, "dp", 2 * (index + 1)) for index, block in enumerate(results[half_count:-2])
    ]
    far_back = [send(block, "dp", mask) for block, mask in zip(results, far_masks)]
    (crossing,) = call(
        functools.partial(crossing_kernel, block_rows),
        [],
        [results[-1]] + near_back,
        [((half_count // 2 * block_rows, model_width), BF16)],
    )
    crossed = send(crossing, "dp", 1)
    (far_back,) = call(
        stack_kernel,
        [],
        far_back,
        [((half_count * block_rows, model_width), BF16)],
        flops=10**10,
    )
    came_back = [far_back, crossed, results[-2]] + near_back
    places = {mask: (0, index * block_rows) for index, mask in enumerate(far_masks)}
    places[0] = (2, 0)
    for index in range(half_count // 2):
        places[2 * index + 1] = (1, index * block_rows)
        if index > 0:
            places[2 * index] = (2 + index, 0)
    (out,) = call(
        functools.partial(
            place_kernel, per_peer, piece_rows, [places[mask] for mask in range(dp_count)]
        ),
        [slots],
        came_back,
        [(tokens.shape, BF16)],
    )
    return out


def solution(mesh):
    return jax.shard_map(
        body,
        mesh=mesh,
        in_specs=(
            P("dp", None, "seq", None),
            P("dp", None),
            P("dp", None, None),
            P("dp", None),
            P("dp", None, None, None),
            P(None, None, "seq"),
            P(),
            P("seq", None),
        ),
        out_specs=P("dp", None, "seq", None),
        check_vma=False,
    )
```

```python
import functools
import math

import jax
import jax.numpy as jnp
from jax import lax
from jax.experimental import pallas as pl
from jax.experimental.pallas import tpu as pltpu
from jax.sharding import PartitionSpec as P

HEADS = 16
EPSILON = 1e-06
BF16 = jnp.bfloat16
F32 = jnp.float32


def send(array, axis, mask):
    if mask == 0:
        return array
    count = lax.axis_size(axis)
    return lax.ppermute(array, axis, [(i, i ^ mask) for i in range(count)])


def route_kernel(per_peer, piece_rows, place_ref, owner_hbm, token_hbm, *refs):
    slot_ref, own_ref, other_ref, filled_ref, owner_ref, token_ref, sems = refs
    peers = filled_ref.shape[0]
    owner_copy = pltpu.make_async_copy(owner_hbm, owner_ref, sems.at[0])
    token_copy = pltpu.make_async_copy(token_hbm, token_ref, sems.at[1])
    owner_copy.start()
    token_copy.start()
    for peer in range(peers):
        filled_ref[peer] = peer * per_peer
    owner_copy.wait()

    @pl.loop(0, peers * per_peer, unroll=8)
    def _(slot):
        peer = jnp.bitwise_xor(owner_ref[0, slot], place_ref[0])
        at = filled_ref[peer]
        filled_ref[peer] = at + 1
        slot_ref[at] = slot

    token_copy.wait()
    for peer in range(peers):
        ref = own_ref if peer % 2 == 0 else other_ref
        for m in range(per_peer):
            at = (peer // 2 * per_peer + m) * piece_rows
            ref[at : at + piece_rows, :] = token_ref[0, slot_ref[peer * per_peer + m]]


def merge_kernel(rows, own_hbm, other_ref, *refs):
    refs, own_ref, sem = refs[:-2], refs[-2], refs[-1]
    copy = pltpu.make_async_copy(own_hbm, own_ref, sem)
    copy.start()
    for index, ref in enumerate(refs):
        ref[rows:] = other_ref[index * rows : (index + 1) * rows]
    copy.wait()
    for index, ref in enumerate(refs):
        ref[:rows] = own_ref[index * rows : (index + 1) * rows]


def sides_kernel(*refs):
    count = len(refs) // 2
    for index in range(count):
        rows = refs[count + index].shape[0]
        start = 0 if index < count // 2 else rows
        refs[count + index][...] = refs[index][start : start + rows]


def half_kernel(core_ref, weight_hbm, out_ref, sem):
    rows = out_ref.shape[0]
    start = pl.multiple_of(core_ref[0] * rows, 16)
    copy = pltpu.make_async_copy(weight_hbm.at[pl.ds(start, rows), :], out_ref, sem)
    copy.start()
    copy.wait()


def place_kernel(per_peer, piece_rows, places, slot_ref, *refs):
    block_refs, out_ref = refs[:-1], refs[-1]
    for peer, (block, first) in enumerate(places):
        for m in range(per_peer):
            slot = slot_ref[peer * per_peer + m]
            start = first + m * piece_rows
            out_ref[0, slot] = block_refs[block][start : start + piece_rows, :]


def stack_kernel(*refs):
    start = 0
    for ref in refs[:-1]:
        refs[-1][start : start + ref.shape[0]] = ref[...]
        start += ref.shape[0]


def crossing_kernel(rows, own_ref, *refs):
    refs[-1][:rows] = own_ref[...]
    for index, ref in enumerate(refs[:-1]):
        refs[-1][(index + 1) * rows : (index + 2) * rows] = ref[rows:]


def arrival_of(piece, per_peer, owner_place):
    source = jnp.bitwise_xor(lax.div(piece, per_peer), owner_place)
    return source * per_peer + lax.rem(piece, per_peer)


def row_codes(rows, first_piece, per_peer, piece_rows, token_rows, owner_place, place, table):
    row = lax.broadcasted_iota(jnp.int32, (rows, 1), 0)
    arrival = arrival_of(first_piece + lax.div(row, piece_rows), per_peer, owner_place)
    lane = lax.broadcasted_iota(jnp.int32, (1, table.shape[1]), 1)
    found = jnp.zeros((rows, 1), jnp.int32)
    for clip in range(table.shape[0]):
        number = jnp.where(
            arrival == table[clip : clip + 1], lane + clip * table.shape[1], 0
        )
        found += jnp.sum(number, axis=1, keepdims=True)
    return found * token_rows + place * piece_rows + lax.rem(row, piece_rows)


def pick(clip, table):
    rows = jnp.broadcast_to(table[0:1], (clip.shape[0], table.shape[1]))
    for index in range(1, table.shape[0]):
        rows = jnp.where(clip == index, table[index : index + 1], rows)
    return rows


def norm_kernel(
    clip_tokens, codes_of, owner_ref, place_ref, table_ref, modulation_ref, *refs
):
    block_refs, out_ref = refs[:-1], refs[-1]
    code = codes_of(out_ref.shape[0], owner_ref[0], place_ref[0], table_ref[0])
    clip = lax.div(code, clip_tokens)
    rows = jnp.concatenate([ref[...].astype(F32) for ref in block_refs], axis=0)
    average = jnp.mean(rows, axis=-1, keepdims=True)
    centered = rows - average
    variance = jnp.mean(centered * centered, axis=-1, keepdims=True)
    normed = centered * lax.rsqrt(variance + EPSILON)
    shift = pick(clip, modulation_ref[0].astype(F32))
    scale = pick(clip, modulation_ref[1].astype(F32))
    out_ref[...] = (normed * (1.0 + scale) + shift).astype(BF16)


def project_kernel(head_size, weight_ref, gain_ref, *refs):
    hidden_refs, out_ref = refs[:-1], refs[-1]
    hidden = jnp.concatenate([ref[...] for ref in hidden_refs], axis=0)
    projected = lax.dot_general(
        weight_ref[...], hidden, (((1,), (1,)), ((), ())), preferred_element_type=F32
    )
    width = weight_ref.shape[0] // 3
    shape = (head_size, head_size)
    diagonal = lax.broadcasted_iota(jnp.int32, shape, 0) == lax.broadcasted_iota(
        jnp.int32, shape, 1
    )
    found = []
    for part in range(2):
        gain = jnp.sum(
            jnp.where(diagonal, gain_ref[part : part + 1, :], 0.0), axis=1, keepdims=True
        )
        for start in range(part * width, (part + 1) * width, head_size):
            value = projected[start : start + head_size]
            square = jnp.sum(value * value, axis=0, keepdims=True) * (1.0 / head_size)
            found.append(value * lax.rsqrt(square + EPSILON) * gain)
    found.append(projected[2 * width :])
    out_ref[...] = jnp.concatenate(found, axis=0).astype(BF16)


def token_codes(tokens, group_rows, per_peer, piece_rows, owner_ref, place_ref, table_ref):
    clips, per_clip = table_ref.shape[1:]
    seq_count = tokens // 2 // group_rows
    token = lax.broadcasted_iota(jnp.int32, (1, tokens), 1)
    row = lax.rem(token, group_rows)
    block = lax.div(token, group_rows)
    piece = lax.div(block, seq_count) * (group_rows // piece_rows) + lax.div(row, piece_rows)
    arrival = arrival_of(piece, per_peer, owner_ref[0])
    found = jnp.zeros_like(token)
    for clip in range(clips):
        for p in range(per_clip):
            found = jnp.where(arrival == table_ref[0, clip, p], clip * per_clip + p, found)
    source = jnp.bitwise_xor(lax.rem(block, seq_count), place_ref[0])
    return found * (piece_rows * seq_count) + source * piece_rows + lax.rem(row, piece_rows)


def gather_kernel(
    first, group_rows, per_peer, piece_rows, owner_ref, place_ref, table_ref, stacked_ref, *refs
):
    out_ref = refs[-1]
    clips, _, clip_tokens = out_ref.shape
    code = token_codes(
        clips * clip_tokens, group_rows, per_peer, piece_rows, owner_ref, place_ref, table_ref
    )[:, first : first + stacked_ref.shape[1]]
    position = lax.broadcasted_iota(jnp.int32, (clip_tokens, 1), 0)
    for clip in range(clips):
        chosen = jnp.where(code == position + clip * clip_tokens, 1.0, 0.0).astype(BF16)
        picked = lax.dot_general(
            stacked_ref[...], chosen, (((1,), (1,)), ((), ())), preferred_element_type=F32
        )
        if len(refs) > 1:
            picked += refs[0][clip].astype(F32)
        out_ref[clip] = picked.astype(BF16)


def attention_kernel(
    head_size, per_peer, piece_rows, length_ref, owner_ref, place_ref, table_ref, *refs
):
    early_ref, late_ref, out_refs = refs[0], refs[1], refs[2:]
    clips, features, clip_tokens = early_ref.shape
    width, tokens = features // 3, clips * clip_tokens
    seq_count = len(out_refs)
    group_rows = tokens // 2 // seq_count
    code = token_codes(
        tokens, group_rows, per_peer, piece_rows, owner_ref, place_ref, table_ref
    )
    position = lax.broadcasted_iota(jnp.int32, (clip_tokens, 1), 0)
    key = lax.broadcasted_iota(jnp.int32, (8, clip_tokens), 1)
    heads = range(0, width, head_size)
    scale = math.log2(math.e) / math.sqrt(head_size)
    attended, chosen_by_clip = [], []
    for clip in range(clips):
        chosen = jnp.where(code == position + clip * clip_tokens, 1.0, 0.0).astype(BF16)
        picked = early_ref[clip].astype(F32) + lax.dot_general(
            late_ref[...],
            chosen[:, tokens - late_ref.shape[1] :],
            (((1,), (1,)), ((), ())),
            preferred_element_type=F32,
        )
        in_clip = jnp.where(key < length_ref[0, clip], 1.0, 0.0)
        scores = [
            jnp.dot(
                jnp.transpose(picked[width + head : width + head + head_size]).astype(BF16),
                picked[head : head + head_size].astype(BF16),
                preferred_element_type=F32,
            )
            for head in heads
        ]
        unscaled = [jnp.exp2(score * scale).astype(BF16) for score in scores]
        outs = []
        for head, weights in zip(heads, unscaled):
            values = picked[2 * width + head : 2 * width + head + head_size] * in_clip[:1]
            values = jnp.concatenate([values, in_clip], axis=0).astype(BF16)
            summed = jnp.dot(values, weights, preferred_element_type=F32)
            outs.append(summed[:head_size] * (1.0 / summed[head_size : head_size + 1]))
        attended.append(jnp.concatenate(outs, axis=0).astype(BF16))
        chosen_by_clip.append(chosen)
    back = jnp.dot(
        jnp.concatenate(attended, axis=1),
        jnp.concatenate(chosen_by_clip, axis=0),
        preferred_element_type=F32,
    ).astype(BF16)
    for index, ref in enumerate(out_refs):
        for group in range(2):
            start = (group * seq_count + index) * group_rows
            ref[:, group * group_rows : (group + 1) * group_rows] = back[
                :, start : start + group_rows
            ]


def projected_rows(masks, halves, core_ref, head_refs, weight_refs):
    branch = None
    for mask, head_ref in zip(masks, head_refs):
        parts = 1 if mask == 0 else halves
        for part in range(parts):
            weight = weight_refs[part][...]
            head = head_ref[...]
            if parts == 2:
                rows = weight.shape[0]
                start = jnp.bitwise_xor(core_ref[0], part) * rows
                head = head_ref[pl.ds(pl.multiple_of(start, 16), rows), :]
            term = lax.dot_general(
                head, weight, (((0,), (0,)), ((), ())), preferred_element_type=F32
            )
            branch = term if branch is None else branch + term
        weight_refs = weight_refs[parts:]
    return branch


def sides_output_kernel(masks, halves, core_ref, *refs):
    refs[-1][...] = projected_rows(
        masks, halves, core_ref, refs[: len(masks)], refs[len(masks) : -1]
    )


def residual_kernel(
    clip_tokens, codes_of, length_ref, owner_ref, place_ref, table_ref, modulation_ref, *refs
):
    block_refs, (base_ref, gate_ref) = refs[:-2], refs[-2:]
    code = codes_of(base_ref.shape[0], owner_ref[0], place_ref[0], table_ref[0])
    clip = lax.div(code, clip_tokens)
    limit = jnp.zeros_like(code)
    for index in range(length_ref.shape[1]):
        limit = jnp.where(clip == index, length_ref[0, index], limit)
    kept = lax.rem(code, clip_tokens) < limit
    rows = jnp.concatenate([ref[...].astype(F32) for ref in block_refs], axis=0)
    base_ref[...] = jnp.where(kept, rows, 0.0).astype(BF16)
    gate = pick(clip, modulation_ref[2].astype(F32))
    gate_ref[...] = jnp.where(kept, gate, 0.0).astype(BF16)


def output_kernel(masks, halves, owner_masks, core_ref, base_ref, gate_ref, partial_ref, *refs):
    head_refs, refs = refs[: len(masks)], refs[len(masks) :]
    weight_refs, out_refs = refs[: len(masks) * halves], refs[len(masks) * halves :]
    branch = partial_ref[...] + projected_rows(masks, halves, core_ref, head_refs, weight_refs)
    result = base_ref[...].astype(F32) + gate_ref[...].astype(F32) * branch
    rows = result.shape[0] // len(owner_masks)
    for index, (out, first) in enumerate(owner_masks):
        out_refs[out][first : first + rows] = result[index * rows : (index + 1) * rows].astype(
            BF16
        )


def body(
    tokens, slot_owner, clip_pieces, clip_length, modulation, qkv_weight, qk_gain, proj_weight
):
    dp_count = lax.axis_size("dp")
    seq_count = lax.axis_size("seq")
    pieces_here = tokens.shape[1]
    piece_rows = tokens.shape[2]
    model_width = tokens.shape[3]
    per_peer = pieces_here // dp_count
    head_size = qk_gain.shape[1]
    heads = HEADS // seq_count
    head_width = heads * head_size
    clips_here, per_clip = clip_pieces.shape[1:]
    clip_tokens = per_clip * piece_rows * seq_count
    block_rows = per_peer * piece_rows
    rows_here = pieces_here * piece_rows
    group_rows = rows_here // 2
    chips = dp_count // 2
    owner_place = lax.axis_index("dp").astype(jnp.int32)
    place = lax.axis_index("seq").astype(jnp.int32).reshape(1)
    core = lax.rem(owner_place, 2).reshape(1)
    owner_place = owner_place.reshape(1)
    halves = 2 if heads % 2 == 0 else 1

    smem = pl.BlockSpec(memory_space=pltpu.SMEM)
    vmem = pl.BlockSpec(memory_space=pltpu.VMEM)

    def call(
        kernel, scalars, inputs, outputs, scratch=(), out_scalars=0, limit=16, flops=10**9, where=vmem
    ):
        return pl.pallas_call(
            kernel,
            in_specs=[smem] * len(scalars)
            + (where if isinstance(where, list) else [where] * len(inputs)),
            out_specs=[smem] * out_scalars + [vmem] * (len(outputs) - out_scalars),
            out_shape=[jax.ShapeDtypeStruct(shape, dtype) for shape, dtype in outputs],
            scratch_shapes=list(scratch),
            compiler_params=pltpu.CompilerParams(vmem_limit_bytes=int(limit * 2**20)),
            cost_estimate=pl.CostEstimate(
                flops=flops, bytes_accessed=2**20, transcendentals=0
            ),
        )(*scalars, *inputs)

    x_count = math.isqrt(seq_count)
    anywhere = pl.BlockSpec(memory_space=pltpu.HBM)
    along_x = list(range(1, x_count))
    along_y = list(range(x_count, seq_count, x_count))

    proj_own = proj_weight
    if halves == 2:
        (proj_own,) = call(
            half_kernel,
            [core],
            [proj_weight],
            [((head_width // 2, model_width), BF16)],
            scratch=[pltpu.SemaphoreType.DMA],
            where=anywhere,
        )
    proj_parts = {mask: send(proj_own, "seq", mask) for mask in along_y + along_x}

    slots, own, other = call(
        functools.partial(route_kernel, per_peer, piece_rows),
        [owner_place],
        [slot_owner, tokens],
        [((pieces_here,), jnp.int32)] + [((chips * block_rows, model_width), BF16)] * 2,
        scratch=[
            pltpu.SMEM((dp_count,), jnp.int32),
            pltpu.SMEM(slot_owner.shape, jnp.int32),
            pltpu.VMEM(tokens.shape, BF16),
            pltpu.SemaphoreType.DMA((2,)),
        ],
        out_scalars=1,
        limit=59,
        flops=3 * 10**10,
        where=anywhere,
    )
    payloads = call(
        functools.partial(merge_kernel, block_rows),
        [],
        [own, send(other, "dp", 1)],
        [((2 * block_rows, model_width), BF16)] * chips,
        scratch=[pltpu.VMEM(own.shape, BF16), pltpu.SemaphoreType.DMA],
        where=[anywhere, vmem],
    )
    arrived = [send(payload, "dp", 2 * mask) for mask, payload in enumerate(payloads)]

    def codes_of(group):
        return lambda rows, *places: row_codes(
            rows,
            group * (pieces_here // 2),
            per_peer,
            piece_rows,
            piece_rows * seq_count,
            *places,
        )

    weight = jnp.transpose(qkv_weight, (1, 2, 0)).reshape(3 * head_width, model_width)
    factors = jnp.transpose(modulation[0], (1, 0, 2))
    def project(blocks, flops=3 * 10**9):
        (projected,) = call(
            functools.partial(project_kernel, head_size),
            [],
            [weight, qk_gain] + blocks,
            [((3 * head_width, sum(block.shape[0] for block in blocks)), BF16)],
            flops=flops,
        )
        return projected

    near, far = [
        call(
            functools.partial(norm_kernel, clip_tokens, codes_of(group)),
            [owner_place, place],
            [clip_pieces, factors] + arrived[group * chips // 2 : (group + 1) * chips // 2],
            [((group_rows, model_width), BF16)],
            flops=(1 + 9 * group) * 10**9,
        )[0]
        for group in range(2)
    ]
    near, proj_parts = lax.optimization_barrier((near, proj_parts))
    near, proj_parts = lax.optimization_barrier((near, proj_parts))
    sides = {mask: send(near, "seq", mask) for mask in along_y + along_x}
    far, sides = lax.optimization_barrier((far, sides))
    far_blocks = [send(far, "seq", mask) for mask in range(seq_count)]
    halved = call(
        sides_kernel,
        [],
        [sides[mask] for mask in along_y + along_x],
        [((group_rows // 2, model_width), BF16)] * len(sides),
    )
    halved = dict(zip(along_y + along_x, halved))
    near_blocks = []
    for mask in range(seq_count):
        mx = mask % x_count
        my = mask - mx
        if mx > 0 and my > 0:
            near_blocks += [send(halved[my], "seq", mx), send(halved[mx], "seq", my)]
        else:
            near_blocks.append(sides[mask] if mask > 0 else near)
    stacked_near = project(near_blocks)
    def gather(first, *arrays):
        (gathered,) = call(
            functools.partial(gather_kernel, first, group_rows, per_peer, piece_rows),
            [owner_place, place, clip_pieces],
            list(arrays),
            [((clips_here, 3 * head_width, clip_tokens), BF16)],
            limit=16 if clip_tokens <= 256 else 48,
            flops=3 * 10**9,
        )
        return gathered

    gathered = gather(0, stacked_near)
    gathered, proj_parts = lax.optimization_barrier((gathered, proj_parts))
    early_blocks, late_blocks = far_blocks[: seq_count // 2], far_blocks[seq_count // 2 :]
    residual = call(
        functools.partial(residual_kernel, clip_tokens, codes_of(0)),
        [clip_length, owner_place, place],
        [clip_pieces, factors] + arrived,
        [((rows_here, model_width), BF16)] * 2,
    )
    early_blocks, gathered, residual = lax.optimization_barrier(
        (early_blocks, gathered, list(residual))
    )
    gathered = gather(seq_count * group_rows, project(early_blocks), gathered)
    swapped = {mask: send(proj_parts[mask], "dp", 1) for mask in proj_parts} if halves == 2 else {}
    gathered, proj_parts = lax.optimization_barrier((gathered, proj_parts))
    for my in along_y:
        for mx in along_x:
            proj_parts[my + mx] = send(proj_parts[my], "seq", mx)
    late_blocks, gathered = lax.optimization_barrier((late_blocks, gathered))
    stacked_late, swapped = lax.optimization_barrier((project(late_blocks, 10**8), swapped))

    attended = call(
        functools.partial(attention_kernel, head_size, per_peer, piece_rows),
        [clip_length, owner_place, place, clip_pieces],
        [gathered, stacked_late],
        [((head_width, rows_here), BF16)] * seq_count,
        limit=16 if clip_tokens <= 256 else 48,
        flops=10**8,
    )
    returned = [send(array, "seq", mask) for mask, array in enumerate(attended)]
    if halves == 2:
        _, late = lax.optimization_barrier((attended[0], proj_parts))
        swapped |= {mask: send(late[mask], "dp", 1) for mask in late if mask not in swapped}
    proj_parts = proj_parts | {seq_count + mask: swapped[mask] for mask in swapped}

    half_count = dp_count // 2
    far_masks = list(range(half_count, dp_count))
    outs = {mask: (index, 0) for index, mask in enumerate(far_masks)}
    for mask in range(2, half_count):
        outs[mask] = (half_count + mask // 2 - 1, mask % 2 * block_rows)
    outs[0], outs[1] = [(half_count + half_count // 2 - 1 + core_of, 0) for core_of in range(2)]

    def weights_of(masks):
        return [
            part
            for mask in masks
            for part in (
                [proj_weight]
                if mask == 0
                else [proj_parts[mask + half * seq_count] for half in range(halves)]
            )
        ]

    beside = [0] + along_x + along_y
    across = [mask for mask in range(seq_count) if mask not in beside]
    (partial,) = call(
        functools.partial(sides_output_kernel, beside, halves),
        [core],
        [returned[mask] for mask in beside] + weights_of(beside),
        [((rows_here, model_width), F32)],
        flops=10**10,
    )
    results = call(
        functools.partial(output_kernel, across, halves, [outs[mask] for mask in range(dp_count)]),
        [core],
        residual + [partial] + [returned[mask] for mask in across] + weights_of(across),
        [((block_rows, model_width), BF16)] * half_count
        + [((2 * block_rows, model_width), BF16)] * (half_count // 2 - 1)
        + [((block_rows, model_width), BF16)] * 2,
        flops=3 * 10**9,
    )
    near_back = [
        send(block, "dp", 2 * (index + 1)) for index, block in enumerate(results[half_count:-2])
    ]
    far_back = [send(block, "dp", mask) for block, mask in zip(results, far_masks)]
    (crossing,) = call(
        functools.partial(crossing_kernel, block_rows),
        [],
        [results[-1]] + near_back,
        [((half_count // 2 * block_rows, model_width), BF16)],
    )
    crossed = send(crossing, "dp", 1)
    (far_back,) = call(
        stack_kernel,
        [],
        far_back,
        [((half_count * block_rows, model_width), BF16)],
        flops=10**10,
    )
    came_back = [far_back, crossed, results[-2]] + near_back
    places = {mask: (0, index * block_rows) for index, mask in enumerate(far_masks)}
    places[0] = (2, 0)
    for index in range(half_count // 2):
        places[2 * index + 1] = (1, index * block_rows)
        if index > 0:
            places[2 * index] = (2 + index, 0)
    (out,) = call(
        functools.partial(
            place_kernel, per_peer, piece_rows, [places[mask] for mask in range(dp_count)]
        ),
        [slots],
        came_back,
        [(tokens.shape, BF16)],
    )
    return out


def solution(mesh):
    return jax.shard_map(
        body,
        mesh=mesh,
        in_specs=(
            P("dp", None, "seq", None),
            P("dp", None),
            P("dp", None, None),
            P("dp", None),
            P("dp", None, None, None),
            P(None, None, "seq"),
            P(),
            P("seq", None),
        ),
        out_specs=P("dp", None, "seq", None),
        check_vma=False,
    )
```

```python
import functools
import math

import jax
import jax.numpy as jnp
from jax import lax
from jax.experimental import pallas as pl
from jax.experimental.pallas import tpu as pltpu
from jax.sharding import PartitionSpec as P

HEADS = 16
EPSILON = 1e-06
BF16 = jnp.bfloat16
F32 = jnp.float32


def send(array, axis, mask):
    if mask == 0:
        return array
    count = lax.axis_size(axis)
    return lax.ppermute(array, axis, [(i, i ^ mask) for i in range(count)])


def route_kernel(per_peer, piece_rows, place_ref, owner_hbm, token_hbm, *refs):
    slot_ref, own_ref, other_ref, filled_ref, owner_ref, token_ref, sems = refs
    peers = filled_ref.shape[0]
    owner_copy = pltpu.make_async_copy(owner_hbm, owner_ref, sems.at[0])
    token_copy = pltpu.make_async_copy(token_hbm, token_ref, sems.at[1])
    owner_copy.start()
    token_copy.start()
    for peer in range(peers):
        filled_ref[peer] = peer * per_peer
    owner_copy.wait()

    @pl.loop(0, peers * per_peer, unroll=8)
    def _(slot):
        peer = jnp.bitwise_xor(owner_ref[0, slot], place_ref[0])
        at = filled_ref[peer]
        filled_ref[peer] = at + 1
        slot_ref[at] = slot

    token_copy.wait()
    for peer in range(peers):
        ref = own_ref if peer % 2 == 0 else other_ref
        for m in range(per_peer):
            at = (peer // 2 * per_peer + m) * piece_rows
            ref[at : at + piece_rows, :] = token_ref[0, slot_ref[peer * per_peer + m]]


def merge_kernel(rows, own_hbm, other_ref, *refs):
    refs, own_ref, sem = refs[:-2], refs[-2], refs[-1]
    copy = pltpu.make_async_copy(own_hbm, own_ref, sem)
    copy.start()
    for index, ref in enumerate(refs):
        ref[rows:] = other_ref[index * rows : (index + 1) * rows]
    copy.wait()
    for index, ref in enumerate(refs):
        ref[:rows] = own_ref[index * rows : (index + 1) * rows]


def sides_kernel(*refs):
    count = len(refs) // 2
    for index in range(count):
        rows = refs[count + index].shape[0]
        start = 0 if index < count // 2 else rows
        refs[count + index][...] = refs[index][start : start + rows]


def half_kernel(core_ref, weight_hbm, out_ref, sem):
    rows = out_ref.shape[0]
    start = pl.multiple_of(core_ref[0] * rows, 16)
    copy = pltpu.make_async_copy(weight_hbm.at[pl.ds(start, rows), :], out_ref, sem)
    copy.start()
    copy.wait()


def place_kernel(per_peer, piece_rows, places, slot_ref, *refs):
    block_refs, out_ref = refs[:-1], refs[-1]
    for peer, (block, first) in enumerate(places):
        for m in range(per_peer):
            slot = slot_ref[peer * per_peer + m]
            start = first + m * piece_rows
            out_ref[0, slot] = block_refs[block][start : start + piece_rows, :]


def stack_kernel(*refs):
    start = 0
    for ref in refs[:-1]:
        refs[-1][start : start + ref.shape[0]] = ref[...]
        start += ref.shape[0]


def crossing_kernel(rows, own_ref, *refs):
    refs[-1][:rows] = own_ref[...]
    for index, ref in enumerate(refs[:-1]):
        refs[-1][(index + 1) * rows : (index + 2) * rows] = ref[rows:]


def arrival_of(piece, per_peer, owner_place):
    source = jnp.bitwise_xor(lax.div(piece, per_peer), owner_place)
    return source * per_peer + lax.rem(piece, per_peer)


def row_codes(rows, first_piece, per_peer, piece_rows, token_rows, owner_place, place, table):
    row = lax.broadcasted_iota(jnp.int32, (rows, 1), 0)
    arrival = arrival_of(first_piece + lax.div(row, piece_rows), per_peer, owner_place)
    lane = lax.broadcasted_iota(jnp.int32, (1, table.shape[1]), 1)
    found = jnp.zeros((rows, 1), jnp.int32)
    for clip in range(table.shape[0]):
        number = jnp.where(
            arrival == table[clip : clip + 1], lane + clip * table.shape[1], 0
        )
        found += jnp.sum(number, axis=1, keepdims=True)
    return found * token_rows + place * piece_rows + lax.rem(row, piece_rows)


def pick(clip, table):
    rows = jnp.broadcast_to(table[0:1], (clip.shape[0], table.shape[1]))
    for index in range(1, table.shape[0]):
        rows = jnp.where(clip == index, table[index : index + 1], rows)
    return rows


def norm_kernel(
    clip_tokens, codes_of, owner_ref, place_ref, table_ref, modulation_ref, *refs
):
    block_refs, out_ref = refs[:-1], refs[-1]
    code = codes_of(out_ref.shape[0], owner_ref[0], place_ref[0], table_ref[0])
    clip = lax.div(code, clip_tokens)
    rows = jnp.concatenate([ref[...].astype(F32) for ref in block_refs], axis=0)
    average = jnp.mean(rows, axis=-1, keepdims=True)
    centered = rows - average
    variance = jnp.mean(centered * centered, axis=-1, keepdims=True)
    normed = centered * lax.rsqrt(variance + EPSILON)
    shift = pick(clip, modulation_ref[0].astype(F32))
    scale = pick(clip, modulation_ref[1].astype(F32))
    out_ref[...] = (normed * (1.0 + scale) + shift).astype(BF16)


def project_kernel(head_size, weight_ref, gain_ref, *refs):
    hidden_refs, out_ref = refs[:-1], refs[-1]
    hidden = jnp.concatenate([ref[...] for ref in hidden_refs], axis=0)
    projected = lax.dot_general(
        weight_ref[...], hidden, (((1,), (1,)), ((), ())), preferred_element_type=F32
    )
    width = weight_ref.shape[0] // 3
    shape = (head_size, head_size)
    diagonal = lax.broadcasted_iota(jnp.int32, shape, 0) == lax.broadcasted_iota(
        jnp.int32, shape, 1
    )
    found = []
    for part in range(2):
        gain = jnp.sum(
            jnp.where(diagonal, gain_ref[part : part + 1, :], 0.0), axis=1, keepdims=True
        )
        for start in range(part * width, (part + 1) * width, head_size):
            value = projected[start : start + head_size]
            square = jnp.sum(value * value, axis=0, keepdims=True) * (1.0 / head_size)
            found.append(value * lax.rsqrt(square + EPSILON) * gain)
    found.append(projected[2 * width :])
    out_ref[...] = jnp.concatenate(found, axis=0).astype(BF16)


def token_codes(tokens, group_rows, per_peer, piece_rows, owner_ref, place_ref, table_ref):
    clips, per_clip = table_ref.shape[1:]
    seq_count = tokens // 2 // group_rows
    token = lax.broadcasted_iota(jnp.int32, (1, tokens), 1)
    row = lax.rem(token, group_rows)
    block = lax.div(token, group_rows)
    piece = lax.div(block, seq_count) * (group_rows // piece_rows) + lax.div(row, piece_rows)
    arrival = arrival_of(piece, per_peer, owner_ref[0])
    found = jnp.zeros_like(token)
    for clip in range(clips):
        for p in range(per_clip):
            found = jnp.where(arrival == table_ref[0, clip, p], clip * per_clip + p, found)
    source = jnp.bitwise_xor(lax.rem(block, seq_count), place_ref[0])
    return found * (piece_rows * seq_count) + source * piece_rows + lax.rem(row, piece_rows)


def gather_kernel(
    first, group_rows, per_peer, piece_rows, owner_ref, place_ref, table_ref, stacked_ref, *refs
):
    out_ref = refs[-1]
    clips, _, clip_tokens = out_ref.shape
    code = token_codes(
        clips * clip_tokens, group_rows, per_peer, piece_rows, owner_ref, place_ref, table_ref
    )[:, first : first + stacked_ref.shape[1]]
    position = lax.broadcasted_iota(jnp.int32, (clip_tokens, 1), 0)
    for clip in range(clips):
        chosen = jnp.where(code == position + clip * clip_tokens, 1.0, 0.0).astype(BF16)
        picked = lax.dot_general(
            stacked_ref[...], chosen, (((1,), (1,)), ((), ())), preferred_element_type=F32
        )
        if len(refs) > 1:
            picked += refs[0][clip].astype(F32)
        out_ref[clip] = picked.astype(BF16)


def attention_kernel(
    head_size, per_peer, piece_rows, length_ref, owner_ref, place_ref, table_ref, *refs
):
    early_ref, late_ref, out_refs = refs[0], refs[1], refs[2:]
    clips, features, clip_tokens = early_ref.shape
    width, tokens = features // 3, clips * clip_tokens
    seq_count = len(out_refs)
    group_rows = tokens // 2 // seq_count
    code = token_codes(
        tokens, group_rows, per_peer, piece_rows, owner_ref, place_ref, table_ref
    )
    position = lax.broadcasted_iota(jnp.int32, (clip_tokens, 1), 0)
    key = lax.broadcasted_iota(jnp.int32, (8, clip_tokens), 1)
    heads = range(0, width, head_size)
    scale = math.log2(math.e) / math.sqrt(head_size)
    attended, chosen_by_clip = [], []
    for clip in range(clips):
        chosen = jnp.where(code == position + clip * clip_tokens, 1.0, 0.0).astype(BF16)
        picked = early_ref[clip].astype(F32) + lax.dot_general(
            late_ref[...],
            chosen[:, tokens - late_ref.shape[1] :],
            (((1,), (1,)), ((), ())),
            preferred_element_type=F32,
        )
        in_clip = jnp.where(key < length_ref[0, clip], 1.0, 0.0)
        scores = [
            jnp.dot(
                jnp.transpose(picked[width + head : width + head + head_size]).astype(BF16),
                picked[head : head + head_size].astype(BF16),
                preferred_element_type=F32,
            )
            for head in heads
        ]
        unscaled = [jnp.exp2(score * scale).astype(BF16) for score in scores]
        outs = []
        for head, weights in zip(heads, unscaled):
            values = picked[2 * width + head : 2 * width + head + head_size] * in_clip[:1]
            values = jnp.concatenate([values, in_clip], axis=0).astype(BF16)
            summed = jnp.dot(values, weights, preferred_element_type=F32)
            outs.append(summed[:head_size] * (1.0 / summed[head_size : head_size + 1]))
        attended.append(jnp.concatenate(outs, axis=0).astype(BF16))
        chosen_by_clip.append(chosen)
    back = jnp.dot(
        jnp.concatenate(attended, axis=1),
        jnp.concatenate(chosen_by_clip, axis=0),
        preferred_element_type=F32,
    ).astype(BF16)
    for index, ref in enumerate(out_refs):
        for group in range(2):
            start = (group * seq_count + index) * group_rows
            ref[:, group * group_rows : (group + 1) * group_rows] = back[
                :, start : start + group_rows
            ]


def projected_rows(masks, halves, core_ref, head_refs, weight_refs):
    branch = None
    for mask, head_ref in zip(masks, head_refs):
        parts = 1 if mask == 0 else halves
        for part in range(parts):
            weight = weight_refs[part][...]
            head = head_ref[...]
            if parts == 2:
                rows = weight.shape[0]
                start = jnp.bitwise_xor(core_ref[0], part) * rows
                head = head_ref[pl.ds(pl.multiple_of(start, 16), rows), :]
            term = lax.dot_general(
                head, weight, (((0,), (0,)), ((), ())), preferred_element_type=F32
            )
            branch = term if branch is None else branch + term
        weight_refs = weight_refs[parts:]
    return branch


def sides_output_kernel(masks, halves, core_ref, *refs):
    refs[-1][...] = projected_rows(
        masks, halves, core_ref, refs[: len(masks)], refs[len(masks) : -1]
    )


def residual_kernel(
    clip_tokens, codes_of, length_ref, owner_ref, place_ref, table_ref, modulation_ref, *refs
):
    block_refs, (base_ref, gate_ref) = refs[:-2], refs[-2:]
    code = codes_of(base_ref.shape[0], owner_ref[0], place_ref[0], table_ref[0])
    clip = lax.div(code, clip_tokens)
    limit = jnp.zeros_like(code)
    for index in range(length_ref.shape[1]):
        limit = jnp.where(clip == index, length_ref[0, index], limit)
    kept = lax.rem(code, clip_tokens) < limit
    rows = jnp.concatenate([ref[...].astype(F32) for ref in block_refs], axis=0)
    base_ref[...] = jnp.where(kept, rows, 0.0).astype(BF16)
    gate = pick(clip, modulation_ref[2].astype(F32))
    gate_ref[...] = jnp.where(kept, gate, 0.0).astype(BF16)


def output_kernel(masks, halves, owner_masks, core_ref, base_ref, gate_ref, partial_ref, *refs):
    head_refs, refs = refs[: len(masks)], refs[len(masks) :]
    weight_refs, out_refs = refs[: len(masks) * halves], refs[len(masks) * halves :]
    branch = partial_ref[...] + projected_rows(masks, halves, core_ref, head_refs, weight_refs)
    result = base_ref[...].astype(F32) + gate_ref[...].astype(F32) * branch
    rows = result.shape[0] // len(owner_masks)
    for index, (out, first) in enumerate(owner_masks):
        out_refs[out][first : first + rows] = result[index * rows : (index + 1) * rows].astype(
            BF16
        )


def body(
    tokens, slot_owner, clip_pieces, clip_length, modulation, qkv_weight, qk_gain, proj_weight
):
    dp_count = lax.axis_size("dp")
    seq_count = lax.axis_size("seq")
    pieces_here = tokens.shape[1]
    piece_rows = tokens.shape[2]
    model_width = tokens.shape[3]
    per_peer = pieces_here // dp_count
    head_size = qk_gain.shape[1]
    heads = HEADS // seq_count
    head_width = heads * head_size
    clips_here, per_clip = clip_pieces.shape[1:]
    clip_tokens = per_clip * piece_rows * seq_count
    block_rows = per_peer * piece_rows
    rows_here = pieces_here * piece_rows
    group_rows = rows_here // 2
    chips = dp_count // 2
    owner_place = lax.axis_index("dp").astype(jnp.int32)
    place = lax.axis_index("seq").astype(jnp.int32).reshape(1)
    core = lax.rem(owner_place, 2).reshape(1)
    owner_place = owner_place.reshape(1)
    halves = 2 if heads % 2 == 0 else 1

    smem = pl.BlockSpec(memory_space=pltpu.SMEM)
    vmem = pl.BlockSpec(memory_space=pltpu.VMEM)

    def call(
        kernel, scalars, inputs, outputs, scratch=(), out_scalars=0, limit=16, flops=10**9, where=vmem
    ):
        return pl.pallas_call(
            kernel,
            in_specs=[smem] * len(scalars)
            + (where if isinstance(where, list) else [where] * len(inputs)),
            out_specs=[smem] * out_scalars + [vmem] * (len(outputs) - out_scalars),
            out_shape=[jax.ShapeDtypeStruct(shape, dtype) for shape, dtype in outputs],
            scratch_shapes=list(scratch),
            compiler_params=pltpu.CompilerParams(vmem_limit_bytes=int(limit * 2**20)),
            cost_estimate=pl.CostEstimate(
                flops=flops, bytes_accessed=2**20, transcendentals=0
            ),
        )(*scalars, *inputs)

    x_count = math.isqrt(seq_count)
    anywhere = pl.BlockSpec(memory_space=pltpu.HBM)
    along_x = list(range(1, x_count))
    along_y = list(range(x_count, seq_count, x_count))

    proj_own = proj_weight
    if halves == 2:
        (proj_own,) = call(
            half_kernel,
            [core],
            [proj_weight],
            [((head_width // 2, model_width), BF16)],
            scratch=[pltpu.SemaphoreType.DMA],
            where=anywhere,
        )
    proj_parts = {mask: send(proj_own, "seq", mask) for mask in along_y + along_x}

    slots, own, other = call(
        functools.partial(route_kernel, per_peer, piece_rows),
        [owner_place],
        [slot_owner, tokens],
        [((pieces_here,), jnp.int32)] + [((chips * block_rows, model_width), BF16)] * 2,
        scratch=[
            pltpu.SMEM((dp_count,), jnp.int32),
            pltpu.SMEM(slot_owner.shape, jnp.int32),
            pltpu.VMEM(tokens.shape, BF16),
            pltpu.SemaphoreType.DMA((2,)),
        ],
        out_scalars=1,
        limit=59,
        flops=3 * 10**10,
        where=anywhere,
    )
    payloads = call(
        functools.partial(merge_kernel, block_rows),
        [],
        [own, send(other, "dp", 1)],
        [((2 * block_rows, model_width), BF16)] * chips,
        scratch=[pltpu.VMEM(own.shape, BF16), pltpu.SemaphoreType.DMA],
        where=[anywhere, vmem],
    )
    arrived = [send(payload, "dp", 2 * mask) for mask, payload in enumerate(payloads)]

    def codes_of(group):
        return lambda rows, *places: row_codes(
            rows,
            group * (pieces_here // 2),
            per_peer,
            piece_rows,
            piece_rows * seq_count,
            *places,
        )

    weight = jnp.transpose(qkv_weight, (1, 2, 0)).reshape(3 * head_width, model_width)
    factors = jnp.transpose(modulation[0], (1, 0, 2))
    def project(blocks, flops=3 * 10**9):
        (projected,) = call(
            functools.partial(project_kernel, head_size),
            [],
            [weight, qk_gain] + blocks,
            [((3 * head_width, sum(block.shape[0] for block in blocks)), BF16)],
            flops=flops,
        )
        return projected

    near, far = [
        call(
            functools.partial(norm_kernel, clip_tokens, codes_of(group)),
            [owner_place, place],
            [clip_pieces, factors] + arrived[group * chips // 2 : (group + 1) * chips // 2],
            [((group_rows, model_width), BF16)],
            flops=(1 + 9 * group) * 10**9,
        )[0]
        for group in range(2)
    ]
    near, proj_parts = lax.optimization_barrier((near, proj_parts))
    near, proj_parts = lax.optimization_barrier((near, proj_parts))
    sides = {mask: send(near, "seq", mask) for mask in along_y + along_x}
    far, sides = lax.optimization_barrier((far, sides))
    far_blocks = [send(far, "seq", mask) for mask in range(seq_count)]
    halved = call(
        sides_kernel,
        [],
        [sides[mask] for mask in along_y + along_x],
        [((group_rows // 2, model_width), BF16)] * len(sides),
    )
    halved = dict(zip(along_y + along_x, halved))
    near_blocks = []
    for mask in range(seq_count):
        mx = mask % x_count
        my = mask - mx
        if mx > 0 and my > 0:
            near_blocks += [send(halved[my], "seq", mx), send(halved[mx], "seq", my)]
        else:
            near_blocks.append(sides[mask] if mask > 0 else near)
    stacked_near = project(near_blocks)
    def gather(first, *arrays):
        (gathered,) = call(
            functools.partial(gather_kernel, first, group_rows, per_peer, piece_rows),
            [owner_place, place, clip_pieces],
            list(arrays),
            [((clips_here, 3 * head_width, clip_tokens), BF16)],
            limit=16 if clip_tokens <= 256 else 48,
            flops=3 * 10**9,
        )
        return gathered

    gathered = gather(0, stacked_near)
    gathered, proj_parts, settled = lax.optimization_barrier((gathered, proj_parts, arrived))
    early_blocks, late_blocks = far_blocks[: seq_count // 2], far_blocks[seq_count // 2 :]
    residual = call(
        functools.partial(residual_kernel, clip_tokens, codes_of(0)),
        [clip_length, owner_place, place],
        [clip_pieces, factors] + settled,
        [((rows_here, model_width), BF16)] * 2,
    )
    early_blocks, gathered, residual = lax.optimization_barrier(
        (early_blocks, gathered, list(residual))
    )
    gathered = gather(seq_count * group_rows, project(early_blocks), gathered)
    swapped = {mask: send(proj_parts[mask], "dp", 1) for mask in proj_parts} if halves == 2 else {}
    gathered, proj_parts = lax.optimization_barrier((gathered, proj_parts))
    for my in along_y:
        for mx in along_x:
            proj_parts[my + mx] = send(proj_parts[my], "seq", mx)
    late_blocks, gathered = lax.optimization_barrier((late_blocks, gathered))
    stacked_late, swapped = lax.optimization_barrier((project(late_blocks, 10**8), swapped))

    attended = call(
        functools.partial(attention_kernel, head_size, per_peer, piece_rows),
        [clip_length, owner_place, place, clip_pieces],
        [gathered, stacked_late],
        [((head_width, rows_here), BF16)] * seq_count,
        limit=16 if clip_tokens <= 256 else 48,
        flops=10**8,
    )
    returned = [send(array, "seq", mask) for mask, array in enumerate(attended)]
    if halves == 2:
        _, late = lax.optimization_barrier((attended[0], proj_parts))
        swapped |= {mask: send(late[mask], "dp", 1) for mask in late if mask not in swapped}
    proj_parts = proj_parts | {seq_count + mask: swapped[mask] for mask in swapped}

    half_count = dp_count // 2
    far_masks = list(range(half_count, dp_count))
    outs = {mask: (index, 0) for index, mask in enumerate(far_masks)}
    for mask in range(2, half_count):
        outs[mask] = (half_count + mask // 2 - 1, mask % 2 * block_rows)
    outs[0], outs[1] = [(half_count + half_count // 2 - 1 + core_of, 0) for core_of in range(2)]

    def weights_of(masks):
        return [
            part
            for mask in masks
            for part in (
                [proj_weight]
                if mask == 0
                else [proj_parts[mask + half * seq_count] for half in range(halves)]
            )
        ]

    beside = [0] + along_x + along_y
    across = [mask for mask in range(seq_count) if mask not in beside]
    (partial,) = call(
        functools.partial(sides_output_kernel, beside, halves),
        [core],
        [returned[mask] for mask in beside] + weights_of(beside),
        [((rows_here, model_width), F32)],
        flops=10**10,
    )
    results = call(
        functools.partial(output_kernel, across, halves, [outs[mask] for mask in range(dp_count)]),
        [core],
        residual + [partial] + [returned[mask] for mask in across] + weights_of(across),
        [((block_rows, model_width), BF16)] * half_count
        + [((2 * block_rows, model_width), BF16)] * (half_count // 2 - 1)
        + [((block_rows, model_width), BF16)] * 2,
        flops=3 * 10**9,
    )
    near_back = [
        send(block, "dp", 2 * (index + 1)) for index, block in enumerate(results[half_count:-2])
    ]
    far_back = [send(block, "dp", mask) for block, mask in zip(results, far_masks)]
    (crossing,) = call(
        functools.partial(crossing_kernel, block_rows),
        [],
        [results[-1]] + near_back,
        [((half_count // 2 * block_rows, model_width), BF16)],
    )
    crossed = send(crossing, "dp", 1)
    (far_back,) = call(
        stack_kernel,
        [],
        far_back,
        [((half_count * block_rows, model_width), BF16)],
        flops=10**10,
    )
    came_back = [far_back, crossed, results[-2]] + near_back
    places = {mask: (0, index * block_rows) for index, mask in enumerate(far_masks)}
    places[0] = (2, 0)
    for index in range(half_count // 2):
        places[2 * index + 1] = (1, index * block_rows)
        if index > 0:
            places[2 * index] = (2 + index, 0)
    (out,) = call(
        functools.partial(
            place_kernel, per_peer, piece_rows, [places[mask] for mask in range(dp_count)]
        ),
        [slots],
        came_back,
        [(tokens.shape, BF16)],
    )
    return out


def solution(mesh):
    return jax.shard_map(
        body,
        mesh=mesh,
        in_specs=(
            P("dp", None, "seq", None),
            P("dp", None),
            P("dp", None, None),
            P("dp", None),
            P("dp", None, None, None),
            P(None, None, "seq"),
            P(),
            P("seq", None),
        ),
        out_specs=P("dp", None, "seq", None),
        check_vma=False,
    )
```

```python
import functools
import math

import jax
import jax.numpy as jnp
from jax import lax
from jax.experimental import pallas as pl
from jax.experimental.pallas import tpu as pltpu
from jax.sharding import PartitionSpec as P

HEADS = 16
EPSILON = 1e-06
BF16 = jnp.bfloat16
F32 = jnp.float32


def send(array, axis, mask):
    if mask == 0:
        return array
    count = lax.axis_size(axis)
    return lax.ppermute(array, axis, [(i, i ^ mask) for i in range(count)])


def route_kernel(per_peer, piece_rows, place_ref, owner_hbm, token_hbm, *refs):
    slot_ref, own_ref, other_ref, filled_ref, owner_ref, token_ref, sems = refs
    peers = filled_ref.shape[0]
    owner_copy = pltpu.make_async_copy(owner_hbm, owner_ref, sems.at[0])
    token_copy = pltpu.make_async_copy(token_hbm, token_ref, sems.at[1])
    owner_copy.start()
    token_copy.start()
    for peer in range(peers):
        filled_ref[peer] = peer * per_peer
    owner_copy.wait()

    @pl.loop(0, peers * per_peer, unroll=8)
    def _(slot):
        peer = jnp.bitwise_xor(owner_ref[0, slot], place_ref[0])
        at = filled_ref[peer]
        filled_ref[peer] = at + 1
        slot_ref[at] = slot

    token_copy.wait()
    for peer in range(peers):
        ref = own_ref if peer % 2 == 0 else other_ref
        for m in range(per_peer):
            at = (peer // 2 * per_peer + m) * piece_rows
            ref[at : at + piece_rows, :] = token_ref[0, slot_ref[peer * per_peer + m]]


def merge_kernel(rows, own_hbm, other_ref, *refs):
    refs, own_ref, sem = refs[:-2], refs[-2], refs[-1]
    copy = pltpu.make_async_copy(own_hbm, own_ref, sem)
    copy.start()
    for index, ref in enumerate(refs):
        ref[rows:] = other_ref[index * rows : (index + 1) * rows]
    copy.wait()
    for index, ref in enumerate(refs):
        ref[:rows] = own_ref[index * rows : (index + 1) * rows]


def sides_kernel(*refs):
    count = len(refs) // 2
    for index in range(count):
        rows = refs[count + index].shape[0]
        start = 0 if index < count // 2 else rows
        refs[count + index][...] = refs[index][start : start + rows]


def half_kernel(core_ref, weight_hbm, out_ref, sem):
    rows = out_ref.shape[0]
    start = pl.multiple_of(core_ref[0] * rows, 16)
    copy = pltpu.make_async_copy(weight_hbm.at[pl.ds(start, rows), :], out_ref, sem)
    copy.start()
    copy.wait()


def place_kernel(per_peer, piece_rows, places, slot_ref, *refs):
    block_refs, out_ref = refs[:-1], refs[-1]
    for peer, (block, first) in enumerate(places):
        for m in range(per_peer):
            slot = slot_ref[peer * per_peer + m]
            start = first + m * piece_rows
            out_ref[0, slot] = block_refs[block][start : start + piece_rows, :]


def stack_kernel(*refs):
    start = 0
    for ref in refs[:-1]:
        refs[-1][start : start + ref.shape[0]] = ref[...]
        start += ref.shape[0]


def crossing_kernel(rows, own_ref, *refs):
    refs[-1][:rows] = own_ref[...]
    for index, ref in enumerate(refs[:-1]):
        refs[-1][(index + 1) * rows : (index + 2) * rows] = ref[rows:]


def arrival_of(piece, per_peer, owner_place):
    source = jnp.bitwise_xor(lax.div(piece, per_peer), owner_place)
    return source * per_peer + lax.rem(piece, per_peer)


def row_codes(rows, first_piece, per_peer, piece_rows, token_rows, owner_place, place, table):
    row = lax.broadcasted_iota(jnp.int32, (rows, 1), 0)
    arrival = arrival_of(first_piece + lax.div(row, piece_rows), per_peer, owner_place)
    lane = lax.broadcasted_iota(jnp.int32, (1, table.shape[1]), 1)
    found = jnp.zeros((rows, 1), jnp.int32)
    for clip in range(table.shape[0]):
        number = jnp.where(
            arrival == table[clip : clip + 1], lane + clip * table.shape[1], 0
        )
        found += jnp.sum(number, axis=1, keepdims=True)
    return found * token_rows + place * piece_rows + lax.rem(row, piece_rows)


def pick(clip, table):
    rows = jnp.broadcast_to(table[0:1], (clip.shape[0], table.shape[1]))
    for index in range(1, table.shape[0]):
        rows = jnp.where(clip == index, table[index : index + 1], rows)
    return rows


def norm_kernel(
    clip_tokens, codes_of, owner_ref, place_ref, table_ref, modulation_ref, *refs
):
    block_refs, out_ref = refs[:-1], refs[-1]
    code = codes_of(out_ref.shape[0], owner_ref[0], place_ref[0], table_ref[0])
    clip = lax.div(code, clip_tokens)
    rows = jnp.concatenate([ref[...].astype(F32) for ref in block_refs], axis=0)
    average = jnp.mean(rows, axis=-1, keepdims=True)
    centered = rows - average
    variance = jnp.mean(centered * centered, axis=-1, keepdims=True)
    normed = centered * lax.rsqrt(variance + EPSILON)
    shift = pick(clip, modulation_ref[0].astype(F32))
    scale = pick(clip, modulation_ref[1].astype(F32))
    out_ref[...] = (normed * (1.0 + scale) + shift).astype(BF16)


def project_kernel(head_size, weight_ref, gain_ref, *refs):
    hidden_refs, out_ref = refs[:-1], refs[-1]
    hidden = jnp.concatenate([ref[...] for ref in hidden_refs], axis=0)
    projected = lax.dot_general(
        weight_ref[...], hidden, (((1,), (1,)), ((), ())), preferred_element_type=F32
    )
    width = weight_ref.shape[0] // 3
    shape = (head_size, head_size)
    diagonal = lax.broadcasted_iota(jnp.int32, shape, 0) == lax.broadcasted_iota(
        jnp.int32, shape, 1
    )
    found = []
    for part in range(2):
        gain = jnp.sum(
            jnp.where(diagonal, gain_ref[part : part + 1, :], 0.0), axis=1, keepdims=True
        )
        for start in range(part * width, (part + 1) * width, head_size):
            value = projected[start : start + head_size]
            square = jnp.sum(value * value, axis=0, keepdims=True) * (1.0 / head_size)
            found.append(value * lax.rsqrt(square + EPSILON) * gain)
    found.append(projected[2 * width :])
    out_ref[...] = jnp.concatenate(found, axis=0).astype(BF16)


def token_codes(tokens, group_rows, per_peer, piece_rows, owner_ref, place_ref, table_ref):
    clips, per_clip = table_ref.shape[1:]
    seq_count = tokens // 2 // group_rows
    token = lax.broadcasted_iota(jnp.int32, (1, tokens), 1)
    row = lax.rem(token, group_rows)
    block = lax.div(token, group_rows)
    piece = lax.div(block, seq_count) * (group_rows // piece_rows) + lax.div(row, piece_rows)
    arrival = arrival_of(piece, per_peer, owner_ref[0])
    found = jnp.zeros_like(token)
    for clip in range(clips):
        for p in range(per_clip):
            found = jnp.where(arrival == table_ref[0, clip, p], clip * per_clip + p, found)
    source = jnp.bitwise_xor(lax.rem(block, seq_count), place_ref[0])
    return found * (piece_rows * seq_count) + source * piece_rows + lax.rem(row, piece_rows)


def gather_kernel(
    first, group_rows, per_peer, piece_rows, owner_ref, place_ref, table_ref, stacked_ref, *refs
):
    out_ref = refs[-1]
    clips, _, clip_tokens = out_ref.shape
    code = token_codes(
        clips * clip_tokens, group_rows, per_peer, piece_rows, owner_ref, place_ref, table_ref
    )[:, first : first + stacked_ref.shape[1]]
    position = lax.broadcasted_iota(jnp.int32, (clip_tokens, 1), 0)
    for clip in range(clips):
        chosen = jnp.where(code == position + clip * clip_tokens, 1.0, 0.0).astype(BF16)
        picked = lax.dot_general(
            stacked_ref[...], chosen, (((1,), (1,)), ((), ())), preferred_element_type=F32
        )
        if len(refs) > 1:
            picked += refs[0][clip].astype(F32)
        out_ref[clip] = picked.astype(BF16)


def attention_kernel(
    head_size, per_peer, piece_rows, length_ref, owner_ref, place_ref, table_ref, *refs
):
    early_ref, late_ref, out_refs = refs[0], refs[1], refs[2:]
    clips, features, clip_tokens = early_ref.shape
    width, tokens = features // 3, clips * clip_tokens
    seq_count = len(out_refs)
    group_rows = tokens // 2 // seq_count
    code = token_codes(
        tokens, group_rows, per_peer, piece_rows, owner_ref, place_ref, table_ref
    )
    position = lax.broadcasted_iota(jnp.int32, (clip_tokens, 1), 0)
    key = lax.broadcasted_iota(jnp.int32, (8, clip_tokens), 1)
    heads = range(0, width, head_size)
    scale = math.log2(math.e) / math.sqrt(head_size)
    attended, chosen_by_clip = [], []
    for clip in range(clips):
        chosen = jnp.where(code == position + clip * clip_tokens, 1.0, 0.0).astype(BF16)
        picked = early_ref[clip].astype(F32) + lax.dot_general(
            late_ref[...],
            chosen[:, tokens - late_ref.shape[1] :],
            (((1,), (1,)), ((), ())),
            preferred_element_type=F32,
        )
        in_clip = jnp.where(key < length_ref[0, clip], 1.0, 0.0)
        scores = [
            jnp.dot(
                jnp.transpose(picked[width + head : width + head + head_size]).astype(BF16),
                picked[head : head + head_size].astype(BF16),
                preferred_element_type=F32,
            )
            for head in heads
        ]
        unscaled = [jnp.exp2(score * scale).astype(BF16) for score in scores]
        outs = []
        for head, weights in zip(heads, unscaled):
            values = picked[2 * width + head : 2 * width + head + head_size] * in_clip[:1]
            values = jnp.concatenate([values, in_clip], axis=0).astype(BF16)
            summed = jnp.dot(values, weights, preferred_element_type=F32)
            outs.append(summed[:head_size] * (1.0 / summed[head_size : head_size + 1]))
        attended.append(jnp.concatenate(outs, axis=0).astype(BF16))
        chosen_by_clip.append(chosen)
    back = jnp.dot(
        jnp.concatenate(attended, axis=1),
        jnp.concatenate(chosen_by_clip, axis=0),
        preferred_element_type=F32,
    ).astype(BF16)
    for index, ref in enumerate(out_refs):
        for group in range(2):
            start = (group * seq_count + index) * group_rows
            ref[:, group * group_rows : (group + 1) * group_rows] = back[
                :, start : start + group_rows
            ]


def projected_rows(masks, halves, core_ref, head_refs, weight_refs):
    branch = None
    for mask, head_ref in zip(masks, head_refs):
        parts = 1 if mask == 0 else halves
        for part in range(parts):
            weight = weight_refs[part][...]
            head = head_ref[...]
            if parts == 2:
                rows = weight.shape[0]
                start = jnp.bitwise_xor(core_ref[0], part) * rows
                head = head_ref[pl.ds(pl.multiple_of(start, 16), rows), :]
            term = lax.dot_general(
                head, weight, (((0,), (0,)), ((), ())), preferred_element_type=F32
            )
            branch = term if branch is None else branch + term
        weight_refs = weight_refs[parts:]
    return branch


def sides_output_kernel(masks, halves, core_ref, *refs):
    refs[-1][...] = projected_rows(
        masks, halves, core_ref, refs[: len(masks)], refs[len(masks) : -1]
    )


def residual_kernel(
    clip_tokens, codes_of, length_ref, owner_ref, place_ref, table_ref, modulation_ref, *refs
):
    block_refs, (base_ref, gate_ref) = refs[:-2], refs[-2:]
    code = codes_of(base_ref.shape[0], owner_ref[0], place_ref[0], table_ref[0])
    clip = lax.div(code, clip_tokens)
    limit = jnp.zeros_like(code)
    for index in range(length_ref.shape[1]):
        limit = jnp.where(clip == index, length_ref[0, index], limit)
    kept = lax.rem(code, clip_tokens) < limit
    rows = jnp.concatenate([ref[...].astype(F32) for ref in block_refs], axis=0)
    base_ref[...] = jnp.where(kept, rows, 0.0).astype(BF16)
    gate = pick(clip, modulation_ref[2].astype(F32))
    gate_ref[...] = jnp.where(kept, gate, 0.0).astype(BF16)


def output_kernel(masks, halves, owner_masks, core_ref, base_ref, gate_ref, partial_ref, *refs):
    head_refs, refs = refs[: len(masks)], refs[len(masks) :]
    weight_refs, out_refs = refs[: len(masks) * halves], refs[len(masks) * halves :]
    branch = partial_ref[...] + projected_rows(masks, halves, core_ref, head_refs, weight_refs)
    result = base_ref[...].astype(F32) + gate_ref[...].astype(F32) * branch
    rows = result.shape[0] // len(owner_masks)
    for index, (out, first) in enumerate(owner_masks):
        out_refs[out][first : first + rows] = result[index * rows : (index + 1) * rows].astype(
            BF16
        )


def body(
    tokens, slot_owner, clip_pieces, clip_length, modulation, qkv_weight, qk_gain, proj_weight
):
    dp_count = lax.axis_size("dp")
    seq_count = lax.axis_size("seq")
    pieces_here = tokens.shape[1]
    piece_rows = tokens.shape[2]
    model_width = tokens.shape[3]
    per_peer = pieces_here // dp_count
    head_size = qk_gain.shape[1]
    heads = HEADS // seq_count
    head_width = heads * head_size
    clips_here, per_clip = clip_pieces.shape[1:]
    clip_tokens = per_clip * piece_rows * seq_count
    block_rows = per_peer * piece_rows
    rows_here = pieces_here * piece_rows
    group_rows = rows_here // 2
    chips = dp_count // 2
    owner_place = lax.axis_index("dp").astype(jnp.int32)
    place = lax.axis_index("seq").astype(jnp.int32).reshape(1)
    core = lax.rem(owner_place, 2).reshape(1)
    owner_place = owner_place.reshape(1)
    halves = 2 if heads % 2 == 0 else 1

    smem = pl.BlockSpec(memory_space=pltpu.SMEM)
    vmem = pl.BlockSpec(memory_space=pltpu.VMEM)

    def call(
        kernel, scalars, inputs, outputs, scratch=(), out_scalars=0, limit=16, flops=10**9, where=vmem
    ):
        return pl.pallas_call(
            kernel,
            in_specs=[smem] * len(scalars)
            + (where if isinstance(where, list) else [where] * len(inputs)),
            out_specs=[smem] * out_scalars + [vmem] * (len(outputs) - out_scalars),
            out_shape=[jax.ShapeDtypeStruct(shape, dtype) for shape, dtype in outputs],
            scratch_shapes=list(scratch),
            compiler_params=pltpu.CompilerParams(vmem_limit_bytes=int(limit * 2**20)),
            cost_estimate=pl.CostEstimate(
                flops=flops, bytes_accessed=2**20, transcendentals=0
            ),
        )(*scalars, *inputs)

    x_count = math.isqrt(seq_count)
    anywhere = pl.BlockSpec(memory_space=pltpu.HBM)
    along_x = list(range(1, x_count))
    along_y = list(range(x_count, seq_count, x_count))

    proj_own = proj_weight
    if halves == 2:
        (proj_own,) = call(
            half_kernel,
            [core],
            [proj_weight],
            [((head_width // 2, model_width), BF16)],
            scratch=[pltpu.SemaphoreType.DMA],
            where=anywhere,
        )
    proj_parts = {mask: send(proj_own, "seq", mask) for mask in along_y + along_x}

    slots, own, other = call(
        functools.partial(route_kernel, per_peer, piece_rows),
        [owner_place],
        [slot_owner, tokens],
        [((pieces_here,), jnp.int32)] + [((chips * block_rows, model_width), BF16)] * 2,
        scratch=[
            pltpu.SMEM((dp_count,), jnp.int32),
            pltpu.SMEM(slot_owner.shape, jnp.int32),
            pltpu.VMEM(tokens.shape, BF16),
            pltpu.SemaphoreType.DMA((2,)),
        ],
        out_scalars=1,
        limit=59,
        flops=3 * 10**10,
        where=anywhere,
    )
    payloads = call(
        functools.partial(merge_kernel, block_rows),
        [],
        [own, send(other, "dp", 1)],
        [((2 * block_rows, model_width), BF16)] * chips,
        scratch=[pltpu.VMEM(own.shape, BF16), pltpu.SemaphoreType.DMA],
        where=[anywhere, vmem],
    )
    arrived = [send(payload, "dp", 2 * mask) for mask, payload in enumerate(payloads)]

    def codes_of(group):
        return lambda rows, *places: row_codes(
            rows,
            group * (pieces_here // 2),
            per_peer,
            piece_rows,
            piece_rows * seq_count,
            *places,
        )

    weight = jnp.transpose(qkv_weight, (1, 2, 0)).reshape(3 * head_width, model_width)
    factors = jnp.transpose(modulation[0], (1, 0, 2))
    def project(blocks, flops=3 * 10**9):
        (projected,) = call(
            functools.partial(project_kernel, head_size),
            [],
            [weight, qk_gain] + blocks,
            [((3 * head_width, sum(block.shape[0] for block in blocks)), BF16)],
            flops=flops,
        )
        return projected

    near, far = [
        call(
            functools.partial(norm_kernel, clip_tokens, codes_of(group)),
            [owner_place, place],
            [clip_pieces, factors] + arrived[group * chips // 2 : (group + 1) * chips // 2],
            [((group_rows, model_width), BF16)],
            flops=(1 + 9 * group) * 10**9,
        )[0]
        for group in range(2)
    ]
    near, proj_parts = lax.optimization_barrier((near, proj_parts))
    near, proj_parts = lax.optimization_barrier((near, proj_parts))
    sides = {mask: send(near, "seq", mask) for mask in along_y + along_x}
    far, sides = lax.optimization_barrier((far, sides))
    far_blocks = [send(far, "seq", mask) for mask in range(seq_count)]
    halved = call(
        sides_kernel,
        [],
        [sides[mask] for mask in along_x + along_y],
        [((group_rows // 2, model_width), BF16)] * len(sides),
    )
    halved = dict(zip(along_x + along_y, halved))
    near_blocks = []
    for mask in range(seq_count):
        mx = mask % x_count
        my = mask - mx
        if mx > 0 and my > 0:
            near_blocks += [send(halved[mx], "seq", my), send(halved[my], "seq", mx)]
        else:
            near_blocks.append(sides[mask] if mask > 0 else near)
    stacked_near = project(near_blocks)
    def gather(first, *arrays):
        (gathered,) = call(
            functools.partial(gather_kernel, first, group_rows, per_peer, piece_rows),
            [owner_place, place, clip_pieces],
            list(arrays),
            [((clips_here, 3 * head_width, clip_tokens), BF16)],
            limit=16 if clip_tokens <= 256 else 48,
            flops=3 * 10**9,
        )
        return gathered

    gathered = gather(0, stacked_near)
    gathered, proj_parts, settled = lax.optimization_barrier((gathered, proj_parts, arrived))
    early_blocks, late_blocks = far_blocks[: seq_count // 2], far_blocks[seq_count // 2 :]
    residual = call(
        functools.partial(residual_kernel, clip_tokens, codes_of(0)),
        [clip_length, owner_place, place],
        [clip_pieces, factors] + settled,
        [((rows_here, model_width), BF16)] * 2,
    )
    early_blocks, gathered, residual = lax.optimization_barrier(
        (early_blocks, gathered, list(residual))
    )
    gathered = gather(seq_count * group_rows, project(early_blocks), gathered)
    swapped = {mask: send(proj_parts[mask], "dp", 1) for mask in proj_parts} if halves == 2 else {}
    gathered, proj_parts = lax.optimization_barrier((gathered, proj_parts))
    for my in along_y:
        for mx in along_x:
            proj_parts[my + mx] = send(proj_parts[my], "seq", mx)
    late_blocks, gathered = lax.optimization_barrier((late_blocks, gathered))
    stacked_late, swapped = lax.optimization_barrier((project(late_blocks, 10**8), swapped))

    attended = call(
        functools.partial(attention_kernel, head_size, per_peer, piece_rows),
        [clip_length, owner_place, place, clip_pieces],
        [gathered, stacked_late],
        [((head_width, rows_here), BF16)] * seq_count,
        limit=16 if clip_tokens <= 256 else 48,
        flops=10**8,
    )
    returned = [send(array, "seq", mask) for mask, array in enumerate(attended)]
    if halves == 2:
        _, late = lax.optimization_barrier((attended[0], proj_parts))
        swapped |= {mask: send(late[mask], "dp", 1) for mask in late if mask not in swapped}
    proj_parts = proj_parts | {seq_count + mask: swapped[mask] for mask in swapped}

    half_count = dp_count // 2
    far_masks = list(range(half_count, dp_count))
    outs = {mask: (index, 0) for index, mask in enumerate(far_masks)}
    for mask in range(2, half_count):
        outs[mask] = (half_count + mask // 2 - 1, mask % 2 * block_rows)
    outs[0], outs[1] = [(half_count + half_count // 2 - 1 + core_of, 0) for core_of in range(2)]

    def weights_of(masks):
        return [
            part
            for mask in masks
            for part in (
                [proj_weight]
                if mask == 0
                else [proj_parts[mask + half * seq_count] for half in range(halves)]
            )
        ]

    beside = [0] + along_x + along_y
    across = [mask for mask in range(seq_count) if mask not in beside]
    (partial,) = call(
        functools.partial(sides_output_kernel, beside, halves),
        [core],
        [returned[mask] for mask in beside] + weights_of(beside),
        [((rows_here, model_width), F32)],
        flops=10**10,
    )
    results = call(
        functools.partial(output_kernel, across, halves, [outs[mask] for mask in range(dp_count)]),
        [core],
        residual + [partial] + [returned[mask] for mask in across] + weights_of(across),
        [((block_rows, model_width), BF16)] * half_count
        + [((2 * block_rows, model_width), BF16)] * (half_count // 2 - 1)
        + [((block_rows, model_width), BF16)] * 2,
        flops=3 * 10**9,
    )
    near_back = [
        send(block, "dp", 2 * (index + 1)) for index, block in enumerate(results[half_count:-2])
    ]
    far_back = [send(block, "dp", mask) for block, mask in zip(results, far_masks)]
    (crossing,) = call(
        functools.partial(crossing_kernel, block_rows),
        [],
        [results[-1]] + near_back,
        [((half_count // 2 * block_rows, model_width), BF16)],
    )
    crossed = send(crossing, "dp", 1)
    (far_back,) = call(
        stack_kernel,
        [],
        far_back,
        [((half_count * block_rows, model_width), BF16)],
        flops=10**10,
    )
    came_back = [far_back, crossed, results[-2]] + near_back
    places = {mask: (0, index * block_rows) for index, mask in enumerate(far_masks)}
    places[0] = (2, 0)
    for index in range(half_count // 2):
        places[2 * index + 1] = (1, index * block_rows)
        if index > 0:
            places[2 * index] = (2 + index, 0)
    (out,) = call(
        functools.partial(
            place_kernel, per_peer, piece_rows, [places[mask] for mask in range(dp_count)]
        ),
        [slots],
        came_back,
        [(tokens.shape, BF16)],
    )
    return out


def solution(mesh):
    return jax.shard_map(
        body,
        mesh=mesh,
        in_specs=(
            P("dp", None, "seq", None),
            P("dp", None),
            P("dp", None, None),
            P("dp", None),
            P("dp", None, None, None),
            P(None, None, "seq"),
            P(),
            P("seq", None),
        ),
        out_specs=P("dp", None, "seq", None),
        check_vma=False,
    )
```

```python
import functools
import math

import jax
import jax.numpy as jnp
from jax import lax
from jax.experimental import pallas as pl
from jax.experimental.pallas import tpu as pltpu
from jax.sharding import PartitionSpec as P

HEADS = 16
EPSILON = 1e-06
BF16 = jnp.bfloat16
F32 = jnp.float32


def send(array, axis, mask):
    if mask == 0:
        return array
    count = lax.axis_size(axis)
    return lax.ppermute(array, axis, [(i, i ^ mask) for i in range(count)])


def route_kernel(per_peer, piece_rows, place_ref, owner_hbm, token_hbm, *refs):
    slot_ref, own_ref, other_ref, filled_ref, owner_ref, token_ref, sems = refs
    peers = filled_ref.shape[0]
    owner_copy = pltpu.make_async_copy(owner_hbm, owner_ref, sems.at[0])
    token_copy = pltpu.make_async_copy(token_hbm, token_ref, sems.at[1])
    owner_copy.start()
    token_copy.start()
    for peer in range(peers):
        filled_ref[peer] = peer * per_peer
    owner_copy.wait()

    @pl.loop(0, peers * per_peer, unroll=8)
    def _(slot):
        peer = jnp.bitwise_xor(owner_ref[0, slot], place_ref[0])
        at = filled_ref[peer]
        filled_ref[peer] = at + 1
        slot_ref[at] = slot

    token_copy.wait()
    for peer in range(peers):
        ref = own_ref if peer % 2 == 0 else other_ref
        for m in range(per_peer):
            at = (peer // 2 * per_peer + m) * piece_rows
            ref[at : at + piece_rows, :] = token_ref[0, slot_ref[peer * per_peer + m]]


def merge_kernel(rows, own_hbm, other_ref, *refs):
    refs, own_ref, sem = refs[:-2], refs[-2], refs[-1]
    copy = pltpu.make_async_copy(own_hbm, own_ref, sem)
    copy.start()
    for index, ref in enumerate(refs):
        ref[rows:] = other_ref[index * rows : (index + 1) * rows]
    copy.wait()
    for index, ref in enumerate(refs):
        ref[:rows] = own_ref[index * rows : (index + 1) * rows]


def sides_kernel(*refs):
    count = len(refs) // 2
    for index in range(count):
        rows = refs[count + index].shape[0]
        start = 0 if index < count // 2 else rows
        refs[count + index][...] = refs[index][start : start + rows]


def half_kernel(core_ref, weight_hbm, out_ref, sem):
    rows = out_ref.shape[0]
    start = pl.multiple_of(core_ref[0] * rows, 16)
    copy = pltpu.make_async_copy(weight_hbm.at[pl.ds(start, rows), :], out_ref, sem)
    copy.start()
    copy.wait()


def place_kernel(per_peer, piece_rows, places, slot_ref, *refs):
    block_refs, out_ref = refs[:-1], refs[-1]
    for peer, (block, first) in enumerate(places):
        for m in range(per_peer):
            slot = slot_ref[peer * per_peer + m]
            start = first + m * piece_rows
            out_ref[0, slot] = block_refs[block][start : start + piece_rows, :]


def stack_kernel(*refs):
    start = 0
    for ref in refs[:-1]:
        refs[-1][start : start + ref.shape[0]] = ref[...]
        start += ref.shape[0]


def crossing_kernel(rows, own_ref, *refs):
    refs[-1][:rows] = own_ref[...]
    for index, ref in enumerate(refs[:-1]):
        refs[-1][(index + 1) * rows : (index + 2) * rows] = ref[rows:]


def arrival_of(piece, per_peer, owner_place):
    source = jnp.bitwise_xor(lax.div(piece, per_peer), owner_place)
    return source * per_peer + lax.rem(piece, per_peer)


def row_codes(rows, first_piece, per_peer, piece_rows, token_rows, owner_place, place, table):
    row = lax.broadcasted_iota(jnp.int32, (rows, 1), 0)
    arrival = arrival_of(first_piece + lax.div(row, piece_rows), per_peer, owner_place)
    lane = lax.broadcasted_iota(jnp.int32, (1, table.shape[1]), 1)
    found = jnp.zeros((rows, 1), jnp.int32)
    for clip in range(table.shape[0]):
        number = jnp.where(
            arrival == table[clip : clip + 1], lane + clip * table.shape[1], 0
        )
        found += jnp.sum(number, axis=1, keepdims=True)
    return found * token_rows + place * piece_rows + lax.rem(row, piece_rows)


def pick(clip, table):
    rows = jnp.broadcast_to(table[0:1], (clip.shape[0], table.shape[1]))
    for index in range(1, table.shape[0]):
        rows = jnp.where(clip == index, table[index : index + 1], rows)
    return rows


def norm_kernel(
    clip_tokens, codes_of, owner_ref, place_ref, table_ref, modulation_ref, *refs
):
    block_refs, out_ref = refs[:-1], refs[-1]
    code = codes_of(out_ref.shape[0], owner_ref[0], place_ref[0], table_ref[0])
    clip = lax.div(code, clip_tokens)
    rows = jnp.concatenate([ref[...].astype(F32) for ref in block_refs], axis=0)
    average = jnp.mean(rows, axis=-1, keepdims=True)
    centered = rows - average
    variance = jnp.mean(centered * centered, axis=-1, keepdims=True)
    normed = centered * lax.rsqrt(variance + EPSILON)
    shift = pick(clip, modulation_ref[0].astype(F32))
    scale = pick(clip, modulation_ref[1].astype(F32))
    out_ref[...] = (normed * (1.0 + scale) + shift).astype(BF16)


def project_kernel(head_size, weight_ref, gain_ref, *refs):
    hidden_refs, out_ref = refs[:-1], refs[-1]
    hidden = jnp.concatenate([ref[...] for ref in hidden_refs], axis=0)
    projected = lax.dot_general(
        weight_ref[...], hidden, (((1,), (1,)), ((), ())), preferred_element_type=F32
    )
    width = weight_ref.shape[0] // 3
    shape = (head_size, head_size)
    diagonal = lax.broadcasted_iota(jnp.int32, shape, 0) == lax.broadcasted_iota(
        jnp.int32, shape, 1
    )
    found = []
    for part in range(2):
        gain = jnp.sum(
            jnp.where(diagonal, gain_ref[part : part + 1, :], 0.0), axis=1, keepdims=True
        )
        for start in range(part * width, (part + 1) * width, head_size):
            value = projected[start : start + head_size]
            square = jnp.sum(value * value, axis=0, keepdims=True) * (1.0 / head_size)
            found.append(value * lax.rsqrt(square + EPSILON) * gain)
    found.append(projected[2 * width :])
    out_ref[...] = jnp.concatenate(found, axis=0).astype(BF16)


def token_codes(tokens, group_rows, per_peer, piece_rows, owner_ref, place_ref, table_ref):
    clips, per_clip = table_ref.shape[1:]
    seq_count = tokens // 2 // group_rows
    token = lax.broadcasted_iota(jnp.int32, (1, tokens), 1)
    row = lax.rem(token, group_rows)
    block = lax.div(token, group_rows)
    piece = lax.div(block, seq_count) * (group_rows // piece_rows) + lax.div(row, piece_rows)
    arrival = arrival_of(piece, per_peer, owner_ref[0])
    found = jnp.zeros_like(token)
    for clip in range(clips):
        for p in range(per_clip):
            found = jnp.where(arrival == table_ref[0, clip, p], clip * per_clip + p, found)
    source = jnp.bitwise_xor(lax.rem(block, seq_count), place_ref[0])
    return found * (piece_rows * seq_count) + source * piece_rows + lax.rem(row, piece_rows)


def gather_kernel(
    first, group_rows, per_peer, piece_rows, owner_ref, place_ref, table_ref, stacked_ref, *refs
):
    out_ref = refs[-1]
    clips, _, clip_tokens = out_ref.shape
    code = token_codes(
        clips * clip_tokens, group_rows, per_peer, piece_rows, owner_ref, place_ref, table_ref
    )[:, first : first + stacked_ref.shape[1]]
    position = lax.broadcasted_iota(jnp.int32, (clip_tokens, 1), 0)
    for clip in range(clips):
        chosen = jnp.where(code == position + clip * clip_tokens, 1.0, 0.0).astype(BF16)
        picked = lax.dot_general(
            stacked_ref[...], chosen, (((1,), (1,)), ((), ())), preferred_element_type=F32
        )
        if len(refs) > 1:
            picked += refs[0][clip].astype(F32)
        out_ref[clip] = picked.astype(BF16)


def attention_kernel(
    head_size, per_peer, piece_rows, length_ref, owner_ref, place_ref, table_ref, *refs
):
    early_ref, late_ref, out_refs = refs[0], refs[1], refs[2:]
    clips, features, clip_tokens = early_ref.shape
    width, tokens = features // 3, clips * clip_tokens
    seq_count = len(out_refs)
    group_rows = tokens // 2 // seq_count
    code = token_codes(
        tokens, group_rows, per_peer, piece_rows, owner_ref, place_ref, table_ref
    )
    position = lax.broadcasted_iota(jnp.int32, (clip_tokens, 1), 0)
    key = lax.broadcasted_iota(jnp.int32, (8, clip_tokens), 1)
    heads = range(0, width, head_size)
    scale = math.log2(math.e) / math.sqrt(head_size)
    attended, chosen_by_clip = [], []
    for clip in range(clips):
        chosen = jnp.where(code == position + clip * clip_tokens, 1.0, 0.0).astype(BF16)
        picked = early_ref[clip].astype(F32) + lax.dot_general(
            late_ref[...],
            chosen[:, tokens - late_ref.shape[1] :],
            (((1,), (1,)), ((), ())),
            preferred_element_type=F32,
        )
        in_clip = jnp.where(key < length_ref[0, clip], 1.0, 0.0)
        scores = [
            jnp.dot(
                jnp.transpose(picked[width + head : width + head + head_size]).astype(BF16),
                picked[head : head + head_size].astype(BF16),
                preferred_element_type=F32,
            )
            for head in heads
        ]
        unscaled = [jnp.exp2(score * scale).astype(BF16) for score in scores]
        outs = []
        for head, weights in zip(heads, unscaled):
            values = picked[2 * width + head : 2 * width + head + head_size] * in_clip[:1]
            values = jnp.concatenate([values, in_clip], axis=0).astype(BF16)
            summed = jnp.dot(values, weights, preferred_element_type=F32)
            outs.append(summed[:head_size] * (1.0 / summed[head_size : head_size + 1]))
        attended.append(jnp.concatenate(outs, axis=0).astype(BF16))
        chosen_by_clip.append(chosen)
    back = jnp.dot(
        jnp.concatenate(attended, axis=1),
        jnp.concatenate(chosen_by_clip, axis=0),
        preferred_element_type=F32,
    ).astype(BF16)
    for index, ref in enumerate(out_refs):
        for group in range(2):
            start = (group * seq_count + index) * group_rows
            ref[:, group * group_rows : (group + 1) * group_rows] = back[
                :, start : start + group_rows
            ]


def projected_rows(masks, halves, core_ref, head_refs, weight_refs):
    branch = None
    for mask, head_ref in zip(masks, head_refs):
        parts = 1 if mask == 0 else halves
        for part in range(parts):
            weight = weight_refs[part][...]
            head = head_ref[...]
            if parts == 2:
                rows = weight.shape[0]
                start = jnp.bitwise_xor(core_ref[0], part) * rows
                head = head_ref[pl.ds(pl.multiple_of(start, 16), rows), :]
            term = lax.dot_general(
                head, weight, (((0,), (0,)), ((), ())), preferred_element_type=F32
            )
            branch = term if branch is None else branch + term
        weight_refs = weight_refs[parts:]
    return branch


def sides_output_kernel(masks, halves, core_ref, *refs):
    refs[-1][...] = projected_rows(
        masks, halves, core_ref, refs[: len(masks)], refs[len(masks) : -1]
    )


def residual_kernel(
    clip_tokens, codes_of, length_ref, owner_ref, place_ref, table_ref, modulation_ref, *refs
):
    block_refs, (base_ref, gate_ref) = refs[:-2], refs[-2:]
    code = codes_of(base_ref.shape[0], owner_ref[0], place_ref[0], table_ref[0])
    clip = lax.div(code, clip_tokens)
    limit = jnp.zeros_like(code)
    for index in range(length_ref.shape[1]):
        limit = jnp.where(clip == index, length_ref[0, index], limit)
    kept = lax.rem(code, clip_tokens) < limit
    rows = jnp.concatenate([ref[...].astype(F32) for ref in block_refs], axis=0)
    base_ref[...] = jnp.where(kept, rows, 0.0).astype(BF16)
    gate = pick(clip, modulation_ref[2].astype(F32))
    gate_ref[...] = jnp.where(kept, gate, 0.0).astype(BF16)


def output_kernel(masks, halves, owner_masks, core_ref, base_ref, gate_ref, partial_ref, *refs):
    head_refs, refs = refs[: len(masks)], refs[len(masks) :]
    weight_refs, out_refs = refs[: len(masks) * halves], refs[len(masks) * halves :]
    branch = partial_ref[...] + projected_rows(masks, halves, core_ref, head_refs, weight_refs)
    result = base_ref[...].astype(F32) + gate_ref[...].astype(F32) * branch
    rows = result.shape[0] // len(owner_masks)
    for index, (out, first) in enumerate(owner_masks):
        out_refs[out][first : first + rows] = result[index * rows : (index + 1) * rows].astype(
            BF16
        )


def body(
    tokens, slot_owner, clip_pieces, clip_length, modulation, qkv_weight, qk_gain, proj_weight
):
    dp_count = lax.axis_size("dp")
    seq_count = lax.axis_size("seq")
    pieces_here = tokens.shape[1]
    piece_rows = tokens.shape[2]
    model_width = tokens.shape[3]
    per_peer = pieces_here // dp_count
    head_size = qk_gain.shape[1]
    heads = HEADS // seq_count
    head_width = heads * head_size
    clips_here, per_clip = clip_pieces.shape[1:]
    clip_tokens = per_clip * piece_rows * seq_count
    block_rows = per_peer * piece_rows
    rows_here = pieces_here * piece_rows
    group_rows = rows_here // 2
    chips = dp_count // 2
    owner_place = lax.axis_index("dp").astype(jnp.int32)
    place = lax.axis_index("seq").astype(jnp.int32).reshape(1)
    core = lax.rem(owner_place, 2).reshape(1)
    owner_place = owner_place.reshape(1)
    halves = 2 if heads % 2 == 0 else 1

    smem = pl.BlockSpec(memory_space=pltpu.SMEM)
    vmem = pl.BlockSpec(memory_space=pltpu.VMEM)

    def call(
        kernel, scalars, inputs, outputs, scratch=(), out_scalars=0, limit=16, flops=10**9, where=vmem
    ):
        return pl.pallas_call(
            kernel,
            in_specs=[smem] * len(scalars)
            + (where if isinstance(where, list) else [where] * len(inputs)),
            out_specs=[smem] * out_scalars + [vmem] * (len(outputs) - out_scalars),
            out_shape=[jax.ShapeDtypeStruct(shape, dtype) for shape, dtype in outputs],
            scratch_shapes=list(scratch),
            compiler_params=pltpu.CompilerParams(vmem_limit_bytes=int(limit * 2**20)),
            cost_estimate=pl.CostEstimate(
                flops=flops, bytes_accessed=2**20, transcendentals=0
            ),
        )(*scalars, *inputs)

    x_count = math.isqrt(seq_count)
    anywhere = pl.BlockSpec(memory_space=pltpu.HBM)
    along_x = list(range(1, x_count))
    along_y = list(range(x_count, seq_count, x_count))

    proj_own = proj_weight
    if halves == 2:
        (proj_own,) = call(
            half_kernel,
            [core],
            [proj_weight],
            [((head_width // 2, model_width), BF16)],
            scratch=[pltpu.SemaphoreType.DMA],
            where=anywhere,
        )
    proj_parts = {mask: send(proj_own, "seq", mask) for mask in along_y + along_x}

    slots, own, other = call(
        functools.partial(route_kernel, per_peer, piece_rows),
        [owner_place],
        [slot_owner, tokens],
        [((pieces_here,), jnp.int32)] + [((chips * block_rows, model_width), BF16)] * 2,
        scratch=[
            pltpu.SMEM((dp_count,), jnp.int32),
            pltpu.SMEM(slot_owner.shape, jnp.int32),
            pltpu.VMEM(tokens.shape, BF16),
            pltpu.SemaphoreType.DMA((2,)),
        ],
        out_scalars=1,
        limit=59,
        flops=3 * 10**10,
        where=anywhere,
    )
    payloads = call(
        functools.partial(merge_kernel, block_rows),
        [],
        [own, send(other, "dp", 1)],
        [((2 * block_rows, model_width), BF16)] * chips,
        scratch=[pltpu.VMEM(own.shape, BF16), pltpu.SemaphoreType.DMA],
        where=[anywhere, vmem],
    )
    arrived = [send(payload, "dp", 2 * mask) for mask, payload in enumerate(payloads)]

    def codes_of(group):
        return lambda rows, *places: row_codes(
            rows,
            group * (pieces_here // 2),
            per_peer,
            piece_rows,
            piece_rows * seq_count,
            *places,
        )

    weight = jnp.transpose(qkv_weight, (1, 2, 0)).reshape(3 * head_width, model_width)
    factors = jnp.transpose(modulation[0], (1, 0, 2))
    def project(blocks, flops=3 * 10**9):
        (projected,) = call(
            functools.partial(project_kernel, head_size),
            [],
            [weight, qk_gain] + blocks,
            [((3 * head_width, sum(block.shape[0] for block in blocks)), BF16)],
            flops=flops,
        )
        return projected

    near, far = [
        call(
            functools.partial(norm_kernel, clip_tokens, codes_of(group)),
            [owner_place, place],
            [clip_pieces, factors] + arrived[group * chips // 2 : (group + 1) * chips // 2],
            [((group_rows, model_width), BF16)],
            flops=(1 + 9 * group) * 10**9,
        )[0]
        for group in range(2)
    ]
    near, proj_parts = lax.optimization_barrier((near, proj_parts))
    near, proj_parts = lax.optimization_barrier((near, proj_parts))
    sides = {mask: send(near, "seq", mask) for mask in along_y + along_x}
    far, sides = lax.optimization_barrier((far, sides))
    far_blocks = [send(far, "seq", mask) for mask in range(seq_count)]
    halved = call(
        sides_kernel,
        [],
        [sides[mask] for mask in along_x + along_y],
        [((group_rows // 2, model_width), BF16)] * len(sides),
    )
    halved = dict(zip(along_x + along_y, halved))
    near_blocks = []
    for mask in range(seq_count):
        mx = mask % x_count
        my = mask - mx
        if mx > 0 and my > 0:
            near_blocks += [send(halved[mx], "seq", my), send(halved[my], "seq", mx)]
        else:
            near_blocks.append(sides[mask] if mask > 0 else near)
    stacked_near = project(near_blocks)
    def gather(first, *arrays):
        (gathered,) = call(
            functools.partial(gather_kernel, first, group_rows, per_peer, piece_rows),
            [owner_place, place, clip_pieces],
            list(arrays),
            [((clips_here, 3 * head_width, clip_tokens), BF16)],
            limit=16 if clip_tokens <= 256 else 48,
            flops=3 * 10**9,
        )
        return gathered

    gathered = gather(0, stacked_near)
    gathered, proj_parts = lax.optimization_barrier((gathered, proj_parts))
    early_blocks, late_blocks = far_blocks[: seq_count // 2], far_blocks[seq_count // 2 :]
    early_blocks, gathered = lax.optimization_barrier((early_blocks, gathered))
    gathered = gather(seq_count * group_rows, project(early_blocks), gathered)
    swapped = {mask: send(proj_parts[mask], "dp", 1) for mask in proj_parts} if halves == 2 else {}
    gathered, proj_parts = lax.optimization_barrier((gathered, proj_parts))
    for my in along_y:
        for mx in along_x:
            proj_parts[my + mx] = send(proj_parts[my], "seq", mx)
    late_blocks, gathered = lax.optimization_barrier((late_blocks, gathered))
    stacked_late, swapped = lax.optimization_barrier((project(late_blocks, 10**8), swapped))

    attended = call(
        functools.partial(attention_kernel, head_size, per_peer, piece_rows),
        [clip_length, owner_place, place, clip_pieces],
        [gathered, stacked_late],
        [((head_width, rows_here), BF16)] * seq_count,
        limit=16 if clip_tokens <= 256 else 48,
        flops=10**8,
    )
    returned = [send(array, "seq", mask) for mask, array in enumerate(attended)]
    if halves == 2:
        _, late = lax.optimization_barrier((attended[0], proj_parts))
        swapped |= {mask: send(late[mask], "dp", 1) for mask in late if mask not in swapped}
    proj_parts = proj_parts | {seq_count + mask: swapped[mask] for mask in swapped}

    half_count = dp_count // 2
    far_masks = list(range(half_count, dp_count))
    outs = {mask: (index, 0) for index, mask in enumerate(far_masks)}
    for mask in range(2, half_count):
        outs[mask] = (half_count + mask // 2 - 1, mask % 2 * block_rows)
    outs[0], outs[1] = [(half_count + half_count // 2 - 1 + core_of, 0) for core_of in range(2)]

    def weights_of(masks):
        return [
            part
            for mask in masks
            for part in (
                [proj_weight]
                if mask == 0
                else [proj_parts[mask + half * seq_count] for half in range(halves)]
            )
        ]

    beside = [0] + along_x + along_y
    across = [mask for mask in range(seq_count) if mask not in beside]
    _, settled = lax.optimization_barrier((attended[0], arrived))
    residual = call(
        functools.partial(residual_kernel, clip_tokens, codes_of(0)),
        [clip_length, owner_place, place],
        [clip_pieces, factors] + settled,
        [((rows_here, model_width), BF16)] * 2,
    )
    proj_own, residual = lax.optimization_barrier((proj_weight, list(residual)))
    (partial,) = call(
        functools.partial(sides_output_kernel, beside, halves),
        [core],
        [returned[mask] for mask in beside] + [proj_own] + weights_of(beside)[1:],
        [((rows_here, model_width), F32)],
        flops=10**10,
    )
    results = call(
        functools.partial(output_kernel, across, halves, [outs[mask] for mask in range(dp_count)]),
        [core],
        residual + [partial] + [returned[mask] for mask in across] + weights_of(across),
        [((block_rows, model_width), BF16)] * half_count
        + [((2 * block_rows, model_width), BF16)] * (half_count // 2 - 1)
        + [((block_rows, model_width), BF16)] * 2,
        flops=3 * 10**9,
    )
    near_back = [
        send(block, "dp", 2 * (index + 1)) for index, block in enumerate(results[half_count:-2])
    ]
    far_back = [send(block, "dp", mask) for block, mask in zip(results, far_masks)]
    (crossing,) = call(
        functools.partial(crossing_kernel, block_rows),
        [],
        [results[-1]] + near_back,
        [((half_count // 2 * block_rows, model_width), BF16)],
    )
    crossed = send(crossing, "dp", 1)
    (far_back,) = call(
        stack_kernel,
        [],
        far_back,
        [((half_count * block_rows, model_width), BF16)],
        flops=10**10,
    )
    came_back = [far_back, crossed, results[-2]] + near_back
    places = {mask: (0, index * block_rows) for index, mask in enumerate(far_masks)}
    places[0] = (2, 0)
    for index in range(half_count // 2):
        places[2 * index + 1] = (1, index * block_rows)
        if index > 0:
            places[2 * index] = (2 + index, 0)
    (out,) = call(
        functools.partial(
            place_kernel, per_peer, piece_rows, [places[mask] for mask in range(dp_count)]
        ),
        [slots],
        came_back,
        [(tokens.shape, BF16)],
    )
    return out


def solution(mesh):
    return jax.shard_map(
        body,
        mesh=mesh,
        in_specs=(
            P("dp", None, "seq", None),
            P("dp", None),
            P("dp", None, None),
            P("dp", None),
            P("dp", None, None, None),
            P(None, None, "seq"),
            P(),
            P("seq", None),
        ),
        out_specs=P("dp", None, "seq", None),
        check_vma=False,
    )
```

```python
import functools
import math

import jax
import jax.numpy as jnp
from jax import lax
from jax.experimental import pallas as pl
from jax.experimental.pallas import tpu as pltpu
from jax.sharding import PartitionSpec as P

HEADS = 16
EPSILON = 1e-06
BF16 = jnp.bfloat16
F32 = jnp.float32


def send(array, axis, mask):
    if mask == 0:
        return array
    count = lax.axis_size(axis)
    return lax.ppermute(array, axis, [(i, i ^ mask) for i in range(count)])


def route_kernel(per_peer, piece_rows, place_ref, owner_hbm, token_hbm, *refs):
    slot_ref, own_ref, other_ref, filled_ref, owner_ref, token_ref, sems = refs
    peers = filled_ref.shape[0]
    owner_copy = pltpu.make_async_copy(owner_hbm, owner_ref, sems.at[0])
    token_copy = pltpu.make_async_copy(token_hbm, token_ref, sems.at[1])
    owner_copy.start()
    token_copy.start()
    for peer in range(peers):
        filled_ref[peer] = peer * per_peer
    owner_copy.wait()

    @pl.loop(0, peers * per_peer, unroll=8)
    def _(slot):
        peer = jnp.bitwise_xor(owner_ref[0, slot], place_ref[0])
        at = filled_ref[peer]
        filled_ref[peer] = at + 1
        slot_ref[at] = slot

    token_copy.wait()
    for peer in range(peers):
        ref = own_ref if peer % 2 == 0 else other_ref
        for m in range(per_peer):
            at = (peer // 2 * per_peer + m) * piece_rows
            ref[at : at + piece_rows, :] = token_ref[0, slot_ref[peer * per_peer + m]]


def merge_kernel(rows, own_hbm, other_ref, *refs):
    refs, own_ref, sem = refs[:-2], refs[-2], refs[-1]
    copy = pltpu.make_async_copy(own_hbm, own_ref, sem)
    copy.start()
    for index, ref in enumerate(refs):
        ref[rows:] = other_ref[index * rows : (index + 1) * rows]
    copy.wait()
    for index, ref in enumerate(refs):
        ref[:rows] = own_ref[index * rows : (index + 1) * rows]


def sides_kernel(*refs):
    count = len(refs) // 2
    for index in range(count):
        rows = refs[count + index].shape[0]
        start = 0 if index < count // 2 else rows
        refs[count + index][...] = refs[index][start : start + rows]


def half_kernel(core_ref, weight_hbm, out_ref, sem):
    rows = out_ref.shape[0]
    start = pl.multiple_of(core_ref[0] * rows, 16)
    copy = pltpu.make_async_copy(weight_hbm.at[pl.ds(start, rows), :], out_ref, sem)
    copy.start()
    copy.wait()


def place_kernel(per_peer, piece_rows, places, slot_ref, *refs):
    block_refs, out_ref = refs[:-1], refs[-1]
    for peer, (block, first) in enumerate(places):
        for m in range(per_peer):
            slot = slot_ref[peer * per_peer + m]
            start = first + m * piece_rows
            out_ref[0, slot] = block_refs[block][start : start + piece_rows, :]


def stack_kernel(*refs):
    start = 0
    for ref in refs[:-1]:
        refs[-1][start : start + ref.shape[0]] = ref[...]
        start += ref.shape[0]


def crossing_kernel(rows, own_ref, *refs):
    refs[-1][:rows] = own_ref[...]
    for index, ref in enumerate(refs[:-1]):
        refs[-1][(index + 1) * rows : (index + 2) * rows] = ref[rows:]


def arrival_of(piece, per_peer, owner_place):
    source = jnp.bitwise_xor(lax.div(piece, per_peer), owner_place)
    return source * per_peer + lax.rem(piece, per_peer)


def row_codes(rows, first_piece, per_peer, piece_rows, token_rows, owner_place, place, table):
    row = lax.broadcasted_iota(jnp.int32, (rows, 1), 0)
    arrival = arrival_of(first_piece + lax.div(row, piece_rows), per_peer, owner_place)
    lane = lax.broadcasted_iota(jnp.int32, (1, table.shape[1]), 1)
    found = jnp.zeros((rows, 1), jnp.int32)
    for clip in range(table.shape[0]):
        number = jnp.where(
            arrival == table[clip : clip + 1], lane + clip * table.shape[1], 0
        )
        found += jnp.sum(number, axis=1, keepdims=True)
    return found * token_rows + place * piece_rows + lax.rem(row, piece_rows)


def pick(clip, table):
    rows = jnp.broadcast_to(table[0:1], (clip.shape[0], table.shape[1]))
    for index in range(1, table.shape[0]):
        rows = jnp.where(clip == index, table[index : index + 1], rows)
    return rows


def norm_kernel(
    clip_tokens, codes_of, owner_ref, place_ref, table_ref, modulation_ref, *refs
):
    block_refs, out_ref = refs[:-1], refs[-1]
    code = codes_of(out_ref.shape[0], owner_ref[0], place_ref[0], table_ref[0])
    clip = lax.div(code, clip_tokens)
    rows = jnp.concatenate([ref[...].astype(F32) for ref in block_refs], axis=0)
    average = jnp.mean(rows, axis=-1, keepdims=True)
    centered = rows - average
    variance = jnp.mean(centered * centered, axis=-1, keepdims=True)
    normed = centered * lax.rsqrt(variance + EPSILON)
    shift = pick(clip, modulation_ref[0].astype(F32))
    scale = pick(clip, modulation_ref[1].astype(F32))
    out_ref[...] = (normed * (1.0 + scale) + shift).astype(BF16)


def project_kernel(head_size, weight_ref, gain_ref, *refs):
    hidden_refs, out_ref = refs[:-1], refs[-1]
    hidden = jnp.concatenate([ref[...] for ref in hidden_refs], axis=0)
    projected = lax.dot_general(
        weight_ref[...], hidden, (((1,), (1,)), ((), ())), preferred_element_type=F32
    )
    width = weight_ref.shape[0] // 3
    shape = (head_size, head_size)
    diagonal = lax.broadcasted_iota(jnp.int32, shape, 0) == lax.broadcasted_iota(
        jnp.int32, shape, 1
    )
    found = []
    for part in range(2):
        gain = jnp.sum(
            jnp.where(diagonal, gain_ref[part : part + 1, :], 0.0), axis=1, keepdims=True
        )
        for start in range(part * width, (part + 1) * width, head_size):
            value = projected[start : start + head_size]
            square = jnp.sum(value * value, axis=0, keepdims=True) * (1.0 / head_size)
            found.append(value * lax.rsqrt(square + EPSILON) * gain)
    found.append(projected[2 * width :])
    out_ref[...] = jnp.concatenate(found, axis=0).astype(BF16)


def token_codes(tokens, group_rows, per_peer, piece_rows, owner_ref, place_ref, table_ref):
    clips, per_clip = table_ref.shape[1:]
    seq_count = tokens // 2 // group_rows
    token = lax.broadcasted_iota(jnp.int32, (1, tokens), 1)
    row = lax.rem(token, group_rows)
    block = lax.div(token, group_rows)
    piece = lax.div(block, seq_count) * (group_rows // piece_rows) + lax.div(row, piece_rows)
    arrival = arrival_of(piece, per_peer, owner_ref[0])
    found = jnp.zeros_like(token)
    for clip in range(clips):
        for p in range(per_clip):
            found = jnp.where(arrival == table_ref[0, clip, p], clip * per_clip + p, found)
    source = jnp.bitwise_xor(lax.rem(block, seq_count), place_ref[0])
    return found * (piece_rows * seq_count) + source * piece_rows + lax.rem(row, piece_rows)


def gather_kernel(
    first, group_rows, per_peer, piece_rows, owner_ref, place_ref, table_ref, stacked_ref, *refs
):
    out_ref = refs[-1]
    clips, _, clip_tokens = out_ref.shape
    code = token_codes(
        clips * clip_tokens, group_rows, per_peer, piece_rows, owner_ref, place_ref, table_ref
    )[:, first : first + stacked_ref.shape[1]]
    position = lax.broadcasted_iota(jnp.int32, (clip_tokens, 1), 0)
    for clip in range(clips):
        chosen = jnp.where(code == position + clip * clip_tokens, 1.0, 0.0).astype(BF16)
        picked = lax.dot_general(
            stacked_ref[...], chosen, (((1,), (1,)), ((), ())), preferred_element_type=F32
        )
        if len(refs) > 1:
            picked += refs[0][clip].astype(F32)
        out_ref[clip] = picked.astype(BF16)


def chosen_kernel(group_rows, per_peer, piece_rows, owner_ref, place_ref, table_ref, out_ref):
    rows, tokens = out_ref.shape
    code = token_codes(
        tokens, group_rows, per_peer, piece_rows, owner_ref, place_ref, table_ref
    )
    row = lax.broadcasted_iota(jnp.int32, (rows, 1), 0)
    out_ref[...] = jnp.where(code == row, 1.0, 0.0).astype(BF16)


def attention_kernel(
    head_size, per_peer, piece_rows, length_ref, owner_ref, place_ref, table_ref, *refs
):
    early_ref, late_ref, refs = refs[0], refs[1], refs[2:]
    one_hot_ref = None
    if refs[0].shape[0] == refs[0].shape[1]:
        one_hot_ref, refs = refs[0], refs[1:]
    out_refs = refs
    clips, features, clip_tokens = early_ref.shape
    width, tokens = features // 3, clips * clip_tokens
    seq_count = len(out_refs)
    group_rows = tokens // 2 // seq_count
    code = token_codes(
        tokens, group_rows, per_peer, piece_rows, owner_ref, place_ref, table_ref
    )
    position = lax.broadcasted_iota(jnp.int32, (clip_tokens, 1), 0)
    key = lax.broadcasted_iota(jnp.int32, (8, clip_tokens), 1)
    heads = range(0, width, head_size)
    scale = math.log2(math.e) / math.sqrt(head_size)
    attended, chosen_by_clip = [], []
    for clip in range(clips):
        if one_hot_ref is not None:
            chosen = one_hot_ref[clip * clip_tokens : (clip + 1) * clip_tokens]
        else:
            chosen = jnp.where(code == position + clip * clip_tokens, 1.0, 0.0).astype(BF16)
        picked = early_ref[clip].astype(F32) + lax.dot_general(
            late_ref[...],
            chosen[:, tokens - late_ref.shape[1] :],
            (((1,), (1,)), ((), ())),
            preferred_element_type=F32,
        )
        in_clip = jnp.where(key < length_ref[0, clip], 1.0, 0.0)
        scores = [
            jnp.dot(
                jnp.transpose(picked[width + head : width + head + head_size]).astype(BF16),
                picked[head : head + head_size].astype(BF16),
                preferred_element_type=F32,
            )
            for head in heads
        ]
        unscaled = [jnp.exp2(score * scale).astype(BF16) for score in scores]
        outs = []
        for head, weights in zip(heads, unscaled):
            values = picked[2 * width + head : 2 * width + head + head_size] * in_clip[:1]
            values = jnp.concatenate([values, in_clip], axis=0).astype(BF16)
            summed = jnp.dot(values, weights, preferred_element_type=F32)
            outs.append(summed[:head_size] * (1.0 / summed[head_size : head_size + 1]))
        attended.append(jnp.concatenate(outs, axis=0).astype(BF16))
        chosen_by_clip.append(chosen)
    back = jnp.dot(
        jnp.concatenate(attended, axis=1),
        jnp.concatenate(chosen_by_clip, axis=0),
        preferred_element_type=F32,
    ).astype(BF16)
    for index, ref in enumerate(out_refs):
        for group in range(2):
            start = (group * seq_count + index) * group_rows
            ref[:, group * group_rows : (group + 1) * group_rows] = back[
                :, start : start + group_rows
            ]


def projected_rows(masks, halves, core_ref, head_refs, weight_refs):
    branch = None
    for mask, head_ref in zip(masks, head_refs):
        parts = 1 if mask == 0 else halves
        for part in range(parts):
            weight = weight_refs[part][...]
            head = head_ref[...]
            if parts == 2:
                rows = weight.shape[0]
                start = jnp.bitwise_xor(core_ref[0], part) * rows
                head = head_ref[pl.ds(pl.multiple_of(start, 16), rows), :]
            term = lax.dot_general(
                head, weight, (((0,), (0,)), ((), ())), preferred_element_type=F32
            )
            branch = term if branch is None else branch + term
        weight_refs = weight_refs[parts:]
    return branch


def sides_output_kernel(masks, halves, core_ref, *refs):
    refs[-1][...] = projected_rows(
        masks, halves, core_ref, refs[: len(masks)], refs[len(masks) : -1]
    )


def residual_kernel(
    clip_tokens, codes_of, length_ref, owner_ref, place_ref, table_ref, modulation_ref, *refs
):
    block_refs, (base_ref, gate_ref) = refs[:-2], refs[-2:]
    code = codes_of(base_ref.shape[0], owner_ref[0], place_ref[0], table_ref[0])
    clip = lax.div(code, clip_tokens)
    limit = jnp.zeros_like(code)
    for index in range(length_ref.shape[1]):
        limit = jnp.where(clip == index, length_ref[0, index], limit)
    kept = lax.rem(code, clip_tokens) < limit
    rows = jnp.concatenate([ref[...].astype(F32) for ref in block_refs], axis=0)
    base_ref[...] = jnp.where(kept, rows, 0.0).astype(BF16)
    gate = pick(clip, modulation_ref[2].astype(F32))
    gate_ref[...] = jnp.where(kept, gate, 0.0).astype(BF16)


def output_kernel(masks, halves, owner_masks, core_ref, base_ref, gate_ref, partial_ref, *refs):
    head_refs, refs = refs[: len(masks)], refs[len(masks) :]
    weight_refs, out_refs = refs[: len(masks) * halves], refs[len(masks) * halves :]
    branch = partial_ref[...] + projected_rows(masks, halves, core_ref, head_refs, weight_refs)
    result = base_ref[...].astype(F32) + gate_ref[...].astype(F32) * branch
    rows = result.shape[0] // len(owner_masks)
    for index, (out, first) in enumerate(owner_masks):
        out_refs[out][first : first + rows] = result[index * rows : (index + 1) * rows].astype(
            BF16
        )


def body(
    tokens, slot_owner, clip_pieces, clip_length, modulation, qkv_weight, qk_gain, proj_weight
):
    dp_count = lax.axis_size("dp")
    seq_count = lax.axis_size("seq")
    pieces_here = tokens.shape[1]
    piece_rows = tokens.shape[2]
    model_width = tokens.shape[3]
    per_peer = pieces_here // dp_count
    head_size = qk_gain.shape[1]
    heads = HEADS // seq_count
    head_width = heads * head_size
    clips_here, per_clip = clip_pieces.shape[1:]
    clip_tokens = per_clip * piece_rows * seq_count
    block_rows = per_peer * piece_rows
    rows_here = pieces_here * piece_rows
    group_rows = rows_here // 2
    chips = dp_count // 2
    owner_place = lax.axis_index("dp").astype(jnp.int32)
    place = lax.axis_index("seq").astype(jnp.int32).reshape(1)
    core = lax.rem(owner_place, 2).reshape(1)
    owner_place = owner_place.reshape(1)
    halves = 2 if heads % 2 == 0 else 1

    smem = pl.BlockSpec(memory_space=pltpu.SMEM)
    vmem = pl.BlockSpec(memory_space=pltpu.VMEM)

    def call(
        kernel, scalars, inputs, outputs, scratch=(), out_scalars=0, limit=16, flops=10**9, where=vmem
    ):
        return pl.pallas_call(
            kernel,
            in_specs=[smem] * len(scalars)
            + (where if isinstance(where, list) else [where] * len(inputs)),
            out_specs=[smem] * out_scalars + [vmem] * (len(outputs) - out_scalars),
            out_shape=[jax.ShapeDtypeStruct(shape, dtype) for shape, dtype in outputs],
            scratch_shapes=list(scratch),
            compiler_params=pltpu.CompilerParams(vmem_limit_bytes=int(limit * 2**20)),
            cost_estimate=pl.CostEstimate(
                flops=flops, bytes_accessed=2**20, transcendentals=0
            ),
        )(*scalars, *inputs)

    x_count = math.isqrt(seq_count)
    anywhere = pl.BlockSpec(memory_space=pltpu.HBM)
    along_x = list(range(1, x_count))
    along_y = list(range(x_count, seq_count, x_count))

    proj_own = proj_weight
    if halves == 2:
        (proj_own,) = call(
            half_kernel,
            [core],
            [proj_weight],
            [((head_width // 2, model_width), BF16)],
            scratch=[pltpu.SemaphoreType.DMA],
            where=anywhere,
        )
    proj_parts = {mask: send(proj_own, "seq", mask) for mask in along_y + along_x}

    slots, own, other = call(
        functools.partial(route_kernel, per_peer, piece_rows),
        [owner_place],
        [slot_owner, tokens],
        [((pieces_here,), jnp.int32)] + [((chips * block_rows, model_width), BF16)] * 2,
        scratch=[
            pltpu.SMEM((dp_count,), jnp.int32),
            pltpu.SMEM(slot_owner.shape, jnp.int32),
            pltpu.VMEM(tokens.shape, BF16),
            pltpu.SemaphoreType.DMA((2,)),
        ],
        out_scalars=1,
        limit=59,
        flops=3 * 10**10,
        where=anywhere,
    )
    payloads = call(
        functools.partial(merge_kernel, block_rows),
        [],
        [own, send(other, "dp", 1)],
        [((2 * block_rows, model_width), BF16)] * chips,
        scratch=[pltpu.VMEM(own.shape, BF16), pltpu.SemaphoreType.DMA],
        where=[anywhere, vmem],
    )
    arrived = [send(payload, "dp", 2 * mask) for mask, payload in enumerate(payloads)]

    def codes_of(group):
        return lambda rows, *places: row_codes(
            rows,
            group * (pieces_here // 2),
            per_peer,
            piece_rows,
            piece_rows * seq_count,
            *places,
        )

    weight = jnp.transpose(qkv_weight, (1, 2, 0)).reshape(3 * head_width, model_width)
    factors = jnp.transpose(modulation[0], (1, 0, 2))
    def project(blocks, flops=3 * 10**9):
        (projected,) = call(
            functools.partial(project_kernel, head_size),
            [],
            [weight, qk_gain] + blocks,
            [((3 * head_width, sum(block.shape[0] for block in blocks)), BF16)],
            flops=flops,
        )
        return projected

    def hidden_rows(group, placed):
        return call(
            functools.partial(norm_kernel, clip_tokens, codes_of(group)),
            [placed, place],
            [clip_pieces, factors] + arrived[group * chips // 2 : (group + 1) * chips // 2],
            [((group_rows, model_width), BF16)],
            flops=(1 + 9 * group) * 10**9,
        )[0]

    near = hidden_rows(0, owner_place)
    one_hot, placed = [], owner_place
    if clip_tokens <= 256:
        _, early = lax.optimization_barrier((near, owner_place))
        one_hot = call(
            functools.partial(chosen_kernel, group_rows, per_peer, piece_rows),
            [early, place, clip_pieces],
            [],
            [((clips_here * clip_tokens, clips_here * clip_tokens), BF16)],
        )
        one_hot, placed = lax.optimization_barrier((list(one_hot), owner_place))
    far = hidden_rows(1, placed)
    near, proj_parts = lax.optimization_barrier((near, proj_parts))
    near, proj_parts = lax.optimization_barrier((near, proj_parts))
    sides = {mask: send(near, "seq", mask) for mask in along_y + along_x}
    far, sides = lax.optimization_barrier((far, sides))
    far_blocks = [send(far, "seq", mask) for mask in range(seq_count)]
    halved = call(
        sides_kernel,
        [],
        [sides[mask] for mask in along_x + along_y],
        [((group_rows // 2, model_width), BF16)] * len(sides),
    )
    halved = dict(zip(along_x + along_y, halved))
    near_blocks = []
    for mask in range(seq_count):
        mx = mask % x_count
        my = mask - mx
        if mx > 0 and my > 0:
            near_blocks += [send(halved[mx], "seq", my), send(halved[my], "seq", mx)]
        else:
            near_blocks.append(sides[mask] if mask > 0 else near)
    stacked_near = project(near_blocks)
    def gather(first, *arrays):
        (gathered,) = call(
            functools.partial(gather_kernel, first, group_rows, per_peer, piece_rows),
            [owner_place, place, clip_pieces],
            list(arrays),
            [((clips_here, 3 * head_width, clip_tokens), BF16)],
            limit=16 if clip_tokens <= 256 else 48,
            flops=3 * 10**9,
        )
        return gathered

    gathered = gather(0, stacked_near)
    gathered, proj_parts, settled = lax.optimization_barrier((gathered, proj_parts, arrived))
    early_blocks, late_blocks = far_blocks[: seq_count // 2], far_blocks[seq_count // 2 :]
    residual = call(
        functools.partial(residual_kernel, clip_tokens, codes_of(0)),
        [clip_length, owner_place, place],
        [clip_pieces, factors] + settled,
        [((rows_here, model_width), BF16)] * 2,
    )
    early_blocks, gathered, residual = lax.optimization_barrier(
        (early_blocks, gathered, list(residual))
    )
    gathered = gather(seq_count * group_rows, project(early_blocks), gathered)
    swapped = {mask: send(proj_parts[mask], "dp", 1) for mask in proj_parts} if halves == 2 else {}
    gathered, proj_parts = lax.optimization_barrier((gathered, proj_parts))
    for my in along_y:
        for mx in along_x:
            proj_parts[my + mx] = send(proj_parts[my], "seq", mx)
    late_blocks, gathered = lax.optimization_barrier((late_blocks, gathered))
    stacked_late, swapped = lax.optimization_barrier((project(late_blocks, 10**8), swapped))

    attended = call(
        functools.partial(attention_kernel, head_size, per_peer, piece_rows),
        [clip_length, owner_place, place, clip_pieces],
        [gathered, stacked_late] + one_hot,
        [((head_width, rows_here), BF16)] * seq_count,
        limit=16 if clip_tokens <= 256 else 48,
        flops=10**8,
    )
    returned = [send(array, "seq", mask) for mask, array in enumerate(attended)]
    if halves == 2:
        _, late = lax.optimization_barrier((attended[0], proj_parts))
        swapped |= {mask: send(late[mask], "dp", 1) for mask in late if mask not in swapped}
    proj_parts = proj_parts | {seq_count + mask: swapped[mask] for mask in swapped}

    half_count = dp_count // 2
    far_masks = list(range(half_count, dp_count))
    outs = {mask: (index, 0) for index, mask in enumerate(far_masks)}
    for mask in range(2, half_count):
        outs[mask] = (half_count + mask // 2 - 1, mask % 2 * block_rows)
    outs[0], outs[1] = [(half_count + half_count // 2 - 1 + core_of, 0) for core_of in range(2)]

    def weights_of(masks):
        return [
            part
            for mask in masks
            for part in (
                [proj_weight]
                if mask == 0
                else [proj_parts[mask + half * seq_count] for half in range(halves)]
            )
        ]

    beside = [0] + along_x + along_y
    across = [mask for mask in range(seq_count) if mask not in beside]
    (partial,) = call(
        functools.partial(sides_output_kernel, beside, halves),
        [core],
        [returned[mask] for mask in beside] + weights_of(beside),
        [((rows_here, model_width), F32)],
        flops=10**10,
    )
    results = call(
        functools.partial(output_kernel, across, halves, [outs[mask] for mask in range(dp_count)]),
        [core],
        residual + [partial] + [returned[mask] for mask in across] + weights_of(across),
        [((block_rows, model_width), BF16)] * half_count
        + [((2 * block_rows, model_width), BF16)] * (half_count // 2 - 1)
        + [((block_rows, model_width), BF16)] * 2,
        flops=3 * 10**9,
    )
    near_back = [
        send(block, "dp", 2 * (index + 1)) for index, block in enumerate(results[half_count:-2])
    ]
    far_back = [send(block, "dp", mask) for block, mask in zip(results, far_masks)]
    (crossing,) = call(
        functools.partial(crossing_kernel, block_rows),
        [],
        [results[-1]] + near_back,
        [((half_count // 2 * block_rows, model_width), BF16)],
    )
    crossed = send(crossing, "dp", 1)
    (far_back,) = call(
        stack_kernel,
        [],
        far_back,
        [((half_count * block_rows, model_width), BF16)],
        flops=10**10,
    )
    came_back = [far_back, crossed, results[-2]] + near_back
    places = {mask: (0, index * block_rows) for index, mask in enumerate(far_masks)}
    places[0] = (2, 0)
    for index in range(half_count // 2):
        places[2 * index + 1] = (1, index * block_rows)
        if index > 0:
            places[2 * index] = (2 + index, 0)
    (out,) = call(
        functools.partial(
            place_kernel, per_peer, piece_rows, [places[mask] for mask in range(dp_count)]
        ),
        [slots],
        came_back,
        [(tokens.shape, BF16)],
    )
    return out


def solution(mesh):
    return jax.shard_map(
        body,
        mesh=mesh,
        in_specs=(
            P("dp", None, "seq", None),
            P("dp", None),
            P("dp", None, None),
            P("dp", None),
            P("dp", None, None, None),
            P(None, None, "seq"),
            P(),
            P("seq", None),
        ),
        out_specs=P("dp", None, "seq", None),
        check_vma=False,
    )
```

```python
import functools
import math

import jax
import jax.numpy as jnp
from jax import lax
from jax.experimental import pallas as pl
from jax.experimental.pallas import tpu as pltpu
from jax.sharding import PartitionSpec as P

HEADS = 16
EPSILON = 1e-06
BF16 = jnp.bfloat16
F32 = jnp.float32


def send(array, axis, mask):
    if mask == 0:
        return array
    count = lax.axis_size(axis)
    return lax.ppermute(array, axis, [(i, i ^ mask) for i in range(count)])


def route_kernel(per_peer, piece_rows, place_ref, owner_hbm, token_hbm, *refs):
    slot_ref, own_ref, other_ref, filled_ref, owner_ref, token_ref, sems = refs
    peers = filled_ref.shape[0]
    owner_copy = pltpu.make_async_copy(owner_hbm, owner_ref, sems.at[0])
    token_copy = pltpu.make_async_copy(token_hbm, token_ref, sems.at[1])
    owner_copy.start()
    token_copy.start()
    for peer in range(peers):
        filled_ref[peer] = peer * per_peer
    owner_copy.wait()

    @pl.loop(0, peers * per_peer, unroll=8)
    def _(slot):
        peer = jnp.bitwise_xor(owner_ref[0, slot], place_ref[0])
        at = filled_ref[peer]
        filled_ref[peer] = at + 1
        slot_ref[at] = slot

    token_copy.wait()
    for peer in range(peers):
        ref = own_ref if peer % 2 == 0 else other_ref
        for m in range(per_peer):
            at = (peer // 2 * per_peer + m) * piece_rows
            ref[at : at + piece_rows, :] = token_ref[0, slot_ref[peer * per_peer + m]]


def merge_kernel(rows, own_hbm, other_ref, *refs):
    refs, own_ref, sem = refs[:-2], refs[-2], refs[-1]
    copy = pltpu.make_async_copy(own_hbm, own_ref, sem)
    copy.start()
    for index, ref in enumerate(refs):
        ref[rows:] = other_ref[index * rows : (index + 1) * rows]
    copy.wait()
    for index, ref in enumerate(refs):
        ref[:rows] = own_ref[index * rows : (index + 1) * rows]


def sides_kernel(*refs):
    count = len(refs) // 2
    for index in range(count):
        rows = refs[count + index].shape[0]
        start = 0 if index < count // 2 else rows
        refs[count + index][...] = refs[index][start : start + rows]


def half_kernel(core_ref, weight_hbm, out_ref, sem):
    rows = out_ref.shape[0]
    start = pl.multiple_of(core_ref[0] * rows, 16)
    copy = pltpu.make_async_copy(weight_hbm.at[pl.ds(start, rows), :], out_ref, sem)
    copy.start()
    copy.wait()


def place_kernel(per_peer, piece_rows, places, slot_ref, *refs):
    block_refs, out_ref = refs[:-1], refs[-1]
    for peer, (block, first) in enumerate(places):
        for m in range(per_peer):
            slot = slot_ref[peer * per_peer + m]
            start = first + m * piece_rows
            out_ref[0, slot] = block_refs[block][start : start + piece_rows, :]


def stack_kernel(*refs):
    start = 0
    for ref in refs[:-1]:
        refs[-1][start : start + ref.shape[0]] = ref[...]
        start += ref.shape[0]


def crossing_kernel(rows, own_ref, *refs):
    refs[-1][:rows] = own_ref[...]
    for index, ref in enumerate(refs[:-1]):
        refs[-1][(index + 1) * rows : (index + 2) * rows] = ref[rows:]


def arrival_of(piece, per_peer, owner_place):
    source = jnp.bitwise_xor(lax.div(piece, per_peer), owner_place)
    return source * per_peer + lax.rem(piece, per_peer)


def row_codes(rows, first_piece, per_peer, piece_rows, token_rows, owner_place, place, table):
    row = lax.broadcasted_iota(jnp.int32, (rows, 1), 0)
    arrival = arrival_of(first_piece + lax.div(row, piece_rows), per_peer, owner_place)
    lane = lax.broadcasted_iota(jnp.int32, (1, table.shape[1]), 1)
    found = jnp.zeros((rows, 1), jnp.int32)
    for clip in range(table.shape[0]):
        number = jnp.where(
            arrival == table[clip : clip + 1], lane + clip * table.shape[1], 0
        )
        found += jnp.sum(number, axis=1, keepdims=True)
    return found * token_rows + place * piece_rows + lax.rem(row, piece_rows)


def pick(clip, table):
    rows = jnp.broadcast_to(table[0:1], (clip.shape[0], table.shape[1]))
    for index in range(1, table.shape[0]):
        rows = jnp.where(clip == index, table[index : index + 1], rows)
    return rows


def norm_kernel(
    clip_tokens, codes_of, owner_ref, place_ref, table_ref, modulation_ref, *refs
):
    block_refs, out_ref = refs[:-1], refs[-1]
    code = codes_of(out_ref.shape[0], owner_ref[0], place_ref[0], table_ref[0])
    clip = lax.div(code, clip_tokens)
    rows = jnp.concatenate([ref[...].astype(F32) for ref in block_refs], axis=0)
    average = jnp.mean(rows, axis=-1, keepdims=True)
    centered = rows - average
    variance = jnp.mean(centered * centered, axis=-1, keepdims=True)
    normed = centered * lax.rsqrt(variance + EPSILON)
    shift = pick(clip, modulation_ref[0].astype(F32))
    scale = pick(clip, modulation_ref[1].astype(F32))
    out_ref[...] = (normed * (1.0 + scale) + shift).astype(BF16)


def project_kernel(head_size, weight_ref, gain_ref, *refs):
    hidden_refs, out_ref = refs[:-1], refs[-1]
    hidden = jnp.concatenate([ref[...] for ref in hidden_refs], axis=0)
    projected = lax.dot_general(
        weight_ref[...], hidden, (((1,), (1,)), ((), ())), preferred_element_type=F32
    )
    width = weight_ref.shape[0] // 3
    shape = (head_size, head_size)
    diagonal = lax.broadcasted_iota(jnp.int32, shape, 0) == lax.broadcasted_iota(
        jnp.int32, shape, 1
    )
    found = []
    for part in range(2):
        gain = jnp.sum(
            jnp.where(diagonal, gain_ref[part : part + 1, :], 0.0), axis=1, keepdims=True
        )
        for start in range(part * width, (part + 1) * width, head_size):
            value = projected[start : start + head_size]
            square = jnp.sum(value * value, axis=0, keepdims=True) * (1.0 / head_size)
            found.append(value * lax.rsqrt(square + EPSILON) * gain)
    found.append(projected[2 * width :])
    out_ref[...] = jnp.concatenate(found, axis=0).astype(BF16)


def token_codes(tokens, group_rows, per_peer, piece_rows, owner_ref, place_ref, table_ref):
    clips, per_clip = table_ref.shape[1:]
    seq_count = tokens // 2 // group_rows
    token = lax.broadcasted_iota(jnp.int32, (1, tokens), 1)
    row = lax.rem(token, group_rows)
    block = lax.div(token, group_rows)
    piece = lax.div(block, seq_count) * (group_rows // piece_rows) + lax.div(row, piece_rows)
    arrival = arrival_of(piece, per_peer, owner_ref[0])
    found = jnp.zeros_like(token)
    for clip in range(clips):
        for p in range(per_clip):
            found = jnp.where(arrival == table_ref[0, clip, p], clip * per_clip + p, found)
    source = jnp.bitwise_xor(lax.rem(block, seq_count), place_ref[0])
    return found * (piece_rows * seq_count) + source * piece_rows + lax.rem(row, piece_rows)


def gather_kernel(
    first, group_rows, per_peer, piece_rows, owner_ref, place_ref, table_ref, stacked_ref, *refs
):
    out_ref = refs[-1]
    clips, _, clip_tokens = out_ref.shape
    one_hot_ref, refs = (refs[0], refs[1:]) if len(refs[0].shape) == 2 else (None, refs)
    columns = slice(first, first + stacked_ref.shape[1])
    code = token_codes(
        clips * clip_tokens, group_rows, per_peer, piece_rows, owner_ref, place_ref, table_ref
    )[:, first : first + stacked_ref.shape[1]]
    position = lax.broadcasted_iota(jnp.int32, (clip_tokens, 1), 0)
    for clip in range(clips):
        if one_hot_ref is not None:
            chosen = one_hot_ref[clip * clip_tokens : (clip + 1) * clip_tokens, columns]
        else:
            chosen = jnp.where(code == position + clip * clip_tokens, 1.0, 0.0).astype(BF16)
        picked = lax.dot_general(
            stacked_ref[...], chosen, (((1,), (1,)), ((), ())), preferred_element_type=F32
        )
        if len(refs) > 1:
            picked += refs[0][clip].astype(F32)
        out_ref[clip] = picked.astype(BF16)


def chosen_kernel(group_rows, per_peer, piece_rows, owner_ref, place_ref, table_ref, out_ref):
    rows, tokens = out_ref.shape
    code = token_codes(
        tokens, group_rows, per_peer, piece_rows, owner_ref, place_ref, table_ref
    )
    row = lax.broadcasted_iota(jnp.int32, (rows, 1), 0)
    out_ref[...] = jnp.where(code == row, 1.0, 0.0).astype(BF16)


def attention_kernel(
    head_size, per_peer, piece_rows, length_ref, owner_ref, place_ref, table_ref, *refs
):
    early_ref, late_ref, refs = refs[0], refs[1], refs[2:]
    one_hot_ref = None
    if refs[0].shape[0] == refs[0].shape[1]:
        one_hot_ref, refs = refs[0], refs[1:]
    out_refs = refs
    clips, features, clip_tokens = early_ref.shape
    width, tokens = features // 3, clips * clip_tokens
    seq_count = len(out_refs)
    group_rows = tokens // 2 // seq_count
    code = token_codes(
        tokens, group_rows, per_peer, piece_rows, owner_ref, place_ref, table_ref
    )
    position = lax.broadcasted_iota(jnp.int32, (clip_tokens, 1), 0)
    key = lax.broadcasted_iota(jnp.int32, (8, clip_tokens), 1)
    heads = range(0, width, head_size)
    scale = math.log2(math.e) / math.sqrt(head_size)
    attended, chosen_by_clip = [], []
    for clip in range(clips):
        if one_hot_ref is not None:
            chosen = one_hot_ref[clip * clip_tokens : (clip + 1) * clip_tokens]
        else:
            chosen = jnp.where(code == position + clip * clip_tokens, 1.0, 0.0).astype(BF16)
        picked = early_ref[clip].astype(F32) + lax.dot_general(
            late_ref[...],
            chosen[:, tokens - late_ref.shape[1] :],
            (((1,), (1,)), ((), ())),
            preferred_element_type=F32,
        )
        in_clip = jnp.where(key < length_ref[0, clip], 1.0, 0.0)
        scores = [
            jnp.dot(
                jnp.transpose(picked[width + head : width + head + head_size]).astype(BF16),
                picked[head : head + head_size].astype(BF16),
                preferred_element_type=F32,
            )
            for head in heads
        ]
        unscaled = [jnp.exp2(score * scale).astype(BF16) for score in scores]
        outs = []
        for head, weights in zip(heads, unscaled):
            values = picked[2 * width + head : 2 * width + head + head_size] * in_clip[:1]
            values = jnp.concatenate([values, in_clip], axis=0).astype(BF16)
            summed = jnp.dot(values, weights, preferred_element_type=F32)
            outs.append(summed[:head_size] * (1.0 / summed[head_size : head_size + 1]))
        attended.append(jnp.concatenate(outs, axis=0).astype(BF16))
        chosen_by_clip.append(chosen)
    back = jnp.dot(
        jnp.concatenate(attended, axis=1),
        jnp.concatenate(chosen_by_clip, axis=0),
        preferred_element_type=F32,
    ).astype(BF16)
    for index, ref in enumerate(out_refs):
        for group in range(2):
            start = (group * seq_count + index) * group_rows
            ref[:, group * group_rows : (group + 1) * group_rows] = back[
                :, start : start + group_rows
            ]


def projected_rows(masks, halves, core_ref, head_refs, weight_refs):
    branch = None
    for mask, head_ref in zip(masks, head_refs):
        parts = 1 if mask == 0 else halves
        for part in range(parts):
            weight = weight_refs[part][...]
            head = head_ref[...]
            if parts == 2:
                rows = weight.shape[0]
                start = jnp.bitwise_xor(core_ref[0], part) * rows
                head = head_ref[pl.ds(pl.multiple_of(start, 16), rows), :]
            term = lax.dot_general(
                head, weight, (((0,), (0,)), ((), ())), preferred_element_type=F32
            )
            branch = term if branch is None else branch + term
        weight_refs = weight_refs[parts:]
    return branch


def sides_output_kernel(masks, halves, core_ref, *refs):
    refs[-1][...] = projected_rows(
        masks, halves, core_ref, refs[: len(masks)], refs[len(masks) : -1]
    )


def residual_kernel(
    clip_tokens, codes_of, length_ref, owner_ref, place_ref, table_ref, modulation_ref, *refs
):
    block_refs, (base_ref, gate_ref) = refs[:-2], refs[-2:]
    code = codes_of(base_ref.shape[0], owner_ref[0], place_ref[0], table_ref[0])
    clip = lax.div(code, clip_tokens)
    limit = jnp.zeros_like(code)
    for index in range(length_ref.shape[1]):
        limit = jnp.where(clip == index, length_ref[0, index], limit)
    kept = lax.rem(code, clip_tokens) < limit
    rows = jnp.concatenate([ref[...].astype(F32) for ref in block_refs], axis=0)
    base_ref[...] = jnp.where(kept, rows, 0.0).astype(BF16)
    gate = pick(clip, modulation_ref[2].astype(F32))
    gate_ref[...] = jnp.where(kept, gate, 0.0).astype(BF16)


def output_kernel(masks, halves, owner_masks, core_ref, base_ref, gate_ref, partial_ref, *refs):
    head_refs, refs = refs[: len(masks)], refs[len(masks) :]
    weight_refs, out_refs = refs[: len(masks) * halves], refs[len(masks) * halves :]
    branch = partial_ref[...] + projected_rows(masks, halves, core_ref, head_refs, weight_refs)
    result = base_ref[...].astype(F32) + gate_ref[...].astype(F32) * branch
    rows = result.shape[0] // len(owner_masks)
    for index, (out, first) in enumerate(owner_masks):
        out_refs[out][first : first + rows] = result[index * rows : (index + 1) * rows].astype(
            BF16
        )


def body(
    tokens, slot_owner, clip_pieces, clip_length, modulation, qkv_weight, qk_gain, proj_weight
):
    dp_count = lax.axis_size("dp")
    seq_count = lax.axis_size("seq")
    pieces_here = tokens.shape[1]
    piece_rows = tokens.shape[2]
    model_width = tokens.shape[3]
    per_peer = pieces_here // dp_count
    head_size = qk_gain.shape[1]
    heads = HEADS // seq_count
    head_width = heads * head_size
    clips_here, per_clip = clip_pieces.shape[1:]
    clip_tokens = per_clip * piece_rows * seq_count
    block_rows = per_peer * piece_rows
    rows_here = pieces_here * piece_rows
    group_rows = rows_here // 2
    chips = dp_count // 2
    owner_place = lax.axis_index("dp").astype(jnp.int32)
    place = lax.axis_index("seq").astype(jnp.int32).reshape(1)
    core = lax.rem(owner_place, 2).reshape(1)
    owner_place = owner_place.reshape(1)
    halves = 2 if heads % 2 == 0 else 1

    smem = pl.BlockSpec(memory_space=pltpu.SMEM)
    vmem = pl.BlockSpec(memory_space=pltpu.VMEM)

    def call(
        kernel, scalars, inputs, outputs, scratch=(), out_scalars=0, limit=16, flops=10**9, where=vmem
    ):
        return pl.pallas_call(
            kernel,
            in_specs=[smem] * len(scalars)
            + (where if isinstance(where, list) else [where] * len(inputs)),
            out_specs=[smem] * out_scalars + [vmem] * (len(outputs) - out_scalars),
            out_shape=[jax.ShapeDtypeStruct(shape, dtype) for shape, dtype in outputs],
            scratch_shapes=list(scratch),
            compiler_params=pltpu.CompilerParams(vmem_limit_bytes=int(limit * 2**20)),
            cost_estimate=pl.CostEstimate(
                flops=flops, bytes_accessed=2**20, transcendentals=0
            ),
        )(*scalars, *inputs)

    x_count = math.isqrt(seq_count)
    anywhere = pl.BlockSpec(memory_space=pltpu.HBM)
    along_x = list(range(1, x_count))
    along_y = list(range(x_count, seq_count, x_count))

    proj_own = proj_weight
    if halves == 2:
        (proj_own,) = call(
            half_kernel,
            [core],
            [proj_weight],
            [((head_width // 2, model_width), BF16)],
            scratch=[pltpu.SemaphoreType.DMA],
            where=anywhere,
        )
    proj_parts = {mask: send(proj_own, "seq", mask) for mask in along_y + along_x}

    slots, own, other = call(
        functools.partial(route_kernel, per_peer, piece_rows),
        [owner_place],
        [slot_owner, tokens],
        [((pieces_here,), jnp.int32)] + [((chips * block_rows, model_width), BF16)] * 2,
        scratch=[
            pltpu.SMEM((dp_count,), jnp.int32),
            pltpu.SMEM(slot_owner.shape, jnp.int32),
            pltpu.VMEM(tokens.shape, BF16),
            pltpu.SemaphoreType.DMA((2,)),
        ],
        out_scalars=1,
        limit=59,
        flops=3 * 10**10,
        where=anywhere,
    )
    payloads = call(
        functools.partial(merge_kernel, block_rows),
        [],
        [own, send(other, "dp", 1)],
        [((2 * block_rows, model_width), BF16)] * chips,
        scratch=[pltpu.VMEM(own.shape, BF16), pltpu.SemaphoreType.DMA],
        where=[anywhere, vmem],
    )
    arrived = [send(payload, "dp", 2 * mask) for mask, payload in enumerate(payloads)]

    def codes_of(group):
        return lambda rows, *places: row_codes(
            rows,
            group * (pieces_here // 2),
            per_peer,
            piece_rows,
            piece_rows * seq_count,
            *places,
        )

    weight = jnp.transpose(qkv_weight, (1, 2, 0)).reshape(3 * head_width, model_width)
    factors = jnp.transpose(modulation[0], (1, 0, 2))
    def project(blocks, flops=3 * 10**9):
        (projected,) = call(
            functools.partial(project_kernel, head_size),
            [],
            [weight, qk_gain] + blocks,
            [((3 * head_width, sum(block.shape[0] for block in blocks)), BF16)],
            flops=flops,
        )
        return projected

    def hidden_rows(group, placed):
        return call(
            functools.partial(norm_kernel, clip_tokens, codes_of(group)),
            [placed, place],
            [clip_pieces, factors] + arrived[group * chips // 2 : (group + 1) * chips // 2],
            [((group_rows, model_width), BF16)],
            flops=(1 + 9 * group) * 10**9,
        )[0]

    near = hidden_rows(0, owner_place)
    one_hot, placed = [], owner_place
    if clip_tokens <= 256:
        _, early = lax.optimization_barrier((near, owner_place))
        one_hot = call(
            functools.partial(chosen_kernel, group_rows, per_peer, piece_rows),
            [early, place, clip_pieces],
            [],
            [((clips_here * clip_tokens, clips_here * clip_tokens), BF16)],
        )
        one_hot, placed = lax.optimization_barrier((list(one_hot), owner_place))
    far = hidden_rows(1, placed)
    near, proj_parts = lax.optimization_barrier((near, proj_parts))
    near, proj_parts = lax.optimization_barrier((near, proj_parts))
    sides = {mask: send(near, "seq", mask) for mask in along_y + along_x}
    far, sides = lax.optimization_barrier((far, sides))
    far_blocks = [send(far, "seq", mask) for mask in range(seq_count)]
    halved = call(
        sides_kernel,
        [],
        [sides[mask] for mask in along_x + along_y],
        [((group_rows // 2, model_width), BF16)] * len(sides),
    )
    halved = dict(zip(along_x + along_y, halved))
    near_blocks = []
    for mask in range(seq_count):
        mx = mask % x_count
        my = mask - mx
        if mx > 0 and my > 0:
            near_blocks += [send(halved[mx], "seq", my), send(halved[my], "seq", mx)]
        else:
            near_blocks.append(sides[mask] if mask > 0 else near)
    stacked_near = project(near_blocks)
    def gather(first, *arrays):
        (gathered,) = call(
            functools.partial(gather_kernel, first, group_rows, per_peer, piece_rows),
            [owner_place, place, clip_pieces],
            [arrays[0], *one_hot, *arrays[1:]],
            [((clips_here, 3 * head_width, clip_tokens), BF16)],
            limit=16 if clip_tokens <= 256 else 48,
            flops=3 * 10**9,
        )
        return gathered

    gathered = gather(0, stacked_near)
    gathered, proj_parts, settled = lax.optimization_barrier((gathered, proj_parts, arrived))
    early_blocks, late_blocks = far_blocks[: seq_count // 2], far_blocks[seq_count // 2 :]
    residual = call(
        functools.partial(residual_kernel, clip_tokens, codes_of(0)),
        [clip_length, owner_place, place],
        [clip_pieces, factors] + settled,
        [((rows_here, model_width), BF16)] * 2,
    )
    early_blocks, gathered, residual = lax.optimization_barrier(
        (early_blocks, gathered, list(residual))
    )
    gathered = gather(seq_count * group_rows, project(early_blocks), gathered)
    swapped = {mask: send(proj_parts[mask], "dp", 1) for mask in proj_parts} if halves == 2 else {}
    gathered, proj_parts = lax.optimization_barrier((gathered, proj_parts))
    for my in along_y:
        for mx in along_x:
            proj_parts[my + mx] = send(proj_parts[my], "seq", mx)
    late_blocks, gathered = lax.optimization_barrier((late_blocks, gathered))
    stacked_late, swapped = lax.optimization_barrier((project(late_blocks, 10**8), swapped))

    attended = call(
        functools.partial(attention_kernel, head_size, per_peer, piece_rows),
        [clip_length, owner_place, place, clip_pieces],
        [gathered, stacked_late] + one_hot,
        [((head_width, rows_here), BF16)] * seq_count,
        limit=16 if clip_tokens <= 256 else 48,
        flops=10**8,
    )
    returned = [send(array, "seq", mask) for mask, array in enumerate(attended)]
    if halves == 2:
        _, late = lax.optimization_barrier((attended[0], proj_parts))
        swapped |= {mask: send(late[mask], "dp", 1) for mask in late if mask not in swapped}
    proj_parts = proj_parts | {seq_count + mask: swapped[mask] for mask in swapped}

    half_count = dp_count // 2
    far_masks = list(range(half_count, dp_count))
    outs = {mask: (index, 0) for index, mask in enumerate(far_masks)}
    for mask in range(2, half_count):
        outs[mask] = (half_count + mask // 2 - 1, mask % 2 * block_rows)
    outs[0], outs[1] = [(half_count + half_count // 2 - 1 + core_of, 0) for core_of in range(2)]

    def weights_of(masks):
        return [
            part
            for mask in masks
            for part in (
                [proj_weight]
                if mask == 0
                else [proj_parts[mask + half * seq_count] for half in range(halves)]
            )
        ]

    beside = [0] + along_x + along_y
    across = [mask for mask in range(seq_count) if mask not in beside]
    (partial,) = call(
        functools.partial(sides_output_kernel, beside, halves),
        [core],
        [returned[mask] for mask in beside] + weights_of(beside),
        [((rows_here, model_width), F32)],
        flops=10**10,
    )
    results = call(
        functools.partial(output_kernel, across, halves, [outs[mask] for mask in range(dp_count)]),
        [core],
        residual + [partial] + [returned[mask] for mask in across] + weights_of(across),
        [((block_rows, model_width), BF16)] * half_count
        + [((2 * block_rows, model_width), BF16)] * (half_count // 2 - 1)
        + [((block_rows, model_width), BF16)] * 2,
        flops=3 * 10**9,
    )
    near_back = [
        send(block, "dp", 2 * (index + 1)) for index, block in enumerate(results[half_count:-2])
    ]
    far_back = [send(block, "dp", mask) for block, mask in zip(results, far_masks)]
    (crossing,) = call(
        functools.partial(crossing_kernel, block_rows),
        [],
        [results[-1]] + near_back,
        [((half_count // 2 * block_rows, model_width), BF16)],
    )
    crossed = send(crossing, "dp", 1)
    (far_back,) = call(
        stack_kernel,
        [],
        far_back,
        [((half_count * block_rows, model_width), BF16)],
        flops=10**10,
    )
    came_back = [far_back, crossed, results[-2]] + near_back
    places = {mask: (0, index * block_rows) for index, mask in enumerate(far_masks)}
    places[0] = (2, 0)
    for index in range(half_count // 2):
        places[2 * index + 1] = (1, index * block_rows)
        if index > 0:
            places[2 * index] = (2 + index, 0)
    (out,) = call(
        functools.partial(
            place_kernel, per_peer, piece_rows, [places[mask] for mask in range(dp_count)]
        ),
        [slots],
        came_back,
        [(tokens.shape, BF16)],
    )
    return out


def solution(mesh):
    return jax.shard_map(
        body,
        mesh=mesh,
        in_specs=(
            P("dp", None, "seq", None),
            P("dp", None),
            P("dp", None, None),
            P("dp", None),
            P("dp", None, None, None),
            P(None, None, "seq"),
            P(),
            P("seq", None),
        ),
        out_specs=P("dp", None, "seq", None),
        check_vma=False,
    )
```
